32 devices in a mesh: dp: 8 (over z, y), mp: 4 (over x, core).
Axes of the slice: x: 2, y: 2, z: 4, core: 2. Of those that a mesh axis runs over, the one named last changes fastest.
Arguments:
- tokens: bfloat16 [32768, 1152], P(('dp', 'mp')), may hold values from -6 to 6
- condition: bfloat16 [16, 1152], P('dp'), may hold values from -6 to 6
- grid_rows: int32 [128], P('dp'), may hold values from 12 to 20, as said below
- grid_cols: int32 [128], P('dp'), may hold values from 12 to 20, as said below
- frame_start: int32 [128], P('dp'), may hold values from 0 to 3856, as said below
- frame_item: int32 [128], P('dp'), may hold values from 0 to 1, as said below
- group_frames: int32 [8], P('dp'), may hold values from 8 to 16, as said below
- w_qkv: bfloat16 [1152, 3, 1152], P(None, None, 'mp'), may hold values from -0.1875 to 0.1875
- qv_bias: bfloat16 [2, 1152], P(None, 'mp'), may hold values from -3 to 3
- w_out: bfloat16 [1152, 1152], P('mp'), may hold values from -1.5 to 1.5
- b_out: bfloat16 [1152], replicated, may hold values from -2 to 2
- w_up: bfloat16 [1152, 4608], P(None, 'mp'), may hold values from -0.1875 to 0.1875
- b_up: bfloat16 [4608], P('mp'), may hold values from -3 to 3
- w_down: bfloat16 [4608, 1152], P('mp'), may hold values from -0.09375 to 0.09375
- b_down: bfloat16 [1152], replicated, may hold values from -2 to 2
- w_ada: bfloat16 [1152, 6, 1152], P(None, None, 'mp'), may hold values from -0.1875 to 0.1875
- b_ada: bfloat16 [6, 1152], P(None, 'mp'), may hold values from -2 to 2
- cotangent: bfloat16 [32768, 1152], P(('dp', 'mp')), may hold values from -6 to 6
Outputs:
- output: bfloat16 [32768, 1152], P(('dp', 'mp'))
- grad_tokens: bfloat16 [32768, 1152], P(('dp', 'mp'))
- grad_condition: float32 [16, 1152], P('dp')
- grad_w_qkv: float32 [1152, 3, 1152], P(None, None, 'mp')
- grad_qv_bias: float32 [2, 1152], P(None, 'mp')
- grad_w_out: float32 [1152, 1152], P('mp')
- grad_b_out: float32 [1152], replicated
- grad_w_up: float32 [1152, 4608], P(None, 'mp')
- grad_b_up: float32 [4608], P('mp')
- grad_w_down: float32 [4608, 1152], P('mp')
- grad_b_down: float32 [1152], replicated
- grad_w_ada: float32 [1152, 6, 1152], P(None, None, 'mp')
- grad_b_ada: float32 [6, 1152], P(None, 'mp')
The draws below stay inside these ranges and needn't reach their ends.
Inputs may be any that keep to these rules, and one draw needn't show every extreme that they name: `grid_rows`: each frame slot's grid is one of 16 x 16, 12 x 20, 20 x 12, 14 x 18 (rows x columns). `grid_cols`: paired with grid_rows as stated there. `frame_start`: slot k of a group starts at a row from k * 256 to (k + 1) * 256 - grid_rows[k] * grid_cols[k], so that it ends within its own 256 rows. `frame_item`: slots 0 and 1 of a group name different videos. `group_frames`: some group uses all of the slots and some group exactly half of them, rounded down; used slots come first.
All inputs are finite; a program needn't handle non-finite values.
Results may differ from the reference program's by a relative error of at most 0.02.
Values may be sent and summed in bfloat16 or wider, within the bound.
A program may use at most 448 MiB of HBM per device.

```python
import jax
import jax.numpy as jnp
from jax import lax

D = 1152
HEADS = 16
HEAD = 72
FF = 4608
SLOT = 256
ITEMS_DEV = 2
TOK_DEV = 4096
FRAMES_DEV = 16
TOKENS = 32768
ITEMS = 16
N_DP = 8


def frame_layout(key):
    total = N_DP * FRAMES_DEV
    kinds = jax.random.randint(jax.random.fold_in(key, 11), (total,), 0, 4)
    kinds = kinds.at[total - 1].set(1).at[total - 2].set(2)
    heights = jnp.array([16, 12, 20, 14], jnp.int32)[kinds]
    widths = jnp.array([16, 20, 12, 18], jnp.int32)[kinds]
    room = SLOT - heights * widths
    extra = jax.random.randint(jax.random.fold_in(key, 12), (total,), 0, 1 << 20) % (room + 1)
    extra = extra.at[0].set(0).at[total - 1].set(room[total - 1])
    slots = jnp.arange(total, dtype=jnp.int32) % FRAMES_DEV
    starts = slots * SLOT + extra
    fullest = jax.random.randint(jax.random.fold_in(key, 13), (), 0, N_DP)
    emptiest = (fullest + 1) % N_DP
    counts = jax.random.randint(jax.random.fold_in(key, 14), (N_DP,), FRAMES_DEV // 2, FRAMES_DEV + 1)
    places = jnp.arange(N_DP, dtype=jnp.int32)
    counts = jnp.where(places == fullest, FRAMES_DEV, counts)
    counts = jnp.where(places == emptiest, FRAMES_DEV // 2, counts)
    picks = jax.random.randint(jax.random.fold_in(key, 15), (N_DP, FRAMES_DEV), 0, ITEMS_DEV)
    picks = picks.at[:, 1].set((picks[:, 0] + 1) % ITEMS_DEV)
    return (heights.astype(jnp.int32), widths.astype(jnp.int32), starts.astype(jnp.int32), picks.reshape(total).astype(jnp.int32), counts.astype(jnp.int32))


def draw_grid_rows(key, part):
    shared = frame_layout(key)
    return shared[0]


def draw_grid_cols(key, part):
    shared = frame_layout(key)
    return shared[1]


def draw_frame_start(key, part):
    shared = frame_layout(key)
    return shared[2]


def draw_frame_item(key, part):
    shared = frame_layout(key)
    return shared[3]


def draw_group_frames(key, part):
    shared = frame_layout(key)
    return shared[4]


def steps_of(own_key, extent, split, smallest, high):
    factor_of, own = 1.0, jax.random.fold_in(own_key, 6)
    for axis_at, blocks in split:
        steps = jnp.exp(jax.random.uniform(jax.random.fold_in(own, axis_at), (blocks,), jnp.float32, smallest / len(split), high / len(split)))
        factor_of = factor_of * jnp.repeat(steps, extent[axis_at] // blocks).reshape([-1 if axis == axis_at else 1 for axis in range(len(extent))])
    return factor_of


def gaussian(rng, shape, width, bound, cuts=(), kind=jnp.bfloat16):
    entries = width * jax.random.normal(rng, shape, jnp.float32)
    if cuts:
        entries = entries * steps_of(rng, shape, cuts, -0.22, 0.18)
    return jnp.clip(entries, -bound, bound).astype(kind)


def setup_inputs(seed: int = 0) -> dict:
    key_list = jax.random.split(jax.random.key(seed), 19)
    tokens = gaussian(key_list[0], (TOKENS, D), 1.0, 6.0, ((0, 32),))
    condition = gaussian(key_list[1], (ITEMS, D), 1.0, 6.0, ((0, 8),))
    grid_rows = draw_grid_rows(jax.random.fold_in(key_list[18], 71), 0)
    grid_cols = draw_grid_cols(jax.random.fold_in(key_list[18], 71), 0)
    frame_start = draw_frame_start(jax.random.fold_in(key_list[18], 71), 0)
    frame_item = draw_frame_item(jax.random.fold_in(key_list[18], 71), 0)
    group_frames = draw_group_frames(jax.random.fold_in(key_list[18], 71), 0)
    w_qkv = gaussian(key_list[7], (D, 3, D), D ** -0.5, 0.1875, ((2, 4),))
    qv_bias = gaussian(key_list[8], (2, D), 0.5, 3.0, ((1, 4),))
    w_out = gaussian(key_list[9], (D, D), (D // 64) ** -0.5, 1.5, ((0, 4),))
    b_out = gaussian(key_list[10], (D,), 0.3, 2.0)
    w_up = gaussian(key_list[11], (D, FF), D ** -0.5, 0.1875, ((1, 4),))
    b_up = gaussian(key_list[12], (FF,), 0.5, 3.0, ((0, 4),))
    w_down = gaussian(key_list[13], (FF, D), FF ** -0.5, 0.09375, ((0, 4),))
    b_down = gaussian(key_list[14], (D,), 0.3, 2.0)
    w_ada = gaussian(key_list[15], (D, 6, D), D ** -0.5, 0.1875, ((2, 4),))
    b_ada = gaussian(key_list[16], (6, D), 0.3, 2.0, ((1, 4),))
    cotangent = gaussian(key_list[17], (TOKENS, D), 1.0, 6.0, ((0, 32),))
    return {"tokens": tokens, "condition": condition, "grid_rows": grid_rows, "grid_cols": grid_cols, "frame_start": frame_start, "frame_item": frame_item, "group_frames": group_frames, "w_qkv": w_qkv, "qv_bias": qv_bias, "w_out": w_out, "b_out": b_out, "w_up": w_up, "b_up": b_up, "w_down": w_down, "b_down": b_down, "w_ada": w_ada, "b_ada": b_ada, "cotangent": cotangent}


precise = lax.Precision.HIGHEST
epsilon = 1e-06

@jax.custom_vjp
def low(v):
    return lax.optimization_barrier(v.astype(jnp.bfloat16)).astype(jnp.float32)

@jax.custom_vjp
def low_back(v):
    return v

def low_keep(v):
    return (low(v), None)

def low_pass(kept, grad):
    return (grad,)

def back_keep(v):
    return (v, None)

def back_low(kept, grad):
    return (low(grad),)
low.defvjp(low_keep, low_pass)
low_back.defvjp(back_keep, back_low)

def frame_tables(grid_rows, grid_cols, frame_start, frame_item, used, length):
    rows = jnp.arange(length, dtype=jnp.int32)[:, None]
    slots = jnp.arange(grid_rows.shape[0], dtype=jnp.int32)[None, :]
    ends = (frame_start + grid_rows * grid_cols)[None, :]
    inside = (rows >= frame_start[None, :]) & (rows < ends) & (slots < used)
    frame_id = lax.optimization_barrier(jnp.sum(jnp.where(inside, slots + 1, 0), axis=1)).astype(jnp.int32) - 1
    item_id = lax.optimization_barrier(jnp.sum(jnp.where(inside, frame_item[None, :], 0), axis=1)).astype(jnp.int32)
    return (frame_id, item_id)

def allowed_pairs(frames):
    span = frames.shape[-1]
    place = jnp.arange(span, dtype=jnp.int32)
    same = (frames[..., :, None] == frames[..., None, :]) & (frames[..., :, None] >= 0)
    return same | (place[:, None] == place[None, :])

def layer_norm(values):
    centred = values - lax.optimization_barrier(jnp.mean(values, axis=-1, keepdims=True))
    variance = lax.optimization_barrier(jnp.mean(centred * centred, axis=-1, keepdims=True))
    return centred * lax.rsqrt(variance + epsilon)

def product(left, right):
    return jnp.dot(left, right, precision=precise)

def attend_block(pieces):
    queries, keys, values, frames = pieces
    scores = jnp.einsum('qhe,khe->hqk', queries, keys, precision=precise) * HEAD ** (-0.5)
    scores = low_back(scores)
    scores = jnp.where(allowed_pairs(frames)[None], scores, -1e+30)
    peak = lax.optimization_barrier(jnp.max(scores, axis=-1, keepdims=True))
    weights = jnp.exp(scores - peak)
    probs = low(weights / lax.optimization_barrier(jnp.sum(weights, axis=-1, keepdims=True)))
    return jnp.einsum('hqk,khe->qhe', probs, values, precision=precise)

def group_forward(frame_id, item_id, tokens, condition, w_qkv, qv_bias, w_out, b_out, w_up, b_up, w_down, b_down, w_ada, b_ada):
    length = tokens.shape[0]
    act = low(jax.nn.silu(condition))
    modulation = product(act, w_ada.reshape(D, 6 * D)).reshape(-1, 6, D) + b_ada[None]
    per_token = modulation[item_id]
    shift_one, scale_one, gate_one = (per_token[:, 0], per_token[:, 1], per_token[:, 2])
    shift_two, scale_two, gate_two = (per_token[:, 3], per_token[:, 4], per_token[:, 5])
    normed_one = low(layer_norm(tokens) * (1.0 + scale_one) + shift_one)
    bias = jnp.stack([qv_bias[0], jnp.zeros_like(qv_bias[0]), qv_bias[1]])
    projected = product(normed_one, w_qkv.reshape(D, 3 * D)).reshape(length, 3, D) + bias[None]
    projected = low(low_back(projected))
    span = 2 * SLOT
    blocks = length // span
    queries = projected[:, 0].reshape(blocks, span, HEADS, HEAD)
    keys = projected[:, 1].reshape(blocks, span, HEADS, HEAD)
    values = projected[:, 2].reshape(blocks, span, HEADS, HEAD)
    frames = frame_id.reshape(blocks, span)
    attended = lax.map(jax.checkpoint(attend_block), (queries, keys, values, frames))
    attended = low(low_back(attended.reshape(length, D)))
    branch_one = low_back(product(attended, w_out) + b_out)
    middle = tokens + gate_one * branch_one
    normed_two = low(layer_norm(middle) * (1.0 + scale_two) + shift_two)
    pre_act = low_back(product(normed_two, w_up) + b_up)
    hidden = low(jax.nn.gelu(pre_act, approximate=True))
    branch_two = low_back(product(hidden, w_down) + b_down)
    return middle + gate_two * branch_two

def reference(tokens, condition, grid_rows, grid_cols, frame_start, frame_item, group_frames, w_qkv, qv_bias, w_out, b_out, w_up, b_up, w_down, b_down, w_ada, b_ada, cotangent):
    weights = tuple((w.astype(jnp.float32) for w in (w_qkv, qv_bias, w_out, b_out, w_up, b_up, w_down, b_down, w_ada, b_ada)))
    pieces = (tokens.reshape(N_DP, TOK_DEV, D), condition.reshape(N_DP, ITEMS_DEV, D), grid_rows.reshape(N_DP, FRAMES_DEV), grid_cols.reshape(N_DP, FRAMES_DEV), frame_start.reshape(N_DP, FRAMES_DEV), frame_item.reshape(N_DP, FRAMES_DEV), group_frames, cotangent.reshape(N_DP, TOK_DEV, D))

    def one_group(totals, piece):
        rows_in, cond_in, heights, widths, starts, picks, used, upstream = piece
        frame_id, item_id = frame_tables(heights, widths, starts, picks, used, TOK_DEV)

        def forward(rows_value, cond_value, *params):
            return group_forward(frame_id, item_id, rows_value, cond_value, *params)
        result, pull = jax.vjp(forward, rows_in.astype(jnp.float32), cond_in.astype(jnp.float32), *weights)
        grads = pull(upstream.astype(jnp.float32))
        totals = tuple((a + b for a, b in zip(totals, grads[2:])))
        return (totals, (result.astype(jnp.bfloat16), grads[0].astype(jnp.bfloat16), grads[1]))
    start = tuple((jnp.zeros(w.shape, jnp.float32) for w in weights))
    totals, stacked = lax.scan(one_group, start, pieces)
    output = stacked[0].reshape(TOKENS, D)
    grad_tokens = stacked[1].reshape(TOKENS, D)
    grad_condition = stacked[2].reshape(ITEMS, D)
    return (output, grad_tokens, grad_condition, totals[0], totals[1], totals[2], totals[3], totals[4], totals[5], totals[6], totals[7], totals[8], totals[9])
```

```python
import functools

import jax
import jax.numpy as jnp
from jax import lax
from jax.experimental import pallas as pl
from jax.experimental.pallas import tpu as pltpu
from jax.sharding import PartitionSpec as P

HEAD = 72
SLOT = 256
CHUNK = 128
OUT_SLOTS = 6
MESH = pl.DeviceIdType.MESH
epsilon = 1e-06
f32 = jnp.float32
bf16 = jnp.bfloat16


def frame_tables(grid_rows, grid_cols, frame_start, frame_item, used, first, length):
    rows = first + jnp.arange(length, dtype=jnp.int32)[:, None]
    slots = jnp.arange(grid_rows.shape[0], dtype=jnp.int32)[None, :]
    ends = (frame_start + grid_rows * grid_cols)[None, :]
    inside = (rows >= frame_start[None, :]) & (rows < ends) & (slots < used)
    frame_id = jnp.sum(jnp.where(inside, slots + 1, 0), axis=1) - 1
    item_id = jnp.sum(jnp.where(inside, frame_item[None, :], 0), axis=1)
    return (frame_id, item_id)


def normal(values):
    centred = values - jnp.mean(values, axis=-1, keepdims=True)
    rstd = lax.rsqrt(jnp.mean(centred * centred, axis=-1, keepdims=True) + epsilon)
    return centred * rstd, rstd


def normal_back(grad, scale, normed, rstd):
    u = grad * (1.0 + scale)
    return rstd * (
        u
        - jnp.mean(u, axis=-1, keepdims=True)
        - normed * jnp.mean(u * normed, axis=-1, keepdims=True)
    )


def dot(left, right):
    return jnp.dot(left, right, preferred_element_type=f32)


def row_inner(left, right):
    return lax.dot_general(left, right, (((0,), (0,)), ((), ())), preferred_element_type=f32)


def col_inner(left, right):
    return lax.dot_general(left, right, (((1,), (1,)), ((), ())), preferred_element_type=f32)


def reduce_kernel(count, g_ref, out_ref, lp, rd, s0, sx, rx, tb, ry, ub, rz1, vb, rz2, ob, loads, sends, recvs, outs):
    dp, mp = lax.axis_index("dp"), lax.axis_index("mp")
    core, yb = mp % 2, dp % 2
    xb, z0, z1 = mp // 2, (dp // 2) % 2, dp // 4
    sib = (dp, mp + 1 - 2 * core)
    xn = (dp, mp + 2 - 4 * xb)
    yn = (dp + 1 - 2 * yb, mp)
    z1n = (dp + 2 - 4 * z0, mp)
    z2n = (dp + 4 - 8 * z1, mp)
    half, quarter, eighth = CHUNK // 2, CHUNK // 4, CHUNK // 8

    barrier = pltpu.get_barrier_semaphore()
    for peer in (sib, xn, yn, z1n, z2n):
        pl.semaphore_signal(barrier, inc=1, device_id=peer, device_id_type=MESH)
    pl.semaphore_wait(barrier, 5)

    def rows_of(c):
        return pl.ds(pl.multiple_of(c * CHUNK, CHUNK), CHUNK)

    def remote(stage, src, dst, peer, slot):
        return pltpu.make_async_remote_copy(
            src_ref=src,
            dst_ref=dst,
            send_sem=sends.at[stage, slot],
            recv_sem=recvs.at[stage, slot],
            device_id=peer,
            device_id_type=MESH,
        )

    def load(which, c, slot):
        return pltpu.make_async_copy(
            g_ref.at[2 * which, rows_of(c)], lp.at[slot, which], loads.at[which, slot]
        )

    def d_copy(which, c, slot):
        return remote(which, g_ref.at[2 * which + 1, rows_of(c)], rd.at[slot, which], sib, slot)

    def x_copy(c, slot):
        return remote(2, sx.at[slot], rx.at[slot], xn, slot)

    def y_copy(c, slot):
        part = pl.ds(pl.multiple_of((1 - yb) * half, half), half)
        return remote(3, tb.at[slot, part], ry.at[slot], yn, slot)

    def z1_copy(c, slot):
        part = pl.ds(pl.multiple_of((1 - z0) * quarter, quarter), quarter)
        return remote(4, ub.at[slot, part], rz1.at[slot], z1n, slot)

    def z2_copy(c, slot):
        part = pl.ds(pl.multiple_of((1 - z1) * eighth, eighth), eighth)
        return remote(5, vb.at[slot, part], rz2.at[slot], z2n, slot)

    at_y = pl.multiple_of(yb * half, half)
    at_z1 = pl.multiple_of(yb * half + z0 * quarter, quarter)
    at_z2 = pl.multiple_of(yb * half + z0 * quarter + z1 * eighth, eighth)

    def back(stage, at, size, peer, c, slot):
        place = ob.at[c % OUT_SLOTS, pl.ds(at, size)]
        return remote(stage, place, place, peer, slot)

    def az2_copy(c, slot):
        return back(6, at_z2, eighth, z2n, c, slot)

    def az1_copy(c, slot):
        return back(7, at_z1, quarter, z1n, c, slot)

    def ay_copy(c, slot):
        return back(8, at_y, half, yn, c, slot)

    def out_copy(c, slot):
        return pltpu.make_async_copy(ob.at[c % OUT_SLOTS], out_ref.at[rows_of(c)], outs.at[slot])

    def step(i, carry):
        def stage(lag, work):
            c = i - lag

            @pl.when((c >= 0) & (c < count))
            def _():
                work(c, c % 2)

        def leave(c, slot):
            out_copy(c, slot).wait()

        def store(c, slot):
            ay_copy(c, slot).wait()
            out_copy(c, slot).start()

        def go_ay(c, slot):
            az1_copy(c, slot).wait()
            ay_copy(c, slot).start()

        def go_az1(c, slot):
            az2_copy(c, slot).wait()
            az1_copy(c, slot).start()

        def go_az2(c, slot):
            z2_copy(c, slot).wait()
            mine = vb[slot, pl.ds(pl.multiple_of(z1 * eighth, eighth), eighth)] + rz2[slot]
            ob[c % OUT_SLOTS, pl.ds(at_z2, eighth)] = mine
            az2_copy(c, slot).start()

        def go_z2(c, slot):
            z1_copy(c, slot).wait()
            vb[slot] = ub[slot, pl.ds(pl.multiple_of(z0 * quarter, quarter), quarter)] + rz1[slot]
            z2_copy(c, slot).start()

        def go_z1(c, slot):
            y_copy(c, slot).wait()
            ub[slot] = tb[slot, pl.ds(pl.multiple_of(yb * half, half), half)] + ry[slot]
            z1_copy(c, slot).start()

        def go_y(c, slot):
            x_copy(c, slot).wait()
            tb[slot] = s0[slot] + rx[slot]
            y_copy(c, slot).start()

        def go_x(c, slot):
            for which in range(2):
                load(which, c, slot).wait()
                d_copy(which, c, slot).wait()
            sx[slot] = lp[slot, 1] + rd[slot, 1]
            s0[slot] = lp[slot, 0] + rd[slot, 0]
            x_copy(c, slot).start()

        def go_d(c, slot):
            for which in range(2):
                load(which, c, slot).start()
                d_copy(which, c, slot).start()

        stage(9, leave)
        stage(8, store)
        stage(7, go_ay)
        stage(6, go_az1)
        stage(5, go_az2)
        stage(4, go_z2)
        stage(3, go_z1)
        stage(2, go_y)
        stage(1, go_x)
        stage(0, go_d)
        return carry

    lax.fori_loop(0, count + 10, step, 0)


def reduce_grads(parts):
    shards, rows, width = parts.shape
    count = rows // CHUNK
    half, quarter, eighth = CHUNK // 2, CHUNK // 4, CHUNK // 8

    def buf(*lead):
        return pltpu.VMEM((*lead, width), bf16)

    return pl.pallas_call(
        functools.partial(reduce_kernel, count),
        out_shape=jax.ShapeDtypeStruct((rows, width), bf16),
        in_specs=[pl.BlockSpec(memory_space=pl.ANY)],
        out_specs=pl.BlockSpec(memory_space=pl.ANY),
        scratch_shapes=[
            buf(2, 2, CHUNK),
            buf(2, 2, CHUNK),
            buf(2, CHUNK),
            buf(2, CHUNK),
            buf(2, CHUNK),
            buf(2, CHUNK),
            buf(2, half),
            buf(2, half),
            buf(2, quarter),
            buf(2, quarter),
            buf(2, eighth),
            buf(OUT_SLOTS, CHUNK),
            pltpu.SemaphoreType.DMA((2, 2)),
            pltpu.SemaphoreType.DMA((9, 2)),
            pltpu.SemaphoreType.DMA((9, 2)),
            pltpu.SemaphoreType.DMA((2,)),
        ],
        compiler_params=pltpu.CompilerParams(
            collective_id=0, has_side_effects=True, vmem_limit_bytes=32 << 20
        ),
    )(parts)


def swap(values, axis, bit):
    n = lax.axis_size(axis)
    return lax.ppermute(values, axis, [(i, i ^ bit) for i in range(n)])


def gather_weight(value):
    other = swap(value, "mp", 1)
    rows = value.shape[0] // 2
    side = lax.axis_index("dp") % 2
    mine = swap(lax.dynamic_slice_in_dim(value, side * rows, rows), "mp", 2)
    rest = swap(mine, "dp", 1)
    far = jnp.concatenate(
        [jnp.where(side == 0, mine, rest), jnp.where(side == 0, rest, mine)], axis=0
    )
    return [value, other, far, swap(far, "mp", 1)]


def shards(
    paired,
    tokens,
    condition,
    grid_rows,
    grid_cols,
    frame_start,
    frame_item,
    group_frames,
    w_qkv,
    qv_bias,
    w_out,
    b_out,
    w_up,
    b_up,
    w_down,
    b_down,
    w_ada,
    b_ada,
    cotangent,
):
    own_rows, width = tokens.shape
    local_width = w_qkv.shape[2]
    local_ff = w_up.shape[1]
    heads = local_width // HEAD
    items = condition.shape[0]
    n_mp, n_dp = lax.axis_size("mp"), lax.axis_size("dp")
    mp, dp = lax.axis_index("mp"), lax.axis_index("dp")
    frames = own_rows // SLOT
    scale = HEAD ** (-0.5)
    frame_id, item_id = frame_tables(
        grid_rows, grid_cols, frame_start, frame_item, group_frames[0], mp * own_rows, own_rows
    )
    cond_value = condition.astype(f32)
    act_low = jax.nn.silu(cond_value).astype(bf16)
    ada_flat = w_ada.reshape(width, -1)
    ada_local = dot(act_low, ada_flat) + b_ada.reshape(-1).astype(f32)
    bias_local = jnp.concatenate(
        [
            qv_bias[0].astype(f32),
            jnp.zeros((local_width,), f32),
            qv_bias[1].astype(f32),
            b_up.astype(f32),
        ]
    )
    small = jnp.concatenate([ada_local.reshape(-1), bias_local])
    small = lax.all_gather(small, "mp", axis=0)
    n_ada = items * 6 * local_width
    modulation = small[:, :n_ada].reshape(n_mp, items, 6, local_width)
    modulation = modulation.transpose(1, 2, 0, 3).reshape(items, 6, width)
    order = (mp ^ jnp.arange(n_mp)) if paired else jnp.arange(n_mp)
    biases = small[:, n_ada:][order]
    if paired:
        qkv = gather_weight(w_qkv.reshape(width, 3 * local_width))
        out = gather_weight(w_out)
        up = gather_weight(w_up)
        down = gather_weight(w_down)
    else:
        qkv = list(lax.all_gather(w_qkv.reshape(width, 3 * local_width), "mp", axis=0))
        out = list(lax.all_gather(w_out, "mp", axis=0))
        up = list(lax.all_gather(w_up, "mp", axis=0))
        down = list(lax.all_gather(w_down, "mp", axis=0))

    def per_row(k):
        total = modulation[0, k][None]
        for item in range(1, items):
            total = jnp.where((item_id == item)[:, None], modulation[item, k][None], total)
        return total

    inputs = tokens.astype(f32)
    upstream = cotangent.astype(f32)
    normed, rstd = normal(inputs)
    normed_one = (normed * (1.0 + per_row(1)) + per_row(0)).astype(bf16)
    ids = frame_id.reshape(frames, SLOT)
    place = jnp.arange(SLOT)
    allowed = ((ids[:, :, None] == ids[:, None, :]) & (ids[:, :, None] >= 0)) | (
        place[:, None] == place[None, :]
    )
    allowed = allowed[:, None]
    branch_one = b_out.astype(f32)[None]
    kept = []
    for m in range(n_mp):
        proj = (dot(normed_one, qkv[m]) + biases[m, : 3 * local_width][None]).astype(bf16)
        q, k, v = (
            proj[:, j * local_width : (j + 1) * local_width].reshape(frames, SLOT, heads, HEAD)
            for j in range(3)
        )
        scores = jnp.einsum("bqhe,bkhe->bhqk", q, k, preferred_element_type=f32) * scale
        scores = jnp.where(allowed, scores, -1e30)
        peak = jnp.max(scores, axis=-1, keepdims=True)
        weights = jnp.exp(scores - peak)
        totals = jnp.sum(weights, axis=-1, keepdims=True)
        probs = (weights / totals).astype(bf16)
        log_total = peak + jnp.log(totals)
        attended = jnp.einsum("bhqk,bkhe->bqhe", probs, v, preferred_element_type=f32)
        attended = attended.reshape(own_rows, local_width).astype(bf16)
        branch_one = branch_one + dot(attended, out[m])
        kept.append((q, k, v, log_total, attended))
    middle = inputs + per_row(2) * branch_one
    normed_mid, rstd_mid = normal(middle)
    normed_two = (normed_mid * (1.0 + per_row(4)) + per_row(3)).astype(bf16)
    gate_two = per_row(5)
    dbranch_two = (gate_two * upstream).astype(bf16)
    branch_two = b_down.astype(f32)[None]
    dnormed_two = jnp.zeros((own_rows, width), f32)
    g_up, g_down, g_attn, gb_up, gb_qv = [], [], [], [], []
    for m in range(n_mp):
        pre = dot(normed_two, up[m]) + biases[m, 3 * local_width :][None]
        hidden, pull = jax.vjp(lambda v: jax.nn.gelu(v, approximate=True), pre)
        hidden = hidden.astype(bf16)
        branch_two = branch_two + dot(hidden, down[m])
        dpre = pull(col_inner(dbranch_two, down[m]))[0].astype(bf16)
        g_down.append(row_inner(hidden, dbranch_two).astype(bf16))
        g_up.append(row_inner(normed_two, dpre).astype(bf16))
        gb_up.append(jnp.sum(dpre.astype(f32), axis=0))
        dnormed_two = dnormed_two + col_inner(dpre, up[m])
    output = (middle + gate_two * branch_two).astype(bf16)
    gb_down = jnp.sum(dbranch_two.astype(f32), axis=0)
    dmiddle = upstream + normal_back(dnormed_two, per_row(4), normed_mid, rstd_mid)
    dbranch_one = (per_row(2) * dmiddle).astype(bf16)
    gb_out = jnp.sum(dbranch_one.astype(f32), axis=0)
    dnormed_one = jnp.zeros((own_rows, width), f32)
    for m in range(n_mp):
        q, k, v, log_total, attended = kept[m]
        g_out = row_inner(attended, dbranch_one).astype(bf16)
        datt = col_inner(dbranch_one, out[m]).astype(bf16).reshape(frames, SLOT, heads, HEAD)
        scores = jnp.einsum("bqhe,bkhe->bhqk", q, k, preferred_element_type=f32) * scale
        probs = jnp.exp(jnp.where(allowed, scores, -1e30) - log_total)
        dprobs = jnp.einsum("bqhe,bkhe->bhqk", datt, v, preferred_element_type=f32)
        dv = jnp.einsum("bhqk,bqhe->bkhe", probs.astype(bf16), datt, preferred_element_type=f32)
        rowdot = jnp.sum(dprobs * probs, axis=-1, keepdims=True)
        dscores = (probs * (dprobs - rowdot)).astype(bf16)
        dq = jnp.einsum("bhqk,bkhe->bqhe", dscores, k, preferred_element_type=f32) * scale
        dk = jnp.einsum("bhqk,bqhe->bkhe", dscores, q, preferred_element_type=f32) * scale
        dproj = jnp.concatenate(
            [t.reshape(own_rows, local_width).astype(bf16) for t in (dq, dk, dv)], axis=1
        )
        sums = jnp.sum(dproj.astype(f32), axis=0)
        gb_qv.append(jnp.concatenate([sums[:local_width], sums[2 * local_width :]]))
        g_attn.append(jnp.concatenate([row_inner(dproj, normed_one).astype(bf16), g_out], axis=0))
        dnormed_one = dnormed_one + col_inner(dproj, qkv[m])
    grad_tokens = (dmiddle + normal_back(dnormed_one, per_row(1), normed, rstd)).astype(bf16)

    chosen = [(item_id == item)[:, None] for item in range(items)]

    def by_item(values):
        return jnp.stack([jnp.sum(jnp.where(c, values, 0.0), axis=0) for c in chosen])

    item_grad = jnp.stack(
        [
            by_item(dnormed_one),
            by_item(dnormed_one * normed),
            by_item(dmiddle * branch_one),
            by_item(dnormed_two),
            by_item(dnormed_two * normed_mid),
            by_item(upstream * branch_two),
        ],
        axis=1,
    )
    item_grad = item_grad.reshape(items, 6, n_mp, local_width).transpose(2, 0, 1, 3)[order]

    if paired:
        total_items = items * n_dp
        dmod_all = jnp.zeros((n_mp, total_items, 6, local_width), f32)
        dmod_all = lax.dynamic_update_slice(dmod_all, item_grad, (0, dp * items, 0, 0))
        act_all = jnp.zeros((total_items, width), f32)
        act_all = lax.dynamic_update_slice(act_all, act_low.astype(f32), (dp * items, 0))
        act_all = jnp.where(mp == 0, act_all, 0.0)
        fixed = jnp.concatenate([act_all, gb_out[None], gb_down[None]])
        n_dmod = total_items * 6 * local_width // width
        n_qv = -(-2 * local_width // width)
        tail = jnp.concatenate(
            [
                dmod_all.reshape(n_mp, n_dmod, width),
                jnp.broadcast_to(fixed[None], (n_mp, *fixed.shape)),
                jnp.stack(gb_up)[:, None],
                jnp.pad(jnp.stack(gb_qv), ((0, 0), (0, n_qv * width - 2 * local_width))).reshape(
                    n_mp, n_qv, width
                ),
            ],
            axis=1,
        )
        tail = jnp.pad(tail, ((0, 0), (0, -tail.shape[1] % CHUNK), (0, 0))).astype(bf16)
        parts = jnp.concatenate(
            [jnp.stack(g_up), jnp.stack(g_down), jnp.stack(g_attn), tail], axis=1
        )
        total = reduce_grads(parts)
        g_up, g_down = total[:width], total[width : 2 * width]
        g_attn, tail = total[2 * width : 3 * width], total[3 * width :].astype(f32)
        dmod = tail[:n_dmod].reshape(total_items, 6, local_width)
        at = n_dmod
        act_all = tail[at : at + total_items]
        at = at + total_items
        gb_out, gb_down, gb_up = tail[at], tail[at + 1], tail[at + 2]
        gb_qv = tail[at + 3 : at + 3 + n_qv].reshape(-1)[: 2 * local_width]
        own_dmod = lax.dynamic_slice_in_dim(dmod, dp * items, items)
    else:

        def over_mp(values):
            return lax.psum_scatter(values, "mp", scatter_dimension=0, tiled=False)

        def over_dp(values):
            return lax.psum(values.astype(bf16), "dp").astype(f32)

        own_dmod = over_mp(item_grad)
        dmod = lax.all_gather(own_dmod, "dp", axis=0, tiled=True)
        act_all = lax.all_gather(act_low, "dp", axis=0, tiled=True).astype(f32)
        g_up, g_down, g_attn = (
            over_dp(over_mp(jnp.stack(parts))) for parts in (g_up, g_down, g_attn)
        )
        gb_up = over_dp(over_mp(jnp.stack(gb_up)))
        gb_qv = over_dp(over_mp(jnp.stack(gb_qv)))
        gb_out = lax.psum(gb_out, ("dp", "mp"))
        gb_down = lax.psum(gb_down, ("dp", "mp"))
    grad_w_ada = lax.dot_general(
        act_all, dmod.reshape(dmod.shape[0], -1), (((0,), (0,)), ((), ())), precision=lax.Precision.HIGHEST
    ).reshape(width, 6, local_width)
    grad_b_ada = jnp.sum(dmod, axis=0)
    cond_term = lax.dot_general(
        own_dmod.reshape(items, -1),
        ada_flat.astype(f32),
        (((1,), (1,)), ((), ())),
        precision=lax.Precision.HIGHEST,
    )
    if paired:
        cond_term = cond_term + swap(cond_term, "mp", 1)
        cond_term = cond_term + swap(cond_term, "mp", 2)
    else:
        cond_term = lax.psum(cond_term, "mp")
    grad_condition = jax.vjp(jax.nn.silu, cond_value)[1](cond_term)[0]
    g_qkv = g_attn[: 3 * local_width].astype(f32).T.reshape(width, 3, local_width)
    return (
        output,
        grad_tokens,
        grad_condition,
        g_qkv,
        gb_qv.reshape(2, local_width),
        g_attn[3 * local_width :].astype(f32),
        gb_out,
        g_up.astype(f32),
        gb_up,
        g_down.astype(f32),
        gb_down,
        grad_w_ada,
        grad_b_ada,
    )


def solution(mesh):
    paired = dict(mesh.shape) == {"dp": 8, "mp": 4}
    return jax.shard_map(
        functools.partial(shards, paired),
        mesh=mesh,
        in_specs=(
            P(("dp", "mp"), None),
            P("dp", None),
            P("dp"),
            P("dp"),
            P("dp"),
            P("dp"),
            P("dp"),
            P(None, None, "mp"),
            P(None, "mp"),
            P("mp", None),
            P(),
            P(None, "mp"),
            P("mp"),
            P("mp", None),
            P(),
            P(None, None, "mp"),
            P(None, "mp"),
            P(("dp", "mp"), None),
        ),
        out_specs=(
            P(("dp", "mp"), None),
            P(("dp", "mp"), None),
            P("dp", None),
            P(None, None, "mp"),
            P(None, "mp"),
            P("mp", None),
            P(),
            P(None, "mp"),
            P("mp"),
            P("mp", None),
            P(),
            P(None, None, "mp"),
            P(None, "mp"),
        ),
        check_vma=False,
    )
```

```python
import functools

import jax
import jax.numpy as jnp
from jax import lax
from jax.experimental import pallas as pl
from jax.experimental.pallas import tpu as pltpu
from jax.sharding import PartitionSpec as P

HEAD = 72
SLOT = 256
CHUNK = 128
UNITS = 4
OUT_SLOTS = 6
MESH = pl.DeviceIdType.MESH
epsilon = 1e-06
f32 = jnp.float32
bf16 = jnp.bfloat16


def frame_tables(grid_rows, grid_cols, frame_start, frame_item, used, first, length):
    rows = first + jnp.arange(length, dtype=jnp.int32)[:, None]
    slots = jnp.arange(grid_rows.shape[0], dtype=jnp.int32)[None, :]
    ends = (frame_start + grid_rows * grid_cols)[None, :]
    inside = (rows >= frame_start[None, :]) & (rows < ends) & (slots < used)
    frame_id = jnp.sum(jnp.where(inside, slots + 1, 0), axis=1) - 1
    item_id = jnp.sum(jnp.where(inside, frame_item[None, :], 0), axis=1)
    return (frame_id, item_id)


def normal(values):
    centred = values - jnp.mean(values, axis=-1, keepdims=True)
    rstd = lax.rsqrt(jnp.mean(centred * centred, axis=-1, keepdims=True) + epsilon)
    return centred * rstd, rstd


def normal_back(grad, scale, normed, rstd):
    u = grad * (1.0 + scale)
    return rstd * (
        u
        - jnp.mean(u, axis=-1, keepdims=True)
        - normed * jnp.mean(u * normed, axis=-1, keepdims=True)
    )


def dot(left, right):
    return jnp.dot(left, right, preferred_element_type=f32)


def pieces_of(ff):
    if ff % 128 or ff <= 640:
        return [(0, ff)]
    return [(0, 640), (640, ff - 640)]


def rows_at(i, size):
    return pl.ds(pl.multiple_of(i * size, size), size)


def pick(item_col, mod_ref, k):
    total = mod_ref[0, k : k + 1, :]
    for item in range(1, mod_ref.shape[0]):
        total = jnp.where(item_col == item, mod_ref[item, k : k + 1, :], total)
    return total


def add_by_item(sums_ref, k, item_col, values):
    for item in range(sums_ref.shape[0]):
        part = jnp.sum(jnp.where(item_col == item, values, 0.0), axis=0, keepdims=True)
        sums_ref[item, k : k + 1, :] += part


def tn(left, right):
    return lax.dot_general(left, right, (((0,), (0,)), ((), ())), preferred_element_type=f32)


def nt(left, right):
    return lax.dot_general(left, right, (((1,), (1,)), ((), ())), preferred_element_type=f32)


class Shard:
    def __init__(self, own, others, a, m, part, target, sem):
        self.own, self.others, self.a, self.m, self.part = own, others, a, m, part
        self.target, self.sem = target, sem

    def copy(self, source):
        return pltpu.make_async_copy(source.at[self.part], self.target, self.sem)

    def start(self):
        if self.own is None:
            self.copy(self.others.at[self.a, self.m]).start()
            return

        @pl.when(self.m == 0)
        def _():
            self.copy(self.own[self.a]).start()

        @pl.when(self.m > 0)
        def _():
            self.copy(self.others.at[self.a, self.m - 1]).start()

    def wait(self):
        source = self.others.at[self.a, 0] if self.own is None else self.own[self.a]
        self.copy(source).wait()


def pair_bias(id_col, id_row):
    shape = (SLOT, SLOT)
    one = lax.broadcasted_iota(jnp.int32, shape, 0) == lax.broadcasted_iota(jnp.int32, shape, 1)
    same = (id_col == id_row) & (id_col >= 0)
    return jnp.where(same | one, 0.0, -1e30)


def gather_ticks(own, w_all, sends, recvs):
    dp, mp = lax.axis_index("dp"), lax.axis_index("mp")
    core, yb = mp % 2, dp % 2
    xb, z0 = mp // 2, (dp // 2) % 2
    sib = (dp, mp + 1 - 2 * core)
    xn = (dp, mp + 2 - 4 * xb)
    yn = (dp + 1 - 2 * yb, mp)
    zn = (dp + 2 - 4 * z0, mp)
    rows = w_all.shape[2]
    part = rows // (UNITS * 9)
    count = len(own) * UNITS

    def greet():
        barrier = pltpu.get_barrier_semaphore()
        for peer in (sib, xn, yn, zn):
            pl.semaphore_signal(barrier, inc=1, device_id=peer, device_id_type=MESH)
        pl.semaphore_wait(barrier, 4)

    def remote(stage, slot, src, dst, peer):
        return pltpu.make_async_remote_copy(
            src_ref=src,
            dst_ref=dst,
            send_sem=sends.at[stage, slot],
            recv_sem=recvs.at[stage, slot],
            device_id=peer,
            device_id_type=MESH,
        )

    def near(a):
        return remote(7, a, own[a], w_all.at[a, 0], sib)

    def span(c, at, size):
        return pl.ds(pl.multiple_of((c % UNITS) * 9 * part + at * part, part), size * part)

    by_z, by_y = z0 * 2 + yb, 4 + yb * 2 + z0
    pair_z, pair_y = z0 * 2, 4 + yb * 2

    def x_copies(a, c):
        places = (span(c, by_z, 1), span(c, by_y, 1), span(c, 8, 1))
        return [
            remote(k, c % 2, own[a].at[place], w_all.at[a, 1, place], xn)
            for k, place in enumerate(places)
        ]

    def hand(stage, c, at, size, peer, to=1):
        src = w_all.at[c // UNITS, 1, span(c, at, size)]
        return remote(stage, c % 2, src, w_all.at[c // UNITS, to, span(c, at, size)], peer)

    def second(c):
        return [hand(3, c, by_z, 1, yn), hand(4, c, by_y, 1, zn)]

    def third(c):
        return [hand(5, c, pair_z, 2, zn), hand(6, c, pair_y, 2, yn)]

    def across(c):
        return hand(8, c, 0, 9, sib, 2)

    def begin():
        greet()
        for a in range(len(own)):
            near(a).start()

    def ready(a):
        near(a).wait()

    def tick(i):
        def stage(lag, work):
            c = i - lag

            @pl.when((c >= 0) & (c < count))
            def _():
                work(c)

        def leave(c):
            across(c).wait()

        def go_across(c):
            for copy in third(c):
                copy.wait()
            across(c).start()

        def go_third(c):
            for copy in second(c):
                copy.wait()
            for copy in third(c):
                copy.start()

        def go_second(c):
            for a in range(len(own)):

                @pl.when(c // UNITS == a)
                def _(a=a):
                    for copy in x_copies(a, c):
                        copy.wait()

            for copy in second(c):
                copy.start()

        def go_first(c):
            for a in range(len(own)):

                @pl.when(c // UNITS == a)
                def _(a=a):
                    for copy in x_copies(a, c):
                        copy.start()

        stage(4, leave)
        stage(3, go_across)
        stage(2, go_third)
        stage(1, go_second)
        stage(0, go_first)

    return begin, ready, tick, count + 5


def attend_kernel(n, heads, paired, *refs):
    if paired:
        tokens, item, ids, ids_row, mod, bias, b_out, *refs = refs
        *own, normed_ref, branch_ref, qkv_hbm, lse_ref, att_hbm, w_all, w_buf, qkv_buf, att_buf, w_sem, qkv_sem, att_sem = refs[:-2]
        begin, ready, tick, ticks = gather_ticks(own, w_all, *refs[-2:])
        begin()
    else:
        (
            tokens, item, ids, ids_row, mod, bias, b_out, w_all, normed_ref, branch_ref, qkv_hbm, lse_ref, att_hbm,
            w_buf, qkv_buf, att_buf, w_sem, qkv_sem, att_sem,
        ) = refs
        own = None
    rows, width = tokens.shape
    frames = rows // SLOT
    lw = heads * HEAD
    scale = HEAD ** (-0.5)

    def w_copy(m):
        return Shard(own, w_all, 0, m, slice(None), w_buf.at[m % 2], w_sem.at[m % 2])

    def qkv_copy(m):
        return pltpu.make_async_copy(qkv_buf.at[m % 2], qkv_hbm.at[m], qkv_sem.at[m % 2])

    def att_copy(m):
        return pltpu.make_async_copy(att_buf.at[m % 2], att_hbm.at[m], att_sem.at[m % 2])

    w_copy(0).start()

    def first(f, carry):
        if paired:
            tick(f)
        at = rows_at(f, SLOT)
        col = item[at, :]
        normed, _ = normal(tokens[at, :].astype(f32))
        normed_ref[at, :] = (normed * (1.0 + pick(col, mod, 1)) + pick(col, mod, 0)).astype(bf16)
        branch_ref[at, :] = jnp.broadcast_to(b_out[...], (SLOT, width))
        return carry

    lax.fori_loop(0, frames, first, 0)
    if paired:
        ready(0)

    def shard(m, carry):
        slot = m % 2
        w_copy(m).wait()

        @pl.when(m + 1 < (2 if paired else n))
        def _():
            w_copy(m + 1).start()

        @pl.when(m >= 2)
        def _():
            qkv_copy(m - 2).wait()
            att_copy(m - 2).wait()

        def frame(f, c):
            if paired:
                tick(frames + m * frames + f)
            at = rows_at(f, SLOT)
            proj = nt(w_buf[slot, : 3 * lw, :], normed_ref[at, :]) + bias[m]
            pairs = pair_bias(ids[at, :], ids_row[pl.ds(f, 1), :])
            outs = []
            for h in range(heads):
                q, k, v = (
                    proj[j * lw + h * HEAD : j * lw + (h + 1) * HEAD].astype(bf16)
                    for j in range(3)
                )
                qkv_buf[slot, h, :, at] = q
                qkv_buf[slot, heads + h, :, at] = k
                qkv_buf[slot, 2 * heads + h, :, at] = v
                scores = tn(k, q) * scale + pairs
                peak = jnp.max(scores, axis=0, keepdims=True)
                weights = jnp.exp(scores - peak)
                total = jnp.sum(weights, axis=0, keepdims=True)
                lse_ref[m, h : h + 1, at] = peak + jnp.log(total)
                probs = (weights * (1.0 / total)).astype(bf16)
                outs.append(jnp.dot(v, probs, preferred_element_type=f32))
            att = jnp.concatenate(outs, axis=0).astype(bf16)
            att_buf[slot, :, at] = att
            branch_ref[at, :] += tn(att, w_buf[slot, 3 * lw :, :])
            return c

        lax.fori_loop(0, frames, frame, 0)
        qkv_copy(m).start()
        att_copy(m).start()
        if paired:
            @pl.when((m >= 1) & (m + 1 < n))
            def _():
                w_copy(m + 1).start()

        return carry

    lax.fori_loop(0, n, shard, 0)
    if paired:

        def drain(i, carry):
            tick(i)
            return carry

        lax.fori_loop(frames * (n + 1), ticks, drain, 0)
        ready(1)
        ready(2)
    for m in range(max(n - 2, 0), n):
        qkv_copy(m).wait()
        att_copy(m).wait()


def attend(tokens, item, ids, mod, bias, b_out, weights, paired):
    rows, width = tokens.shape
    n = bias.shape[0]
    depth = weights[0].shape[-2]
    lw = depth // 4
    heads = lw // HEAD
    vmem = pl.BlockSpec(memory_space=pltpu.VMEM)
    hbm = pl.BlockSpec(memory_space=pl.ANY)
    return pl.pallas_call(
        functools.partial(attend_kernel, n, heads, paired),
        out_shape=(
            jax.ShapeDtypeStruct((rows, width), bf16),
            jax.ShapeDtypeStruct((rows, width), f32),
            jax.ShapeDtypeStruct((n, 3 * heads, HEAD, rows), bf16),
            jax.ShapeDtypeStruct((n, heads, rows), f32),
            jax.ShapeDtypeStruct((n, lw, rows), bf16),
        )
        + paired * (jax.ShapeDtypeStruct((3, n - 1, depth, width), bf16),),
        in_specs=[vmem] * 7 + [hbm] * len(weights),
        out_specs=(vmem, vmem, hbm, vmem, hbm) + paired * (hbm,),
        scratch_shapes=[
            pltpu.VMEM((2, depth, width), bf16),
            pltpu.VMEM((2, 3 * heads, HEAD, rows), bf16),
            pltpu.VMEM((2, lw, rows), bf16),
            pltpu.SemaphoreType.DMA((2,)),
            pltpu.SemaphoreType.DMA((2,)),
            pltpu.SemaphoreType.DMA((2,)),
        ]
        + paired
        * [
            pltpu.SemaphoreType.DMA((9, 3)),
            pltpu.SemaphoreType.DMA((9, 3)),
        ],
        compiler_params=pltpu.CompilerParams(
            collective_id=1 if paired else None, has_side_effects=paired, vmem_limit_bytes=56 << 20
        ),
    )(tokens, item[:, None], ids[:, None], ids.reshape(-1, SLOT), mod, bias, b_out, *weights)


def gelu_both(v):
    c = (2.0 / jnp.pi) ** 0.5
    square = v * v
    t = jnp.tanh(c * v * (1.0 + 0.044715 * square))
    half = 0.5 * (1.0 + t)
    slope = half + 0.5 * v * (1.0 - t * t) * (c * (1.0 + 3.0 * 0.044715 * square))
    return v * half, slope


def back_kernel(
    n, heads, pieces, tile, paired,
    tokens, upstream, branch_one, normed_hbm, item, ids, ids_row, mod, b_up, b_down, lse,
    w_all, own_attn, own_up, own_down, qkv_hbm, att_hbm,
    output_ref, gtok_ref, sums_ref, gb_down, gb_out, gb_up, gb_qv, g_all,
    n_buf, d_buf, acc_a, acc_b, up_buf, down_buf, w_buf, hid_buf, dpre_buf, stage_buf, qkv_buf, att_buf, dproj_buf,
    up_sem, down_sem, n_sem, stage_sem, w_sem, qkv_sem, att_sem,
):
    rows, width = tokens.shape
    lw = heads * HEAD
    frames = rows // SLOT
    scale = HEAD ** (-0.5)
    tiles = rows // tile
    own = (own_attn, own_up, own_down) if paired else None
    ff = w_all.shape[2]
    sums_ref[...] = jnp.zeros_like(sums_ref)
    gb_down[...] = jnp.zeros_like(gb_down)
    gb_out[...] = jnp.zeros_like(gb_out)
    gb_up[...] = jnp.zeros_like(gb_up)
    gb_qv[...] = jnp.zeros_like(gb_qv)

    def w_copies(p, m, slot):
        at, size = pieces[p]
        here = pl.ds(at, size)
        up_part, down_part = up_buf.at[slot, :, pl.ds(0, size)], down_buf.at[slot, pl.ds(0, size), :]
        return (
            Shard(own, w_all, 1, m, (slice(None), here), up_part, up_sem.at[slot]),
            Shard(own, w_all, 2, m, (here, slice(None)), down_part, down_sem.at[slot]),
        )

    for copy in w_copies(0, n - 1, 0):
        copy.start()

    def first(i, carry):
        at = rows_at(i, SLOT)
        col = item[at, :]
        middle = tokens[at, :].astype(f32) + pick(col, mod, 2) * branch_one[at, :]
        normed, _ = normal(middle)
        n_buf[at, :] = (normed * (1.0 + pick(col, mod, 4)) + pick(col, mod, 3)).astype(bf16)
        d = (pick(col, mod, 5) * upstream[at, :].astype(f32)).astype(bf16)
        d_buf[at, :] = d
        gb_down[...] += jnp.sum(d.astype(f32), axis=0, keepdims=True)
        acc_a[at, :] = jnp.broadcast_to(b_down[...], (SLOT, width))
        acc_b[at, :] = jnp.zeros((SLOT, width), f32)
        return carry

    lax.fori_loop(0, frames, first, 0)

    def flush(count, target, value):
        slot = count % 2
        size = value.shape[0]

        def copy(s):
            return pltpu.make_async_copy(
                stage_buf.at[s, pl.ds(0, size), :], target, stage_sem.at[s]
            )

        stage_buf[slot, pl.ds(0, size), :] = value.astype(bf16)
        dma = copy(slot)
        dma.start()
        dma.wait()

    for p, (p_at, p_size) in enumerate(pieces):

        def shard(i, carry, p=p, p_at=p_at, p_size=p_size):
            m = n - 1 - i
            slot = (p * n + i) % 2
            for copy in w_copies(p, m, slot):
                copy.wait()

            @pl.when(i + 1 < n)
            def _():
                for copy in w_copies(p, m - 1, 1 - slot):
                    copy.start()

            if p + 1 < len(pieces):

                @pl.when(i + 1 == n)
                def _():
                    for copy in w_copies(p + 1, n - 1, 1 - slot):
                        copy.start()

            bias = b_up[m, :, pl.ds(p_at, p_size)]
            up = up_buf.at[slot, :, pl.ds(0, p_size)]
            down = down_buf.at[slot, pl.ds(0, p_size), :]

            def part(j, c):
                at = rows_at(j, tile)
                pre = jnp.dot(n_buf[at, :], up[...], preferred_element_type=f32) + bias
                hidden, slope = gelu_both(pre)
                hidden = hidden.astype(bf16)
                dpre = nt(d_buf[at, :], down[...]) * slope
                dpre = dpre.astype(bf16)
                hid_buf[at, pl.ds(0, p_size)] = hidden
                dpre_buf[at, pl.ds(0, p_size)] = dpre
                gb_up[m, :, pl.ds(p_at, p_size)] += jnp.sum(
                    dpre.astype(f32), axis=0, keepdims=True
                )
                acc_a[at, :] += jnp.dot(hidden, down[...], preferred_element_type=f32)
                acc_b[at, :] += nt(dpre, up[...])
                return c

            lax.fori_loop(0, tiles, part, 0)
            flush(0, g_all.at[m, pl.ds(p_at, p_size), :], tn(hid_buf[:, pl.ds(0, p_size)], d_buf[...]))
            flush(1, g_all.at[m, pl.ds(ff + p_at, p_size), :], tn(dpre_buf[:, pl.ds(0, p_size)], n_buf[...]))
            return carry

        lax.fori_loop(0, n, shard, 0)

    def a_copies(m, slot):
        return (
            Shard(own, w_all, 0, m, slice(None), w_buf.at[slot], w_sem.at[slot]),
            pltpu.make_async_copy(qkv_hbm.at[m], qkv_buf.at[slot], qkv_sem.at[slot]),
            pltpu.make_async_copy(att_hbm.at[m], att_buf.at[slot], att_sem.at[slot]),
        )

    normed_copy = pltpu.make_async_copy(normed_hbm, n_buf, n_sem)
    normed_copy.start()
    for copy in a_copies(n - 1, 0):
        copy.start()

    def middle_part(i, carry):
        at = rows_at(i, SLOT)
        col = item[at, :]
        gate = pick(col, mod, 2)
        branch = branch_one[at, :]
        middle = tokens[at, :].astype(f32) + gate * branch
        dy = upstream[at, :].astype(f32)
        second = acc_a[at, :]
        output_ref[at, :] = (middle + pick(col, mod, 5) * second).astype(bf16)
        add_by_item(sums_ref, 5, col, dy * second)
        grad = acc_b[at, :]
        normed, rstd = normal(middle)
        add_by_item(sums_ref, 3, col, grad)
        add_by_item(sums_ref, 4, col, grad * normed)
        dmiddle = dy + normal_back(grad, pick(col, mod, 4), normed, rstd)
        acc_a[at, :] = dmiddle
        add_by_item(sums_ref, 2, col, dmiddle * branch)
        d = (gate * dmiddle).astype(bf16)
        d_buf[at, :] = d
        gb_out[...] += jnp.sum(d.astype(f32), axis=0, keepdims=True)
        acc_b[at, :] = jnp.zeros((SLOT, width), f32)
        return carry

    lax.fori_loop(0, frames, middle_part, 0)
    normed_copy.wait()

    def attn(i, carry):
        m = n - 1 - i
        slot = i % 2
        for copy in a_copies(m, slot):
            copy.wait()

        @pl.when(i + 1 < n)
        def _():
            for copy in a_copies(m - 1, 1 - slot):
                copy.start()

        def frame(f, c):
            at = rows_at(f, SLOT)
            datt = nt(w_buf[slot, pl.ds(3 * lw, lw), :], d_buf[at, :])
            pairs = pair_bias(ids[at, :], ids_row[pl.ds(f, 1), :])
            dqs, dks, dvs = [], [], []
            for h in range(heads):
                q = qkv_buf[slot, h, :, at]
                k = qkv_buf[slot, heads + h, :, at]
                v = qkv_buf[slot, 2 * heads + h, :, at]
                d = datt[h * HEAD : (h + 1) * HEAD].astype(bf16)
                scores = tn(k, q) * scale + pairs
                probs = jnp.exp(scores - lse[m, h : h + 1, at])
                dprobs = tn(v, d)
                inner = jnp.sum(dprobs * probs, axis=0, keepdims=True)
                dscores = (probs * (dprobs - inner)).astype(bf16)
                dvs.append(nt(d, probs.astype(bf16)))
                dqs.append(jnp.dot(k, dscores, preferred_element_type=f32) * scale)
                dks.append(nt(q, dscores) * scale)
            dproj = jnp.concatenate(dqs + dks + dvs, axis=0).astype(bf16)
            dproj_buf[:, at] = dproj
            gb_qv[m] += jnp.sum(dproj.astype(f32), axis=1, keepdims=True)
            acc_b[at, :] += tn(dproj, w_buf[slot, pl.ds(0, 3 * lw), :])
            return c

        lax.fori_loop(0, frames, frame, 0)
        flush(0, g_all.at[m, pl.ds(2 * ff + 3 * lw, lw), :], jnp.dot(att_buf[slot], d_buf[...], preferred_element_type=f32))
        for j in range(3):
            flush(1, g_all.at[m, pl.ds(2 * ff + j * lw, lw), :], jnp.dot(dproj_buf[pl.ds(j * lw, lw), :], n_buf[...], preferred_element_type=f32))
        return carry

    lax.fori_loop(0, n, attn, 0)

    def last(i, carry):
        at = rows_at(i, SLOT)
        col = item[at, :]
        normed, rstd = normal(tokens[at, :].astype(f32))
        grad = acc_b[at, :]
        add_by_item(sums_ref, 0, col, grad)
        add_by_item(sums_ref, 1, col, grad * normed)
        gtok_ref[at, :] = (
            acc_a[at, :] + normal_back(grad, pick(col, mod, 1), normed, rstd)
        ).astype(bf16)
        return carry

    lax.fori_loop(0, frames, last, 0)


def backward(tokens, upstream, branch_one, normed_one, item, ids, mod, b_up, b_down, lse, w_all, own, qkv, att):
    rows, width = tokens.shape
    n, ff = b_up.shape[0], b_up.shape[2]
    paired = bool(own)
    own = own or [w_all] * 3
    heads = qkv.shape[1] // 3
    lw = heads * HEAD
    pieces = pieces_of(ff)
    widest = max(size for _, size in pieces)
    tile = min(512, rows)
    vmem = pl.BlockSpec(memory_space=pltpu.VMEM)
    hbm = pl.BlockSpec(memory_space=pl.ANY)
    return pl.pallas_call(
        functools.partial(back_kernel, n, heads, pieces, tile, paired),
        out_shape=(
            jax.ShapeDtypeStruct((rows, width), bf16),
            jax.ShapeDtypeStruct((rows, width), bf16),
            jax.ShapeDtypeStruct(mod.shape, f32),
            jax.ShapeDtypeStruct((1, width), f32),
            jax.ShapeDtypeStruct((1, width), f32),
            jax.ShapeDtypeStruct((n, 1, ff), f32),
            jax.ShapeDtypeStruct((n, 3 * lw, 1), f32),
            jax.ShapeDtypeStruct((n, 2 * ff + 4 * lw, width), bf16),
        ),
        in_specs=[vmem] * 3 + [hbm] + [vmem] * 7 + [hbm] * 6,
        out_specs=(vmem,) * 7 + (hbm,),
        scratch_shapes=[
            pltpu.VMEM((rows, width), bf16),
            pltpu.VMEM((rows, width), bf16),
            pltpu.VMEM((rows, width), f32),
            pltpu.VMEM((rows, width), f32),
            pltpu.VMEM((2, width, widest), bf16),
            pltpu.VMEM((2, widest, width), bf16),
            pltpu.VMEM((2, 4 * lw, width), bf16),
            pltpu.VMEM((rows, widest), bf16),
            pltpu.VMEM((rows, widest), bf16),
            pltpu.VMEM((2, max(widest, lw), width), bf16),
            pltpu.VMEM((2, 3 * heads, HEAD, rows), bf16),
            pltpu.VMEM((2, lw, rows), bf16),
            pltpu.VMEM((3 * lw, rows), bf16),
            pltpu.SemaphoreType.DMA((2,)),
            pltpu.SemaphoreType.DMA((2,)),
            pltpu.SemaphoreType.DMA,
            pltpu.SemaphoreType.DMA((2,)),
            pltpu.SemaphoreType.DMA((2,)),
            pltpu.SemaphoreType.DMA((2,)),
            pltpu.SemaphoreType.DMA((2,)),
        ],
        compiler_params=pltpu.CompilerParams(vmem_limit_bytes=60 << 20),
    )(
        tokens, upstream, branch_one, normed_one, item[:, None], ids[:, None], ids.reshape(-1, SLOT),
        mod, b_up, b_down, lse, w_all, *own, qkv, att,
    )


def reduce_kernel(count, g_ref, tail_ref, out_ref, lp, rd, s0, sx, rx, tb, ry, ub, rz1, vb, rz2, ob, loads, sends, recvs, outs):
    dp, mp = lax.axis_index("dp"), lax.axis_index("mp")
    core, yb = mp % 2, dp % 2
    xb, z0, z1 = mp // 2, (dp // 2) % 2, dp // 4
    sib = (dp, mp + 1 - 2 * core)
    xn = (dp, mp + 2 - 4 * xb)
    yn = (dp + 1 - 2 * yb, mp)
    z1n = (dp + 2 - 4 * z0, mp)
    z2n = (dp + 4 - 8 * z1, mp)
    half, quarter, eighth = CHUNK // 2, CHUNK // 4, CHUNK // 8

    barrier = pltpu.get_barrier_semaphore()
    for peer in (sib, xn, yn, z1n, z2n):
        pl.semaphore_signal(barrier, inc=1, device_id=peer, device_id_type=MESH)
    pl.semaphore_wait(barrier, 5)

    def rows_of(c):
        return pl.ds(pl.multiple_of(c * CHUNK, CHUNK), CHUNK)

    def remote(stage, src, dst, peer, slot):
        return pltpu.make_async_remote_copy(
            src_ref=src,
            dst_ref=dst,
            send_sem=sends.at[stage, slot],
            recv_sem=recvs.at[stage, slot],
            device_id=peer,
            device_id_type=MESH,
        )

    main = g_ref.shape[1] // CHUNK

    def load(which, c, slot, ref):
        part = ref.at[2 * which, rows_of(c)]
        return pltpu.make_async_copy(part, lp.at[slot, which], loads.at[which, slot])

    def d_copy(which, c, slot, ref):
        return remote(which, ref.at[2 * which + 1, rows_of(c)], rd.at[slot, which], sib, slot)

    def x_copy(c, slot):
        return remote(2, sx.at[slot], rx.at[slot], xn, slot)

    def y_copy(c, slot):
        part = pl.ds(pl.multiple_of((1 - yb) * half, half), half)
        return remote(3, tb.at[slot, part], ry.at[slot], yn, slot)

    def z1_copy(c, slot):
        part = pl.ds(pl.multiple_of((1 - z0) * quarter, quarter), quarter)
        return remote(4, ub.at[slot, part], rz1.at[slot], z1n, slot)

    def z2_copy(c, slot):
        part = pl.ds(pl.multiple_of((1 - z1) * eighth, eighth), eighth)
        return remote(5, vb.at[slot, part], rz2.at[slot], z2n, slot)

    at_y = pl.multiple_of(yb * half, half)
    at_z1 = pl.multiple_of(yb * half + z0 * quarter, quarter)
    at_z2 = pl.multiple_of(yb * half + z0 * quarter + z1 * eighth, eighth)

    def back(stage, at, size, peer, c, slot):
        place = ob.at[c % OUT_SLOTS, pl.ds(at, size)]
        return remote(stage, place, place, peer, slot)

    def az2_copy(c, slot):
        return back(6, at_z2, eighth, z2n, c, slot)

    def az1_copy(c, slot):
        return back(7, at_z1, quarter, z1n, c, slot)

    def ay_copy(c, slot):
        return back(8, at_y, half, yn, c, slot)

    def out_copy(c, slot):
        return pltpu.make_async_copy(ob.at[c % OUT_SLOTS], out_ref.at[rows_of(c)], outs.at[slot])

    def step(i, carry):
        def stage(lag, work):
            c = i - lag

            @pl.when((c >= 0) & (c < count))
            def _():
                work(c, c % 2)

        def leave(c, slot):
            out_copy(c, slot).wait()

        def store(c, slot):
            ay_copy(c, slot).wait()
            out_copy(c, slot).start()

        def go_ay(c, slot):
            az1_copy(c, slot).wait()
            ay_copy(c, slot).start()

        def go_az1(c, slot):
            az2_copy(c, slot).wait()
            az1_copy(c, slot).start()

        def go_az2(c, slot):
            z2_copy(c, slot).wait()
            mine = vb[slot, pl.ds(pl.multiple_of(z1 * eighth, eighth), eighth)] + rz2[slot]
            ob[c % OUT_SLOTS, pl.ds(at_z2, eighth)] = mine
            az2_copy(c, slot).start()

        def go_z2(c, slot):
            z1_copy(c, slot).wait()
            vb[slot] = ub[slot, pl.ds(pl.multiple_of(z0 * quarter, quarter), quarter)] + rz1[slot]
            z2_copy(c, slot).start()

        def go_z1(c, slot):
            y_copy(c, slot).wait()
            ub[slot] = tb[slot, pl.ds(pl.multiple_of(yb * half, half), half)] + ry[slot]
            z1_copy(c, slot).start()

        def go_y(c, slot):
            x_copy(c, slot).wait()
            tb[slot] = s0[slot] + rx[slot]
            y_copy(c, slot).start()

        def go_x(c, slot):
            for which in range(2):
                load(which, 0, slot, g_ref).wait()
                d_copy(which, 0, slot, g_ref).wait()
            sx[slot] = lp[slot, 1] + rd[slot, 1]
            s0[slot] = lp[slot, 0] + rd[slot, 0]
            x_copy(c, slot).start()

        def go_d(c, slot):
            @pl.when(c < main)
            def _():
                for which in range(2):
                    load(which, c, slot, g_ref).start()
                    d_copy(which, c, slot, g_ref).start()

            @pl.when(c >= main)
            def _():
                for which in range(2):
                    load(which, c - main, slot, tail_ref).start()
                    d_copy(which, c - main, slot, tail_ref).start()

        stage(9, leave)
        stage(8, store)
        stage(7, go_ay)
        stage(6, go_az1)
        stage(5, go_az2)
        stage(4, go_z2)
        stage(3, go_z1)
        stage(2, go_y)
        stage(1, go_x)
        stage(0, go_d)
        return carry

    lax.fori_loop(0, count + 10, step, 0)


def reduce_grads(parts, tail):
    rows, width = parts.shape[1] + tail.shape[1], parts.shape[2]
    count = rows // CHUNK
    half, quarter, eighth = CHUNK // 2, CHUNK // 4, CHUNK // 8

    def buf(*lead):
        return pltpu.VMEM((*lead, width), bf16)

    return pl.pallas_call(
        functools.partial(reduce_kernel, count),
        out_shape=jax.ShapeDtypeStruct((rows, width), bf16),
        in_specs=[pl.BlockSpec(memory_space=pl.ANY)] * 2,
        out_specs=pl.BlockSpec(memory_space=pl.ANY),
        scratch_shapes=[
            buf(2, 2, CHUNK),
            buf(2, 2, CHUNK),
            buf(2, CHUNK),
            buf(2, CHUNK),
            buf(2, CHUNK),
            buf(2, CHUNK),
            buf(2, half),
            buf(2, half),
            buf(2, quarter),
            buf(2, quarter),
            buf(2, eighth),
            buf(OUT_SLOTS, CHUNK),
            pltpu.SemaphoreType.DMA((2, 2)),
            pltpu.SemaphoreType.DMA((9, 2)),
            pltpu.SemaphoreType.DMA((9, 2)),
            pltpu.SemaphoreType.DMA((2,)),
        ],
        compiler_params=pltpu.CompilerParams(
            collective_id=0, has_side_effects=True, vmem_limit_bytes=32 << 20
        ),
    )(parts, tail)


def swap(values, axis, bit):
    n = lax.axis_size(axis)
    return lax.ppermute(values, axis, [(i, i ^ bit) for i in range(n)])


def shards(
    paired,
    tokens,
    condition,
    grid_rows,
    grid_cols,
    frame_start,
    frame_item,
    group_frames,
    w_qkv,
    qv_bias,
    w_out,
    b_out,
    w_up,
    b_up,
    w_down,
    b_down,
    w_ada,
    b_ada,
    cotangent,
):
    own_rows, width = tokens.shape
    local_width = w_qkv.shape[2]
    local_ff = w_up.shape[1]
    items = condition.shape[0]
    n_mp, n_dp = lax.axis_size("mp"), lax.axis_size("dp")
    mp, dp = lax.axis_index("mp"), lax.axis_index("dp")
    n = width // (4 * HEAD)
    lw, ff = width // n, local_ff * n_mp // n
    frame_id, item_id = frame_tables(
        grid_rows, grid_cols, frame_start, frame_item, group_frames[0], mp * own_rows, own_rows
    )
    cond_value = condition.astype(f32)
    act_low = jax.nn.silu(cond_value).astype(bf16)
    ada_flat = w_ada.reshape(width, -1)
    ada_local = dot(act_low, ada_flat) + b_ada.reshape(-1).astype(f32)
    ada_local = ada_local.reshape(items, 6, local_width)
    qkv_local = w_qkv.transpose(1, 2, 0)
    if paired:
        qkv_bias = jnp.concatenate(
            [qv_bias[0].astype(f32), jnp.zeros((lw,), f32), qv_bias[1].astype(f32)]
        )
        small = jnp.concatenate([ada_local.reshape(-1), qkv_bias, b_up.astype(f32)])
        small = jnp.stack([small] + [swap(small, "mp", bit) for bit in range(1, n)])
        n_ada = ada_local.size
        modulation = small[mp ^ jnp.arange(n), :n_ada].reshape(n, items, 6, lw)
        qkv_bias = small[:, n_ada : n_ada + 3 * lw]
        up_bias = small[:, n_ada + 3 * lw :]
        weights = [
            jnp.concatenate([qkv_local.reshape(3 * lw, width), w_out], axis=0),
            w_up,
            w_down,
        ]
    else:
        modulation = lax.all_gather(ada_local, "mp", axis=0)
        qv = lax.all_gather(qv_bias.astype(f32), "mp", axis=1, tiled=True)
        qkv_bias = jnp.stack([qv[0], jnp.zeros((width,), f32), qv[1]])
        qkv_bias = qkv_bias.reshape(3, n, lw).transpose(1, 0, 2).reshape(n, 3 * lw)
        up_bias = lax.all_gather(b_up.astype(f32), "mp", axis=0, tiled=True).reshape(n, ff)
        qkv = lax.all_gather(qkv_local, "mp", axis=1, tiled=True)
        qkv = qkv.reshape(3, n, lw, width).transpose(1, 0, 2, 3).reshape(n, 3 * lw, width)
        out = lax.all_gather(w_out, "mp", axis=0, tiled=True).reshape(n, lw, width)
        up = lax.all_gather(w_up, "mp", axis=1, tiled=True)
        up = up.reshape(width, n, ff).transpose(1, 0, 2)
        down = lax.all_gather(w_down, "mp", axis=0, tiled=True).reshape(n, ff, width)
        weights = [jnp.stack([jnp.concatenate([qkv, out], axis=1), up, down])]
    modulation = modulation.transpose(1, 2, 0, 3).reshape(items, 6, width)
    b_out_row, b_down_row = (b.astype(f32)[None] for b in (b_out, b_down))
    normed_one, branch_one, qkv, lse, att, *gathered = attend(
        tokens, item_id, frame_id, modulation, qkv_bias[:, :, None], b_out_row, weights, paired
    )
    w_all = gathered[0] if paired else weights[0]
    output, grad_tokens, item_grad, gb_down, gb_out, gb_up, gb_qv, g_all = backward(
        tokens,
        cotangent,
        branch_one,
        normed_one,
        item_id,
        frame_id,
        modulation,
        up_bias[:, None],
        b_down_row,
        lse,
        w_all,
        weights if paired else [],
        qkv,
        att,
    )
    gb_qv = gb_qv.reshape(n, 3, lw)[:, ::2]

    if paired:
        item_grad = item_grad.reshape(items, 6, n, lw).transpose(2, 0, 1, 3)[mp ^ jnp.arange(n)]
        total_items = items * n_dp
        dmod_all = jnp.zeros((n, total_items, 6, lw), f32)
        dmod_all = lax.dynamic_update_slice(dmod_all, item_grad, (0, dp * items, 0, 0))
        act_all = jnp.zeros((total_items, width), f32)
        act_all = lax.dynamic_update_slice(act_all, act_low.astype(f32), (dp * items, 0))
        act_all = jnp.where(mp == 0, act_all, 0.0)
        fixed = jnp.concatenate([act_all, gb_out, gb_down])
        n_dmod = total_items * 6 * lw // width
        tail = jnp.concatenate(
            [
                dmod_all.reshape(n, n_dmod, width),
                jnp.broadcast_to(fixed[None], (n, *fixed.shape)),
                gb_up,
                jnp.pad(gb_qv.reshape(n, 1, 2 * lw), ((0, 0), (0, 0), (0, width - 2 * lw))),
            ],
            axis=1,
        )
        tail = jnp.pad(tail, ((0, 0), (0, -tail.shape[1] % CHUNK), (0, 0))).astype(bf16)
        total = reduce_grads(g_all, tail)
        tail = total[2 * ff + 4 * lw :].astype(f32)
        g_down, g_up = total[:ff].astype(f32), total[ff : 2 * ff].astype(f32).T
        g_qkv = total[2 * ff : 2 * ff + 3 * lw].astype(f32).T.reshape(width, 3, lw)
        g_out = total[2 * ff + 3 * lw : 2 * ff + 4 * lw].astype(f32)
        dmod = tail[:n_dmod].reshape(total_items, 6, lw)
        at = n_dmod
        act_all = tail[at : at + total_items]
        at = at + total_items
        gb_out, gb_down, gb_up = tail[at], tail[at + 1], tail[at + 2]
        gb_qv = tail[at + 3, : 2 * lw].reshape(2, lw)
        own_dmod = lax.dynamic_slice_in_dim(dmod, dp * items, items)
    else:

        def over_all(values, axis):
            part = lax.psum_scatter(values, "mp", scatter_dimension=axis, tiled=True)
            return lax.psum(part.astype(bf16), "dp").astype(f32)

        own_dmod = lax.psum_scatter(item_grad, "mp", scatter_dimension=2, tiled=True)
        dmod = lax.all_gather(own_dmod, "dp", axis=0, tiled=True)
        act_all = lax.all_gather(act_low, "dp", axis=0, tiled=True).astype(f32)
        g_down = over_all(g_all[:, :ff].reshape(n * ff, width), 0)
        g_up = over_all(g_all[:, ff : 2 * ff].reshape(n * ff, width).T, 1)
        g_qkv = g_all[:, 2 * ff : 2 * ff + 3 * lw].reshape(n, 3, lw, width)
        g_qkv = over_all(g_qkv.transpose(3, 1, 0, 2).reshape(width, 3, width), 2)
        g_out = over_all(g_all[:, 2 * ff + 3 * lw :].reshape(width, width), 0)
        gb_up = over_all(gb_up.reshape(-1), 0)
        gb_qv = over_all(gb_qv.transpose(1, 0, 2).reshape(2, width), 1)
        gb_out = lax.psum(gb_out[0], ("dp", "mp"))
        gb_down = lax.psum(gb_down[0], ("dp", "mp"))
    grad_w_ada = lax.dot_general(
        act_all,
        dmod.reshape(dmod.shape[0], -1),
        (((0,), (0,)), ((), ())),
        precision=lax.Precision.HIGHEST,
    ).reshape(width, 6, local_width)
    grad_b_ada = jnp.sum(dmod, axis=0)
    cond_term = lax.dot_general(
        own_dmod.reshape(items, -1),
        ada_flat.astype(f32),
        (((1,), (1,)), ((), ())),
        precision=lax.Precision.HIGHEST,
    )
    if paired:
        cond_term = cond_term + swap(cond_term, "mp", 1)
        cond_term = cond_term + swap(cond_term, "mp", 2)
    else:
        cond_term = lax.psum(cond_term, "mp")
    grad_condition = jax.vjp(jax.nn.silu, cond_value)[1](cond_term)[0]
    return (
        output,
        grad_tokens,
        grad_condition,
        g_qkv,
        gb_qv,
        g_out,
        gb_out,
        g_up,
        gb_up,
        g_down,
        gb_down,
        grad_w_ada,
        grad_b_ada,
    )


def solution(mesh):
    paired = dict(mesh.shape) == {"dp": 8, "mp": 4}
    return jax.shard_map(
        functools.partial(shards, paired),
        mesh=mesh,
        in_specs=(
            P(("dp", "mp"), None),
            P("dp", None),
            P("dp"),
            P("dp"),
            P("dp"),
            P("dp"),
            P("dp"),
            P(None, None, "mp"),
            P(None, "mp"),
            P("mp", None),
            P(),
            P(None, "mp"),
            P("mp"),
            P("mp", None),
            P(),
            P(None, None, "mp"),
            P(None, "mp"),
            P(("dp", "mp"), None),
        ),
        out_specs=(
            P(("dp", "mp"), None),
            P(("dp", "mp"), None),
            P("dp", None),
            P(None, None, "mp"),
            P(None, "mp"),
            P("mp", None),
            P(),
            P(None, "mp"),
            P("mp"),
            P("mp", None),
            P(),
            P(None, None, "mp"),
            P(None, "mp"),
        ),
        check_vma=False,
    )
```

```python
import functools

import jax
import jax.numpy as jnp
from jax import lax
from jax.experimental import pallas as pl
from jax.experimental.pallas import tpu as pltpu
from jax.sharding import PartitionSpec as P

HEAD = 72
SLOT = 256
CHUNK = 128
UNITS = 4
OUT_SLOTS = 6
MESH = pl.DeviceIdType.MESH
epsilon = 1e-06
f32 = jnp.float32
bf16 = jnp.bfloat16


def frame_tables(grid_rows, grid_cols, frame_start, frame_item, used, first, length):
    rows = first + jnp.arange(length, dtype=jnp.int32)[:, None]
    slots = jnp.arange(grid_rows.shape[0], dtype=jnp.int32)[None, :]
    ends = (frame_start + grid_rows * grid_cols)[None, :]
    inside = (rows >= frame_start[None, :]) & (rows < ends) & (slots < used)
    frame_id = jnp.sum(jnp.where(inside, slots + 1, 0), axis=1) - 1
    item_id = jnp.sum(jnp.where(inside, frame_item[None, :], 0), axis=1)
    return (frame_id, item_id)


def normal(values):
    centred = values - jnp.mean(values, axis=-1, keepdims=True)
    rstd = lax.rsqrt(jnp.mean(centred * centred, axis=-1, keepdims=True) + epsilon)
    return centred * rstd, rstd


def normal_back(grad, scale, normed, rstd):
    u = grad * (1.0 + scale)
    return rstd * (
        u
        - jnp.mean(u, axis=-1, keepdims=True)
        - normed * jnp.mean(u * normed, axis=-1, keepdims=True)
    )


def dot(left, right):
    return jnp.dot(left, right, preferred_element_type=f32)


def rows_at(i, size):
    return pl.ds(pl.multiple_of(i * size, size), size)


def pick(item_col, mod_ref, k):
    total = mod_ref[0, k : k + 1, :]
    for item in range(1, mod_ref.shape[0]):
        total = jnp.where(item_col == item, mod_ref[item, k : k + 1, :], total)
    return total


def add_by_item(sums_ref, k, item_col, values):
    for item in range(sums_ref.shape[0]):
        part = jnp.sum(jnp.where(item_col == item, values, 0.0), axis=0, keepdims=True)
        sums_ref[item, k : k + 1, :] += part


def tn(left, right):
    return lax.dot_general(left, right, (((0,), (0,)), ((), ())), preferred_element_type=f32)


def nt(left, right):
    return lax.dot_general(left, right, (((1,), (1,)), ((), ())), preferred_element_type=f32)


class Shard:
    def __init__(self, own, others, a, m, part, target, sem):
        self.own, self.others, self.a, self.m, self.part = own, others, a, m, part
        self.target, self.sem = target, sem

    def copy(self, source):
        return pltpu.make_async_copy(source.at[self.part], self.target, self.sem)

    def start(self):
        if self.own is None:
            self.copy(self.others.at[self.a, self.m]).start()
            return

        @pl.when(self.m == 0)
        def _():
            self.copy(self.own[self.a]).start()

        @pl.when(self.m > 0)
        def _():
            self.copy(self.others.at[self.a, self.m - 1]).start()

    def wait(self):
        source = self.others.at[self.a, 0] if self.own is None else self.own[self.a]
        self.copy(source).wait()


def pair_bias(id_col, id_row):
    shape = (SLOT, SLOT)
    one = lax.broadcasted_iota(jnp.int32, shape, 0) == lax.broadcasted_iota(jnp.int32, shape, 1)
    same = (id_col == id_row) & (id_col >= 0)
    return jnp.where(same | one, 0.0, -1e30)


def gather_ticks(own, w_all, sends, recvs):
    dp, mp = lax.axis_index("dp"), lax.axis_index("mp")
    core, yb = mp % 2, dp % 2
    xb, z0 = mp // 2, (dp // 2) % 2
    sib = (dp, mp + 1 - 2 * core)
    xn = (dp, mp + 2 - 4 * xb)
    yn = (dp + 1 - 2 * yb, mp)
    zn = (dp + 2 - 4 * z0, mp)
    rows = w_all.shape[2]
    part = rows // (UNITS * 9)
    count = len(own) * UNITS

    def greet():
        barrier = pltpu.get_barrier_semaphore()
        for peer in (sib, xn, yn, zn):
            pl.semaphore_signal(barrier, inc=1, device_id=peer, device_id_type=MESH)
        pl.semaphore_wait(barrier, 4)

    def remote(stage, slot, src, dst, peer):
        return pltpu.make_async_remote_copy(
            src_ref=src,
            dst_ref=dst,
            send_sem=sends.at[stage, slot],
            recv_sem=recvs.at[stage, slot],
            device_id=peer,
            device_id_type=MESH,
        )

    def near(a):
        return remote(7, a, own[a], w_all.at[a, 0], sib)

    def span(c, at, size):
        return pl.ds(pl.multiple_of((c % UNITS) * 9 * part + at * part, part), size * part)

    by_z, by_y = z0 * 2 + yb, 4 + yb * 2 + z0
    pair_z, pair_y = z0 * 2, 4 + yb * 2

    def x_copies(a, c):
        places = (span(c, by_z, 1), span(c, by_y, 1), span(c, 8, 1))
        return [
            remote(k, c % 2, own[a].at[place], w_all.at[a, 1, place], xn)
            for k, place in enumerate(places)
        ]

    def hand(stage, c, at, size, peer, to=1):
        src = w_all.at[c // UNITS, 1, span(c, at, size)]
        return remote(stage, c % 2, src, w_all.at[c // UNITS, to, span(c, at, size)], peer)

    def second(c):
        return [hand(3, c, by_z, 1, yn), hand(4, c, by_y, 1, zn)]

    def third(c):
        return [hand(5, c, pair_z, 2, zn), hand(6, c, pair_y, 2, yn)]

    def across(c):
        return hand(8, c, 0, 9, sib, 2)

    def begin():
        greet()
        for a in range(len(own)):
            near(a).start()

    def ready(a):
        near(a).wait()

    def tick(i):
        def stage(lag, work):
            c = i - lag

            @pl.when((c >= 0) & (c < count))
            def _():
                work(c)

        def leave(c):
            across(c).wait()

        def go_across(c):
            for copy in third(c):
                copy.wait()
            across(c).start()

        def go_third(c):
            for copy in second(c):
                copy.wait()
            for copy in third(c):
                copy.start()

        def go_second(c):
            for a in range(len(own)):

                @pl.when(c // UNITS == a)
                def _(a=a):
                    for copy in x_copies(a, c):
                        copy.wait()

            for copy in second(c):
                copy.start()

        def go_first(c):
            for a in range(len(own)):

                @pl.when(c // UNITS == a)
                def _(a=a):
                    for copy in x_copies(a, c):
                        copy.start()

        stage(4, leave)
        stage(3, go_across)
        stage(2, go_third)
        stage(1, go_second)
        stage(0, go_first)

    return begin, ready, tick, count + 5


def attend_kernel(n, heads, paired, *refs):
    if paired:
        tokens, item, ids, ids_row, mod, bias, b_out, *refs = refs
        *own, normed_ref, branch_ref, qkv_hbm, lse_ref, att_hbm, w_all, w_buf, qkv_buf, att_buf, w_sem, qkv_sem, att_sem = refs[:-2]
        begin, ready, tick, ticks = gather_ticks(own, w_all, *refs[-2:])
        begin()
    else:
        (
            tokens, item, ids, ids_row, mod, bias, b_out, w_all, normed_ref, branch_ref, qkv_hbm, lse_ref, att_hbm,
            w_buf, qkv_buf, att_buf, w_sem, qkv_sem, att_sem,
        ) = refs
        own = None
    rows, width = tokens.shape
    frames = rows // SLOT
    lw = heads * HEAD
    scale = HEAD ** (-0.5)

    def w_copy(m):
        return Shard(own, w_all, 0, m, slice(None), w_buf.at[m % 2], w_sem.at[m % 2])

    def qkv_copy(m):
        return pltpu.make_async_copy(qkv_buf.at[m % 2], qkv_hbm.at[m], qkv_sem.at[m % 2])

    def att_copy(m):
        return pltpu.make_async_copy(att_buf.at[m % 2], att_hbm.at[m], att_sem.at[m % 2])

    w_copy(0).start()

    def first(f, carry):
        if paired:
            tick(f)
        at = rows_at(f, SLOT)
        col = item[at, :]
        normed, _ = normal(tokens[at, :].astype(f32))
        normed_ref[at, :] = (normed * (1.0 + pick(col, mod, 1)) + pick(col, mod, 0)).astype(bf16)
        branch_ref[at, :] = jnp.broadcast_to(b_out[...], (SLOT, width))
        return carry

    lax.fori_loop(0, frames, first, 0)
    if paired:
        ready(0)

    def shard(m, carry):
        slot = m % 2
        w_copy(m).wait()

        @pl.when(m + 1 < (2 if paired else n))
        def _():
            w_copy(m + 1).start()

        @pl.when(m >= 2)
        def _():
            qkv_copy(m - 2).wait()
            att_copy(m - 2).wait()

        def frame(f, c):
            if paired:
                tick(frames + m * frames + f)
            at = rows_at(f, SLOT)
            proj = nt(w_buf[slot, : 3 * lw, :], normed_ref[at, :]) + bias[m]
            pairs = pair_bias(ids[at, :], ids_row[pl.ds(f, 1), :])
            outs = []
            for h in range(heads):
                q, k, v = (
                    proj[j * lw + h * HEAD : j * lw + (h + 1) * HEAD].astype(bf16)
                    for j in range(3)
                )
                qkv_buf[slot, h, :, at] = q
                qkv_buf[slot, heads + h, :, at] = k
                qkv_buf[slot, 2 * heads + h, :, at] = v
                scores = tn(k, q) * scale + pairs
                peak = jnp.max(scores, axis=0, keepdims=True)
                weights = jnp.exp(scores - peak)
                total = jnp.sum(weights, axis=0, keepdims=True)
                lse_ref[m, h : h + 1, at] = peak + jnp.log(total)
                probs = (weights * (1.0 / total)).astype(bf16)
                outs.append(jnp.dot(v, probs, preferred_element_type=f32))
            att = jnp.concatenate(outs, axis=0).astype(bf16)
            att_buf[slot, :, at] = att
            branch_ref[at, :] += tn(att, w_buf[slot, 3 * lw :, :])
            return c

        lax.fori_loop(0, frames, frame, 0)
        qkv_copy(m).start()
        att_copy(m).start()
        if paired:
            @pl.when((m >= 1) & (m + 1 < n))
            def _():
                w_copy(m + 1).start()

        return carry

    lax.fori_loop(0, n, shard, 0)
    if paired:

        def drain(i, carry):
            tick(i)
            return carry

        lax.fori_loop(frames * (n + 1), ticks, drain, 0)
        ready(1)
        ready(2)
    for m in range(max(n - 2, 0), n):
        qkv_copy(m).wait()
        att_copy(m).wait()


def attend(tokens, item, ids, mod, bias, b_out, weights, paired):
    rows, width = tokens.shape
    n = bias.shape[0]
    depth = weights[0].shape[-2]
    lw = depth // 4
    heads = lw // HEAD
    vmem = pl.BlockSpec(memory_space=pltpu.VMEM)
    hbm = pl.BlockSpec(memory_space=pl.ANY)
    return pl.pallas_call(
        functools.partial(attend_kernel, n, heads, paired),
        out_shape=(
            jax.ShapeDtypeStruct((rows, width), bf16),
            jax.ShapeDtypeStruct((rows, width), f32),
            jax.ShapeDtypeStruct((n, 3 * heads, HEAD, rows), bf16),
            jax.ShapeDtypeStruct((n, heads, rows), f32),
            jax.ShapeDtypeStruct((n, lw, rows), bf16),
        )
        + paired * (jax.ShapeDtypeStruct((3, n - 1, depth, width), bf16),),
        in_specs=[vmem] * 7 + [hbm] * len(weights),
        out_specs=(vmem, vmem, hbm, vmem, hbm) + paired * (hbm,),
        scratch_shapes=[
            pltpu.VMEM((2, depth, width), bf16),
            pltpu.VMEM((2, 3 * heads, HEAD, rows), bf16),
            pltpu.VMEM((2, lw, rows), bf16),
            pltpu.SemaphoreType.DMA((2,)),
            pltpu.SemaphoreType.DMA((2,)),
            pltpu.SemaphoreType.DMA((2,)),
        ]
        + paired
        * [
            pltpu.SemaphoreType.DMA((9, 3)),
            pltpu.SemaphoreType.DMA((9, 3)),
        ],
        compiler_params=pltpu.CompilerParams(
            collective_id=1 if paired else None, has_side_effects=paired, vmem_limit_bytes=56 << 20
        ),
    )(tokens, item[:, None], ids[:, None], ids.reshape(-1, SLOT), mod, bias, b_out, *weights)


def gelu_both(v):
    c = (2.0 / jnp.pi) ** 0.5
    square = v * v
    t = jnp.tanh(c * v * (1.0 + 0.044715 * square))
    half = 0.5 * (1.0 + t)
    slope = half + 0.5 * v * (1.0 - t * t) * (c * (1.0 + 3.0 * 0.044715 * square))
    return v * half, slope


def pieces_of(ff):
    if ff != 1152:
        return [(0, ff)]
    return [(0, 256), (256, 384), (640, 512)]


def stream_of(ff, lw):
    at, downs, ups = 0, [], []
    for _, size in pieces_of(ff):
        downs.append(at)
        ups.append(at + size)
        at += 2 * size
    return downs, ups, at, at + lw


def split_stream(rows, ff, lw):
    downs, ups, out_row, qkv_row = stream_of(ff, lw)
    sizes = [size for _, size in pieces_of(ff)]
    down, up = (
        jnp.concatenate([rows[at : at + size] for at, size in zip(starts, sizes)])
        for starts in (downs, ups)
    )
    return down, up, rows[out_row:qkv_row], rows[qkv_row : qkv_row + 3 * lw]


X_RUNS = ((2, 0, 4), (6, 4, 6), (12, 10, 8), (20, 18, 2), (23, 20, 7))
L_RUNS = ((4, 0, 4), (8, 4, 6), (16, 10, 8), (24, 18, 2), (27, 20, 7))
LAST_TICK = 34 + 8


def in_runs(tick, runs):
    chunk, inside = 0, False
    for start, first, size in runs:
        here = (tick >= start) & (tick < start + size)
        chunk = jnp.where(here, first + tick - start, chunk)
        inside = here | inside
    return chunk, inside


class Reduction:
    def __init__(self, d_in, s_own, s_far, x_in, out_ref, lp, tb, ry, ub, rz1, vb, rz2, ob, dsend, drecv, xsend, xrecv, loads, sends, recvs, outs):
        self.d_in, self.s_own, self.s_far, self.x_in, self.out_ref = d_in, s_own, s_far, x_in, out_ref
        self.lp, self.tb, self.ry, self.ub, self.rz1, self.vb, self.rz2, self.ob = lp, tb, ry, ub, rz1, vb, rz2, ob
        self.dsend, self.drecv, self.xsend, self.xrecv = dsend, drecv, xsend, xrecv
        self.loads, self.sends, self.recvs, self.outs = loads, sends, recvs, outs
        dp, mp = lax.axis_index("dp"), lax.axis_index("mp")
        core, self.yb = mp % 2, dp % 2
        xb, self.z0, self.z1 = mp // 2, (dp // 2) % 2, dp // 4
        self.sib = (dp, mp + 1 - 2 * core)
        self.xn = (dp, mp + 2 - 4 * xb)
        self.yn = (dp + 1 - 2 * self.yb, mp)
        self.z1n = (dp + 2 - 4 * self.z0, mp)
        self.z2n = (dp + 4 - 8 * self.z1, mp)

    def greet(self):
        barrier = pltpu.get_barrier_semaphore()
        for peer in (self.sib, self.xn, self.yn, self.z1n, self.z2n):
            pl.semaphore_signal(barrier, inc=1, device_id=peer, device_id_type=MESH)
        pl.semaphore_wait(barrier, 5)

    def to_sibling(self, which, flush, source, row, size):
        return pltpu.make_async_remote_copy(
            src_ref=source,
            dst_ref=self.d_in.at[which, pl.ds(row, size)],
            send_sem=self.dsend.at[which, flush],
            recv_sem=self.drecv.at[which, flush],
            device_id=self.sib,
            device_id_type=MESH,
        )

    def x_copy(self, c):
        return pltpu.make_async_remote_copy(
            src_ref=self.s_far.at[rows_at(c, CHUNK)],
            dst_ref=self.x_in.at[rows_at(c, CHUNK)],
            send_sem=self.xsend.at[c],
            recv_sem=self.xrecv.at[c],
            device_id=self.xn,
            device_id_type=MESH,
        )

    def tick(self, tick):
        yb, z0, z1 = self.yb, self.z0, self.z1
        half, quarter, eighth = CHUNK // 2, CHUNK // 4, CHUNK // 8
        at_y = pl.multiple_of(yb * half, half)
        at_z1 = pl.multiple_of(yb * half + z0 * quarter, quarter)
        at_z2 = pl.multiple_of(yb * half + z0 * quarter + z1 * eighth, eighth)
        lp, tb, ub, vb, ob = self.lp, self.tb, self.ub, self.vb, self.ob

        def remote(stage, slot, src, dst, peer):
            return pltpu.make_async_remote_copy(
                src_ref=src,
                dst_ref=dst,
                send_sem=self.sends.at[stage, slot],
                recv_sem=self.recvs.at[stage, slot],
                device_id=peer,
                device_id_type=MESH,
            )

        def load(which, c):
            source = (self.s_own, self.x_in)[which].at[rows_at(c, CHUNK)]
            return pltpu.make_async_copy(source, lp.at[c % 2, which], self.loads.at[which, c % 2])

        def y_copy(c):
            part = rows_at(1 - yb, half)
            return remote(0, c % 2, tb.at[c % 2, part], self.ry.at[c % 2], self.yn)

        def z1_copy(c):
            part = rows_at(1 - z0, quarter)
            return remote(1, c % 2, ub.at[c % 2, part], self.rz1.at[c % 2], self.z1n)

        def z2_copy(c):
            part = rows_at(1 - z1, eighth)
            return remote(2, c % 2, vb.at[c % 2, part], self.rz2.at[c % 2], self.z2n)

        def back(stage, c, at, size, peer):
            place = ob.at[c % OUT_SLOTS, pl.ds(at, size)]
            return remote(stage, c % 2, place, place, peer)

        def az2_copy(c):
            return back(3, c, at_z2, eighth, self.z2n)

        def az1_copy(c):
            return back(4, c, at_z1, quarter, self.z1n)

        def ay_copy(c):
            return back(5, c, at_y, half, self.yn)

        def out_copy(c):
            return pltpu.make_async_copy(
                ob.at[c % OUT_SLOTS], self.out_ref.at[rows_at(c, CHUNK)], self.outs.at[c % 2]
            )

        def stage(lag, work):
            c, inside = in_runs(tick - lag, L_RUNS)

            @pl.when(inside)
            def _():
                work(c)

        def leave(c):
            out_copy(c).wait()

        def store(c):
            ay_copy(c).wait()
            out_copy(c).start()

        def go_ay(c):
            az1_copy(c).wait()
            ay_copy(c).start()

        def go_az1(c):
            az2_copy(c).wait()
            az1_copy(c).start()

        def go_az2(c):
            z2_copy(c).wait()
            ob[c % OUT_SLOTS, pl.ds(at_z2, eighth)] = vb[c % 2, rows_at(z1, eighth)] + self.rz2[c % 2]
            az2_copy(c).start()

        def go_z2(c):
            z1_copy(c).wait()
            vb[c % 2] = ub[c % 2, rows_at(z0, quarter)] + self.rz1[c % 2]
            z2_copy(c).start()

        def go_z1(c):
            y_copy(c).wait()
            ub[c % 2] = tb[c % 2, rows_at(yb, half)] + self.ry[c % 2]
            z1_copy(c).start()

        def go_y(c):
            for which in range(2):
                load(which, c).wait()
            tb[c % 2] = lp[c % 2, 0] + lp[c % 2, 1]
            y_copy(c).start()

        def go_load(c):
            self.x_copy(c).wait()
            for which in range(2):
                load(which, c).start()

        stage(8, leave)
        stage(7, store)
        stage(6, go_ay)
        stage(5, go_az1)
        stage(4, go_az2)
        stage(3, go_z2)
        stage(2, go_z1)
        stage(1, go_y)
        stage(0, go_load)
        c, inside = in_runs(tick, X_RUNS)

        @pl.when(inside)
        def _():
            self.x_copy(c).start()


N_RED = 21


def back_kernel(n, heads, tile, paired, *refs):
    (
        tokens, upstream, branch_one, normed_hbm, item, ids, ids_row, mod, b_up, b_down, lse,
        w_all, own_attn, own_up, own_down, qkv_hbm, att_hbm,
        output_hbm, gtok_hbm, sums_ref, gb_down, gb_out, gb_up, gb_qv, *refs,
    ) = refs
    if paired:
        *shared, (
            n_buf, d_buf, acc_a, acc_b, up_buf, down_buf, w_buf, hid_buf, dpre_buf, stage_buf, qkv_buf, att_buf, datt_buf, dproj_buf,
            up_sem, down_sem, n_sem, stage_sem, w_sem, qkv_sem, att_sem,
        ) = (*refs[:5], refs[5:26])
        r_buf, r_sem, *more = refs[26:]
        red = Reduction(*shared, *more)
        red.greet()
        tick = red.tick
    else:
        (
            g_all, n_buf, d_buf, acc_a, acc_b, up_buf, down_buf, w_buf, hid_buf, dpre_buf, stage_buf, qkv_buf, att_buf, datt_buf, dproj_buf,
            up_sem, down_sem, n_sem, stage_sem, w_sem, qkv_sem, att_sem,
        ) = refs

        def tick(t):
            pass

    rows, width = tokens.shape
    lw = heads * HEAD
    frames = rows // SLOT
    scale = HEAD ** (-0.5)
    tiles = rows // tile
    own = (own_attn, own_up, own_down) if paired else None
    ff = w_all.shape[2]
    pieces = pieces_of(ff)
    downs, ups, out_row, qkv_row = stream_of(ff, lw)
    sums_ref[...] = jnp.zeros_like(sums_ref)
    gb_down[...] = jnp.zeros_like(gb_down)
    gb_out[...] = jnp.zeros_like(gb_out)
    gb_up[...] = jnp.zeros_like(gb_up)

    def landed(m, blocks):
        if not paired:
            return

        @pl.when(m % 2 == 0)
        def _():
            for slot, (flush, row, size) in enumerate(blocks):
                stage = stage_buf.at[slot, pl.ds(0, size)]
                sent = red.to_sibling(m // 2, flush, stage, row, size)
                sent.wait()
                fetch(m // 2, slot, row, size).start()

    def fetch(which, slot, row, size):
        return pltpu.make_async_copy(
            red.d_in.at[which, pl.ds(row, size)], r_buf.at[slot, pl.ds(0, size)], r_sem.at[slot]
        )

    def put(target, slot, row, size):
        return pltpu.make_async_copy(
            stage_buf.at[slot, pl.ds(0, size)], target.at[pl.ds(row, size)], stage_sem.at[slot]
        )

    def settle(blocks):
        if paired:
            for slot, (flush, row, size) in enumerate(blocks):
                put(red.s_own, slot, row, size).wait()

    def leave(m, slot, block, value):
        flush, row, size = block
        if not paired:
            stage_buf[slot, pl.ds(0, size), :] = value.astype(bf16)
            copy = put(g_all.at[m], slot, row, size)
            copy.start()
            copy.wait()
            return

        @pl.when(m % 2 == 1)
        def _():
            stage_buf[slot, pl.ds(0, size), :] = value.astype(bf16)
            stage = stage_buf.at[slot, pl.ds(0, size)]
            red.to_sibling(m // 2, flush, stage, row, size).start()

        @pl.when(m % 2 == 0)
        def _():
            fetch(m // 2, slot, row, size).wait()
            total = value + r_buf[slot, pl.ds(0, size), :].astype(f32)
            stage_buf[slot, pl.ds(0, size), :] = total.astype(bf16)

            @pl.when(m == 0)
            def _():
                put(red.s_own, slot, row, size).start()

            @pl.when(m > 0)
            def _():
                put(red.s_far, slot, row, size).start()

    def w_copies(p, m, slot):
        at, size = pieces[p]
        here = pl.ds(at, size)
        up_part, down_part = up_buf.at[slot, :, pl.ds(0, size)], down_buf.at[slot, pl.ds(0, size), :]
        return (
            Shard(own, w_all, 1, m, (slice(None), here), up_part, up_sem.at[slot]),
            Shard(own, w_all, 2, m, (here, slice(None)), down_part, down_sem.at[slot]),
        )

    for copy in w_copies(0, n - 1, 0):
        copy.start()

    def first(i, carry):
        at = rows_at(i, SLOT)
        col = item[at, :]
        middle = tokens[at, :].astype(f32) + pick(col, mod, 2) * branch_one[at, :]
        normed, _ = normal(middle)
        n_buf[at, :] = (normed * (1.0 + pick(col, mod, 4)) + pick(col, mod, 3)).astype(bf16)
        d = (pick(col, mod, 5) * upstream[at, :].astype(f32)).astype(bf16)
        d_buf[at, :] = d
        gb_down[...] += jnp.sum(d.astype(f32), axis=0, keepdims=True)
        acc_a[at, :] = jnp.broadcast_to(b_down[...], (SLOT, width))
        acc_b[at, :] = jnp.zeros((SLOT, width), f32)
        return carry

    lax.fori_loop(0, frames, first, 0)

    def blocks_of(p):
        size = pieces[p][1]
        return ((2 * p, downs[p], size), (2 * p + 1, ups[p], size))

    now = 0
    for p, (p_at, p_size) in enumerate(pieces):
        beats = 2 if p_size > 384 else 1

        def shard(i, carry, p=p, p_at=p_at, p_size=p_size, beats=beats, now=now):
            m = n - 1 - i
            slot = (p * n + i) % 2
            for copy in w_copies(p, m, slot):
                copy.wait()

            @pl.when(i + 1 < n)
            def _():
                for copy in w_copies(p, m - 1, 1 - slot):
                    copy.start()

            if p + 1 < len(pieces):

                @pl.when(i + 1 == n)
                def _():
                    for copy in w_copies(p + 1, n - 1, 1 - slot):
                        copy.start()

            blocks = blocks_of(p)
            bias = b_up[m, :, pl.ds(p_at, p_size)]
            up = up_buf.at[slot, :, pl.ds(0, p_size)]
            down = down_buf.at[slot, pl.ds(0, p_size), :]

            def part(j, c):
                at = rows_at(j, tile)
                pre = jnp.dot(n_buf[at, :], up[...], preferred_element_type=f32) + bias
                hidden, slope = gelu_both(pre)
                hidden = hidden.astype(bf16)
                dpre = nt(d_buf[at, :], down[...]) * slope
                dpre = dpre.astype(bf16)
                hid_buf[at, pl.ds(0, p_size)] = hidden
                dpre_buf[at, pl.ds(0, p_size)] = dpre
                gb_up[m, :, pl.ds(p_at, p_size)] += jnp.sum(
                    dpre.astype(f32), axis=0, keepdims=True
                )
                acc_a[at, :] += jnp.dot(hidden, down[...], preferred_element_type=f32)
                acc_b[at, :] += nt(dpre, up[...])
                return c

            lax.fori_loop(0, tiles, part, 0)

            @pl.when(i == 2)
            def _():
                settle(blocks)

            if p:

                @pl.when(i == 0)
                def _():
                    settle(blocks_of(p - 1))

            tick(now + beats * i)
            landed(m, blocks)
            leave(m, 0, blocks[0], tn(hid_buf[:, pl.ds(0, p_size)], d_buf[...]))
            leave(m, 1, blocks[1], tn(dpre_buf[:, pl.ds(0, p_size)], n_buf[...]))
            if beats > 1:
                tick(now + beats * i + 1)
            return carry

        lax.fori_loop(0, n, shard, 0)
        now += n * beats
    settle(blocks_of(len(pieces) - 1))

    def a_copies(m, slot):
        return (
            Shard(own, w_all, 0, m, slice(None), w_buf.at[slot], w_sem.at[slot]),
            pltpu.make_async_copy(qkv_hbm.at[m], qkv_buf.at[slot], qkv_sem.at[slot]),
        )

    def att_copy(m, slot):
        return pltpu.make_async_copy(att_hbm.at[m], att_buf.at[slot], att_sem.at[slot])

    normed_copy = pltpu.make_async_copy(normed_hbm, n_buf, n_sem)
    normed_copy.start()
    for copy in a_copies(n - 1, 0):
        copy.start()
    att_copy(n - 1, 0).start()

    def row_copy(target, i):
        return pltpu.make_async_copy(
            stage_buf.at[i % 2, pl.ds(0, SLOT)], target.at[rows_at(i, SLOT)], stage_sem.at[i % 2]
        )

    def row_out(target, i, value):
        @pl.when(i >= 2)
        def _():
            row_copy(target, i - 2).wait()

        stage_buf[i % 2, pl.ds(0, SLOT), :] = value.astype(bf16)
        row_copy(target, i).start()

    def rows_done(target):
        for i in range(max(frames - 2, 0), frames):
            row_copy(target, i).wait()

    def middle_part(i, carry):
        at = rows_at(i, SLOT)
        col = item[at, :]
        gate = pick(col, mod, 2)
        branch = branch_one[at, :]
        middle = tokens[at, :].astype(f32) + gate * branch
        dy = upstream[at, :].astype(f32)
        second = acc_a[at, :]
        row_out(output_hbm, i, middle + pick(col, mod, 5) * second)
        add_by_item(sums_ref, 5, col, dy * second)
        grad = acc_b[at, :]
        normed, rstd = normal(middle)
        add_by_item(sums_ref, 3, col, grad)
        add_by_item(sums_ref, 4, col, grad * normed)
        dmiddle = dy + normal_back(grad, pick(col, mod, 4), normed, rstd)
        acc_a[at, :] = dmiddle
        add_by_item(sums_ref, 2, col, dmiddle * branch)
        d = (gate * dmiddle).astype(bf16)
        d_buf[at, :] = d
        gb_out[...] += jnp.sum(d.astype(f32), axis=0, keepdims=True)
        acc_b[at, :] = jnp.zeros((SLOT, width), f32)

        @pl.when(i % 2 == 1)
        def _():
            tick(now + i // 2)

        return carry

    lax.fori_loop(0, frames, middle_part, 0)
    rows_done(output_hbm)
    now += 2
    normed_copy.wait()
    out_block = (2 * len(pieces), out_row, lw)

    def out_part(i, carry):
        m = n - 1 - i
        slot = i % 2
        att_copy(m, slot).wait()

        @pl.when(i + 1 < n)
        def _():
            att_copy(m - 1, 1 - slot).start()

        @pl.when(i == 2)
        def _():
            settle((out_block,))

        landed(m, (out_block,))
        leave(m, 0, out_block, jnp.dot(att_buf[slot], d_buf[...], preferred_element_type=f32))
        return carry

    lax.fori_loop(0, n, out_part, 0)
    settle((out_block,))
    tick(now)
    now += 1
    some = 3 * lw // 2
    qkv_blocks = tuple((2 * len(pieces) + 1 + j, qkv_row + j * some, some) for j in range(2))

    def attn(i, carry):
        m = n - 1 - i
        slot = i % 2
        for copy in a_copies(m, slot):
            copy.wait()

        @pl.when(i + 1 < n)
        def _():
            for copy in a_copies(m - 1, 1 - slot):
                copy.start()

        datt = nt(w_buf[slot, pl.ds(3 * lw, lw), :], d_buf[...])
        for h in range(heads):
            datt_buf[h] = datt[h * HEAD : (h + 1) * HEAD].astype(bf16)

        def frame(f, c):
            at = rows_at(f, SLOT)
            pairs = pair_bias(ids[at, :], ids_row[pl.ds(f, 1), :])
            dqs, dks, dvs = [], [], []
            for h in range(heads):
                q = qkv_buf[slot, h, :, at]
                k = qkv_buf[slot, heads + h, :, at]
                v = qkv_buf[slot, 2 * heads + h, :, at]
                d = datt_buf[h, :, at]
                scores = tn(k, q) * scale + pairs
                probs = jnp.exp(scores - lse[m, h : h + 1, at])
                dprobs = tn(v, d)
                inner = jnp.sum(dprobs * probs, axis=0, keepdims=True)
                dscores = (probs * (dprobs - inner)).astype(bf16)
                dvs.append(nt(d, probs.astype(bf16)))
                dqs.append(jnp.dot(k, dscores, preferred_element_type=f32) * scale)
                dks.append(nt(q, dscores) * scale)
            dproj_buf[:, at] = jnp.concatenate(dqs + dks + dvs, axis=0).astype(bf16)
            return c

        lax.fori_loop(0, frames, frame, 0)

        @pl.when(i == 2)
        def _():
            settle(qkv_blocks)

        tick(now + 2 * i)
        landed(m, qkv_blocks)
        gb_qv[m] = jnp.sum(dproj_buf[...].astype(f32), axis=1, keepdims=True)
        for j, block in enumerate(qkv_blocks):
            part = dproj_buf[pl.ds(j * some, some), :]
            leave(m, j, block, jnp.dot(part, n_buf[...], preferred_element_type=f32))

        def part(j, c):
            at = rows_at(j, tile)
            acc_b[at, :] += tn(dproj_buf[:, at], w_buf[slot, pl.ds(0, 3 * lw), :])
            return c

        lax.fori_loop(0, tiles, part, 0)
        tick(now + 2 * i + 1)
        return carry

    lax.fori_loop(0, n, attn, 0)
    settle(qkv_blocks)
    now += 2 * n

    def last(i, carry):
        at = rows_at(i, SLOT)
        col = item[at, :]
        normed, rstd = normal(tokens[at, :].astype(f32))
        grad = acc_b[at, :]
        add_by_item(sums_ref, 0, col, grad)
        add_by_item(sums_ref, 1, col, grad * normed)
        row_out(gtok_hbm, i, acc_a[at, :] + normal_back(grad, pick(col, mod, 1), normed, rstd))

        @pl.when(i == 1)
        def _():
            tick(now)

        return carry

    lax.fori_loop(0, frames, last, 0)
    rows_done(gtok_hbm)
    if paired:

        def drain(t, carry):
            tick(t)
            return carry

        lax.fori_loop(now + 1, LAST_TICK + 1, drain, 0)


def backward(tokens, upstream, branch_one, normed_one, item, ids, mod, b_up, b_down, lse, w_all, own, qkv, att):
    rows, width = tokens.shape
    n, ff = b_up.shape[0], b_up.shape[2]
    heads = qkv.shape[1] // 3
    lw = heads * HEAD
    paired = bool(own)
    own = own or [w_all] * 3
    pieces = pieces_of(ff)
    widest = max(size for _, size in pieces)
    tile = min(512, rows)
    total = 2 * ff + 4 * lw
    deep = max(widest, 3 * lw // 2, SLOT)
    slots = 2
    flushes = 2 * len(pieces) + 3
    half, quarter, eighth = CHUNK // 2, CHUNK // 4, CHUNK // 8
    vmem = pl.BlockSpec(memory_space=pltpu.VMEM)
    hbm = pl.BlockSpec(memory_space=pl.ANY)
    dma = pltpu.SemaphoreType.DMA

    def buf(*shape):
        return pltpu.VMEM(shape, bf16)

    grads = [jax.ShapeDtypeStruct((n, total, width), bf16)]
    extra = []
    if paired:
        grads = [jax.ShapeDtypeStruct((2, total, width), bf16)]
        grads += [jax.ShapeDtypeStruct((total, width), bf16)] * 4
        extra = [
            buf(slots, deep, width),
            dma((slots,)),
            buf(2, 2, CHUNK, width),
            buf(2, CHUNK, width),
            buf(2, half, width),
            buf(2, half, width),
            buf(2, quarter, width),
            buf(2, quarter, width),
            buf(2, eighth, width),
            buf(OUT_SLOTS, CHUNK, width),
            dma((2, flushes)),
            dma((2, flushes)),
            dma((total // CHUNK,)),
            dma((total // CHUNK,)),
            dma((2, 2)),
            dma((6, 2)),
            dma((6, 2)),
            dma((2,)),
        ]
    return pl.pallas_call(
        functools.partial(back_kernel, n, heads, tile, paired),
        out_shape=(
            jax.ShapeDtypeStruct((rows, width), bf16),
            jax.ShapeDtypeStruct((rows, width), bf16),
            jax.ShapeDtypeStruct(mod.shape, f32),
            jax.ShapeDtypeStruct((1, width), f32),
            jax.ShapeDtypeStruct((1, width), f32),
            jax.ShapeDtypeStruct((n, 1, ff), f32),
            jax.ShapeDtypeStruct((n, 3 * lw, 1), f32),
            *grads,
        ),
        in_specs=[vmem] * 3 + [hbm] + [vmem] * 7 + [hbm] * 6,
        out_specs=(hbm,) * 2 + (vmem,) * 5 + (hbm,) * len(grads),
        scratch_shapes=[
            buf(rows, width),
            buf(rows, width),
            pltpu.VMEM((rows, width), f32),
            pltpu.VMEM((rows, width), f32),
            buf(2, width, widest),
            buf(2, widest, width),
            buf(2, 4 * lw, width),
            buf(rows, widest),
            buf(rows, widest),
            buf(slots, deep, width),
            buf(2, 3 * heads, HEAD, rows),
            buf(2, lw, rows),
            buf(heads, HEAD, rows),
            buf(3 * lw, rows),
            dma((2,)),
            dma((2,)),
            dma,
            dma((slots,)),
            dma((2,)),
            dma((2,)),
            dma((2,)),
            *extra,
        ],
        compiler_params=pltpu.CompilerParams(
            collective_id=2 if paired else None, has_side_effects=paired, vmem_limit_bytes=63 << 20
        ),
    )(
        tokens, upstream, branch_one, normed_one, item[:, None], ids[:, None], ids.reshape(-1, SLOT),
        mod, b_up, b_down, lse, w_all, *own, qkv, att,
    )


def reduce_kernel(count, g_ref, tail_ref, out_ref, lp, rd, s0, sx, rx, tb, ry, ub, rz1, vb, rz2, ob, loads, sends, recvs, outs):
    dp, mp = lax.axis_index("dp"), lax.axis_index("mp")
    core, yb = mp % 2, dp % 2
    xb, z0, z1 = mp // 2, (dp // 2) % 2, dp // 4
    sib = (dp, mp + 1 - 2 * core)
    xn = (dp, mp + 2 - 4 * xb)
    yn = (dp + 1 - 2 * yb, mp)
    z1n = (dp + 2 - 4 * z0, mp)
    z2n = (dp + 4 - 8 * z1, mp)
    half, quarter, eighth = CHUNK // 2, CHUNK // 4, CHUNK // 8

    barrier = pltpu.get_barrier_semaphore()
    for peer in (sib, xn, yn, z1n, z2n):
        pl.semaphore_signal(barrier, inc=1, device_id=peer, device_id_type=MESH)
    pl.semaphore_wait(barrier, 5)

    def rows_of(c):
        return pl.ds(pl.multiple_of(c * CHUNK, CHUNK), CHUNK)

    def remote(stage, src, dst, peer, slot):
        return pltpu.make_async_remote_copy(
            src_ref=src,
            dst_ref=dst,
            send_sem=sends.at[stage, slot],
            recv_sem=recvs.at[stage, slot],
            device_id=peer,
            device_id_type=MESH,
        )

    main = g_ref.shape[1] // CHUNK

    def load(which, c, slot, ref):
        part = ref.at[2 * which, rows_of(c)]
        return pltpu.make_async_copy(part, lp.at[slot, which], loads.at[which, slot])

    def d_copy(which, c, slot, ref):
        return remote(which, ref.at[2 * which + 1, rows_of(c)], rd.at[slot, which], sib, slot)

    def x_copy(c, slot):
        return remote(2, sx.at[slot], rx.at[slot], xn, slot)

    def y_copy(c, slot):
        part = pl.ds(pl.multiple_of((1 - yb) * half, half), half)
        return remote(3, tb.at[slot, part], ry.at[slot], yn, slot)

    def z1_copy(c, slot):
        part = pl.ds(pl.multiple_of((1 - z0) * quarter, quarter), quarter)
        return remote(4, ub.at[slot, part], rz1.at[slot], z1n, slot)

    def z2_copy(c, slot):
        part = pl.ds(pl.multiple_of((1 - z1) * eighth, eighth), eighth)
        return remote(5, vb.at[slot, part], rz2.at[slot], z2n, slot)

    at_y = pl.multiple_of(yb * half, half)
    at_z1 = pl.multiple_of(yb * half + z0 * quarter, quarter)
    at_z2 = pl.multiple_of(yb * half + z0 * quarter + z1 * eighth, eighth)

    def back(stage, at, size, peer, c, slot):
        place = ob.at[c % OUT_SLOTS, pl.ds(at, size)]
        return remote(stage, place, place, peer, slot)

    def az2_copy(c, slot):
        return back(6, at_z2, eighth, z2n, c, slot)

    def az1_copy(c, slot):
        return back(7, at_z1, quarter, z1n, c, slot)

    def ay_copy(c, slot):
        return back(8, at_y, half, yn, c, slot)

    def out_copy(c, slot):
        return pltpu.make_async_copy(ob.at[c % OUT_SLOTS], out_ref.at[rows_of(c)], outs.at[slot])

    def step(i, carry):
        def stage(lag, work):
            c = i - lag

            @pl.when((c >= 0) & (c < count))
            def _():
                work(c, c % 2)

        def leave(c, slot):
            out_copy(c, slot).wait()

        def store(c, slot):
            ay_copy(c, slot).wait()
            out_copy(c, slot).start()

        def go_ay(c, slot):
            az1_copy(c, slot).wait()
            ay_copy(c, slot).start()

        def go_az1(c, slot):
            az2_copy(c, slot).wait()
            az1_copy(c, slot).start()

        def go_az2(c, slot):
            z2_copy(c, slot).wait()
            mine = vb[slot, pl.ds(pl.multiple_of(z1 * eighth, eighth), eighth)] + rz2[slot]
            ob[c % OUT_SLOTS, pl.ds(at_z2, eighth)] = mine
            az2_copy(c, slot).start()

        def go_z2(c, slot):
            z1_copy(c, slot).wait()
            vb[slot] = ub[slot, pl.ds(pl.multiple_of(z0 * quarter, quarter), quarter)] + rz1[slot]
            z2_copy(c, slot).start()

        def go_z1(c, slot):
            y_copy(c, slot).wait()
            ub[slot] = tb[slot, pl.ds(pl.multiple_of(yb * half, half), half)] + ry[slot]
            z1_copy(c, slot).start()

        def go_y(c, slot):
            x_copy(c, slot).wait()
            tb[slot] = s0[slot] + rx[slot]
            y_copy(c, slot).start()

        def go_x(c, slot):
            for which in range(2):
                load(which, 0, slot, g_ref).wait()
                d_copy(which, 0, slot, g_ref).wait()
            sx[slot] = lp[slot, 1] + rd[slot, 1]
            s0[slot] = lp[slot, 0] + rd[slot, 0]
            x_copy(c, slot).start()

        def go_d(c, slot):
            @pl.when(c < main)
            def _():
                for which in range(2):
                    load(which, c, slot, g_ref).start()
                    d_copy(which, c, slot, g_ref).start()

            @pl.when(c >= main)
            def _():
                for which in range(2):
                    load(which, c - main, slot, tail_ref).start()
                    d_copy(which, c - main, slot, tail_ref).start()

        stage(9, leave)
        stage(8, store)
        stage(7, go_ay)
        stage(6, go_az1)
        stage(5, go_az2)
        stage(4, go_z2)
        stage(3, go_z1)
        stage(2, go_y)
        stage(1, go_x)
        stage(0, go_d)
        return carry

    lax.fori_loop(0, count + 10, step, 0)


def reduce_grads(parts, tail):
    rows, width = parts.shape[1], parts.shape[2]
    count = rows // CHUNK
    half, quarter, eighth = CHUNK // 2, CHUNK // 4, CHUNK // 8

    def buf(*lead):
        return pltpu.VMEM((*lead, width), bf16)

    return pl.pallas_call(
        functools.partial(reduce_kernel, count),
        out_shape=jax.ShapeDtypeStruct((rows, width), bf16),
        in_specs=[pl.BlockSpec(memory_space=pl.ANY)] * 2,
        out_specs=pl.BlockSpec(memory_space=pl.ANY),
        scratch_shapes=[
            buf(2, 2, CHUNK),
            buf(2, 2, CHUNK),
            buf(2, CHUNK),
            buf(2, CHUNK),
            buf(2, CHUNK),
            buf(2, CHUNK),
            buf(2, half),
            buf(2, half),
            buf(2, quarter),
            buf(2, quarter),
            buf(2, eighth),
            buf(OUT_SLOTS, CHUNK),
            pltpu.SemaphoreType.DMA((2, 2)),
            pltpu.SemaphoreType.DMA((9, 2)),
            pltpu.SemaphoreType.DMA((9, 2)),
            pltpu.SemaphoreType.DMA((2,)),
        ],
        compiler_params=pltpu.CompilerParams(
            collective_id=0, has_side_effects=True, vmem_limit_bytes=32 << 20
        ),
    )(parts, tail)


def swap(values, axis, bit):
    n = lax.axis_size(axis)
    return lax.ppermute(values, axis, [(i, i ^ bit) for i in range(n)])


def shards(
    paired,
    tokens,
    condition,
    grid_rows,
    grid_cols,
    frame_start,
    frame_item,
    group_frames,
    w_qkv,
    qv_bias,
    w_out,
    b_out,
    w_up,
    b_up,
    w_down,
    b_down,
    w_ada,
    b_ada,
    cotangent,
):
    own_rows, width = tokens.shape
    local_width = w_qkv.shape[2]
    local_ff = w_up.shape[1]
    items = condition.shape[0]
    n_mp, n_dp = lax.axis_size("mp"), lax.axis_size("dp")
    mp, dp = lax.axis_index("mp"), lax.axis_index("dp")
    n = width // (4 * HEAD)
    lw, ff = width // n, local_ff * n_mp // n
    frame_id, item_id = frame_tables(
        grid_rows, grid_cols, frame_start, frame_item, group_frames[0], mp * own_rows, own_rows
    )
    cond_value = condition.astype(f32)
    act_low = jax.nn.silu(cond_value).astype(bf16)
    ada_flat = w_ada.reshape(width, -1)
    ada_local = dot(act_low, ada_flat) + b_ada.reshape(-1).astype(f32)
    ada_local = ada_local.reshape(items, 6, local_width)
    qkv_local = w_qkv.transpose(1, 2, 0)
    if paired:
        qkv_bias = jnp.concatenate(
            [qv_bias[0].astype(f32), jnp.zeros((lw,), f32), qv_bias[1].astype(f32)]
        )
        small = jnp.concatenate([ada_local.reshape(-1), qkv_bias, b_up.astype(f32)])
        small = jnp.stack([small] + [swap(small, "mp", bit) for bit in range(1, n)])
        n_ada = ada_local.size
        modulation = small[mp ^ jnp.arange(n), :n_ada].reshape(n, items, 6, lw)
        qkv_bias = small[:, n_ada : n_ada + 3 * lw]
        up_bias = small[:, n_ada + 3 * lw :]
        weights = [
            jnp.concatenate([qkv_local.reshape(3 * lw, width), w_out], axis=0),
            w_up,
            w_down,
        ]
    else:
        modulation = lax.all_gather(ada_local, "mp", axis=0)
        qv = lax.all_gather(qv_bias.astype(f32), "mp", axis=1, tiled=True)
        qkv_bias = jnp.stack([qv[0], jnp.zeros((width,), f32), qv[1]])
        qkv_bias = qkv_bias.reshape(3, n, lw).transpose(1, 0, 2).reshape(n, 3 * lw)
        up_bias = lax.all_gather(b_up.astype(f32), "mp", axis=0, tiled=True).reshape(n, ff)
        qkv = lax.all_gather(qkv_local, "mp", axis=1, tiled=True)
        qkv = qkv.reshape(3, n, lw, width).transpose(1, 0, 2, 3).reshape(n, 3 * lw, width)
        out = lax.all_gather(w_out, "mp", axis=0, tiled=True).reshape(n, lw, width)
        up = lax.all_gather(w_up, "mp", axis=1, tiled=True)
        up = up.reshape(width, n, ff).transpose(1, 0, 2)
        down = lax.all_gather(w_down, "mp", axis=0, tiled=True).reshape(n, ff, width)
        weights = [jnp.stack([jnp.concatenate([qkv, out], axis=1), up, down])]
    modulation = modulation.transpose(1, 2, 0, 3).reshape(items, 6, width)
    b_out_row, b_down_row = (b.astype(f32)[None] for b in (b_out, b_down))
    normed_one, branch_one, qkv, lse, att, *gathered = attend(
        tokens, item_id, frame_id, modulation, qkv_bias[:, :, None], b_out_row, weights, paired
    )
    w_all = gathered[0] if paired else weights[0]
    output, grad_tokens, item_grad, gb_down, gb_out, gb_up, gb_qv, *grads = backward(
        tokens,
        cotangent,
        branch_one,
        normed_one,
        item_id,
        frame_id,
        modulation,
        up_bias[:, None],
        b_down_row,
        lse,
        w_all,
        weights if paired else [],
        qkv,
        att,
    )
    gb_qv = gb_qv.reshape(n, 3, lw)[:, ::2]

    if paired:
        item_grad = item_grad.reshape(items, 6, n, lw).transpose(2, 0, 1, 3)[mp ^ jnp.arange(n)]
        total_items = items * n_dp
        dmod_all = jnp.zeros((n, total_items, 6, lw), f32)
        dmod_all = lax.dynamic_update_slice(dmod_all, item_grad, (0, dp * items, 0, 0))
        act_all = jnp.zeros((total_items, width), f32)
        act_all = lax.dynamic_update_slice(act_all, act_low.astype(f32), (dp * items, 0))
        act_all = jnp.where(mp == 0, act_all, 0.0)
        fixed = jnp.concatenate([act_all, gb_out, gb_down])
        n_dmod = total_items * 6 * lw // width
        tail = jnp.concatenate(
            [
                dmod_all.reshape(n, n_dmod, width),
                jnp.broadcast_to(fixed[None], (n, *fixed.shape)),
                gb_up,
                jnp.pad(gb_qv.reshape(n, 1, 2 * lw), ((0, 0), (0, 0), (0, width - 2 * lw))),
            ],
            axis=1,
        )
        tail = jnp.pad(tail, ((0, 0), (0, -tail.shape[1] % CHUNK), (0, 0))).astype(bf16)
        tail = reduce_grads(tail, tail).astype(f32)
        g_down, g_up, g_out, g_qkv = split_stream(grads[4], ff, lw)
        g_down, g_out = g_down.astype(f32), g_out.astype(f32)
        g_up, g_qkv = g_up.astype(f32).T, g_qkv.astype(f32).T.reshape(width, 3, lw)
        dmod = tail[:n_dmod].reshape(total_items, 6, lw)
        at = n_dmod
        act_all = tail[at : at + total_items]
        at = at + total_items
        gb_out, gb_down, gb_up = tail[at], tail[at + 1], tail[at + 2]
        gb_qv = tail[at + 3, : 2 * lw].reshape(2, lw)
        own_dmod = lax.dynamic_slice_in_dim(dmod, dp * items, items)
    else:

        def over_all(values, axis):
            part = lax.psum_scatter(values, "mp", scatter_dimension=axis, tiled=True)
            return lax.psum(part.astype(bf16), "dp").astype(f32)

        own_dmod = lax.psum_scatter(item_grad, "mp", scatter_dimension=2, tiled=True)
        dmod = lax.all_gather(own_dmod, "dp", axis=0, tiled=True)
        act_all = lax.all_gather(act_low, "dp", axis=0, tiled=True).astype(f32)
        g_down, g_up, g_out, g_qkv = jax.vmap(lambda g: split_stream(g, ff, lw))(grads[0])
        g_down = over_all(g_down.reshape(n * ff, width), 0)
        g_up = over_all(g_up.reshape(n * ff, width).T, 1)
        g_qkv = g_qkv.reshape(n, 3, lw, width).transpose(3, 1, 0, 2).reshape(width, 3, width)
        g_qkv = over_all(g_qkv, 2)
        g_out = over_all(g_out.reshape(width, width), 0)
        gb_up = over_all(gb_up.reshape(-1), 0)
        gb_qv = over_all(gb_qv.transpose(1, 0, 2).reshape(2, width), 1)
        gb_out = lax.psum(gb_out[0], ("dp", "mp"))
        gb_down = lax.psum(gb_down[0], ("dp", "mp"))
    grad_w_ada = lax.dot_general(
        act_all,
        dmod.reshape(dmod.shape[0], -1),
        (((0,), (0,)), ((), ())),
        precision=lax.Precision.HIGHEST,
    ).reshape(width, 6, local_width)
    grad_b_ada = jnp.sum(dmod, axis=0)
    cond_term = lax.dot_general(
        own_dmod.reshape(items, -1),
        ada_flat.astype(f32),
        (((1,), (1,)), ((), ())),
        precision=lax.Precision.HIGHEST,
    )
    if paired:
        cond_term = cond_term + swap(cond_term, "mp", 1)
        cond_term = cond_term + swap(cond_term, "mp", 2)
    else:
        cond_term = lax.psum(cond_term, "mp")
    grad_condition = jax.vjp(jax.nn.silu, cond_value)[1](cond_term)[0]
    return (
        output,
        grad_tokens,
        grad_condition,
        g_qkv,
        gb_qv,
        g_out,
        gb_out,
        g_up,
        gb_up,
        g_down,
        gb_down,
        grad_w_ada,
        grad_b_ada,
    )


def solution(mesh):
    paired = dict(mesh.shape) == {"dp": 8, "mp": 4}
    return jax.shard_map(
        functools.partial(shards, paired),
        mesh=mesh,
        in_specs=(
            P(("dp", "mp"), None),
            P("dp", None),
            P("dp"),
            P("dp"),
            P("dp"),
            P("dp"),
            P("dp"),
            P(None, None, "mp"),
            P(None, "mp"),
            P("mp", None),
            P(),
            P(None, "mp"),
            P("mp"),
            P("mp", None),
            P(),
            P(None, None, "mp"),
            P(None, "mp"),
            P(("dp", "mp"), None),
        ),
        out_specs=(
            P(("dp", "mp"), None),
            P(("dp", "mp"), None),
            P("dp", None),
            P(None, None, "mp"),
            P(None, "mp"),
            P("mp", None),
            P(),
            P(None, "mp"),
            P("mp"),
            P("mp", None),
            P(),
            P(None, None, "mp"),
            P(None, "mp"),
        ),
        check_vma=False,
    )
```

```python
import functools

import jax
import jax.numpy as jnp
from jax import lax
from jax.experimental import pallas as pl
from jax.experimental.pallas import tpu as pltpu
from jax.sharding import PartitionSpec as P

HEAD = 72
SLOT = 256
CHUNK = 128
BLOCK = 128
UNROLL = 1
OUT_SLOTS = 10
MESH = pl.DeviceIdType.MESH
epsilon = 1e-06
f32 = jnp.float32
bf16 = jnp.bfloat16


def frame_tables(grid_rows, grid_cols, frame_start, frame_item, used, first, length):
    rows = first + jnp.arange(length, dtype=jnp.int32)[:, None]
    slots = jnp.arange(grid_rows.shape[0], dtype=jnp.int32)[None, :]
    ends = (frame_start + grid_rows * grid_cols)[None, :]
    inside = (rows >= frame_start[None, :]) & (rows < ends) & (slots < used)
    frame_id = jnp.sum(jnp.where(inside, slots + 1, 0), axis=1) - 1
    item_id = jnp.sum(jnp.where(inside, frame_item[None, :], 0), axis=1)
    return (frame_id, item_id)


def normal(values):
    centred = values - jnp.mean(values, axis=-1, keepdims=True)
    rstd = lax.rsqrt(jnp.mean(centred * centred, axis=-1, keepdims=True) + epsilon)
    return centred * rstd, rstd


def normal_back(grad, scale, normed, rstd):
    u = grad * (1.0 + scale)
    return rstd * (
        u
        - jnp.mean(u, axis=-1, keepdims=True)
        - normed * jnp.mean(u * normed, axis=-1, keepdims=True)
    )


def dot(left, right):
    return jnp.dot(left, right, preferred_element_type=f32)


def rows_at(i, size):
    return pl.ds(pl.multiple_of(i * size, size), size)


def pick(item_col, mod_ref, k):
    total = mod_ref[0, k : k + 1, :]
    for item in range(1, mod_ref.shape[0]):
        total = jnp.where(item_col == item, mod_ref[item, k : k + 1, :], total)
    return total


def fold(values):
    return jnp.sum(values.reshape(-1, 8, values.shape[-1]), axis=0)


def add_by_item(sums_ref, k, item_col, values):
    for item in range(sums_ref.shape[0]):
        sums_ref[item, k] += fold(jnp.where(item_col == item, values, 0.0))


def tn(left, right):
    return lax.dot_general(left, right, (((0,), (0,)), ((), ())), preferred_element_type=f32)


def nt(left, right):
    return lax.dot_general(left, right, (((1,), (1,)), ((), ())), preferred_element_type=f32)


class Shard:
    def __init__(self, own, others, a, m, part, target, sem):
        self.own, self.others, self.a, self.m, self.part = own, others, a, m, part
        self.target, self.sem = target, sem

    def copy(self, source):
        return pltpu.make_async_copy(source.at[self.part], self.target, self.sem)

    def start(self):
        if self.own is None:
            self.copy(self.others.at[self.a, self.m]).start()
            return

        @pl.when(self.m == 0)
        def _():
            self.copy(self.own[self.a]).start()

        @pl.when(self.m > 0)
        def _():
            self.copy(self.others.at[self.a, self.m - 1]).start()

    def wait(self):
        source = self.others.at[self.a, 0] if self.own is None else self.own[self.a]
        self.copy(source).wait()


def pair_bias(id_col, id_row):
    shape = (SLOT, SLOT)
    one = lax.broadcasted_iota(jnp.int32, shape, 0) == lax.broadcasted_iota(jnp.int32, shape, 1)
    same = (id_col == id_row) & (id_col >= 0)
    return jnp.where(same | one, 0.0, -1e30)


EXTRA = 3


class Units:
    def __init__(self, a, parts, ticks, place):
        self.a, self.parts, self.place, self.count = a, parts, place, len(ticks)
        self.runs = [[(unit[k], c, 1) for c, unit in enumerate(ticks)] for k in range(4)]


def units_of(depth, pieces):
    attn = depth // 4
    (_, wide), (last_at, last) = pieces[0], pieces[-1]

    def rows(first, part):
        return lambda c, at, size: (pl.ds(pl.multiple_of(first(c) + at * part, part), size * part), slice(None))

    def columns(first, width):
        return lambda c, at, size: (
            pl.ds(pl.multiple_of(at * (depth // 9), depth // 9), size * (depth // 9)),
            pl.ds(pl.multiple_of(first(c), 128), width),
        )

    return (
        Units(0, 9, ((4, 6, 8, 10), (7, 9, 10, 12), (8, 10, 11, 13), (11, 12, 13, 14)), rows(lambda c: c * attn, attn // 9)),
        Units(1, 9, ((15, 17, 19, 21), (17, 19, 21, 23), (21, 23, 25, 27)), columns(lambda c: c * wide, wide)),
        Units(2, 8, ((16, 18, 20, 22), (18, 20, 22, 24), (23, 25, 27, 29)), rows(lambda c: c * wide, wide // 8)),
        Units(1, 9, ((26, 27, 28, 29),), columns(lambda c: last_at, last)),
        Units(2, 8, ((27, 28, 29, 30),), rows(lambda c: last_at, last // 8)),
    )


class Gather:
    def __init__(self, units, own, w_all, sends, recvs, near_send, near_recv):
        self.units, self.own, self.w_all = units, own, w_all
        self.sends, self.recvs, self.near_send, self.near_recv = sends, recvs, near_send, near_recv
        dp, mp = lax.axis_index("dp"), lax.axis_index("mp")
        core, yb = mp % 2, dp % 2
        xb, z0 = mp // 2, (dp // 2) % 2
        self.sib = (dp, mp + 1 - 2 * core)
        self.xn = (dp, mp + 2 - 4 * xb)
        self.yn = (dp + 1 - 2 * yb, mp)
        self.zn = (dp + 2 - 4 * z0, mp)
        self.by_z, self.by_y = z0 * 2 + yb, 4 + yb * 2 + z0
        self.pair_z, self.pair_y = z0 * 2, 4 + yb * 2

    def near(self, a):
        return pltpu.make_async_remote_copy(
            src_ref=self.own[a],
            dst_ref=self.w_all.at[a, 0],
            send_sem=self.near_send.at[a],
            recv_sem=self.near_recv.at[a],
            device_id=self.sib,
            device_id_type=MESH,
        )

    def begin(self):
        self.near(0).start()
        for g, c in ((0, 0), (0, 1), (0, 2), (0, 3), (1, 0), (2, 0), (1, 1), (2, 1), (1, 2), (2, 2), (3, 0), (4, 0)):
            for copy in self.steps(g)[0](c):
                copy.start()
        self.near(1).start()
        self.near(2).start()

    def tick(self, tick):
        for g, units in enumerate(self.units):
            steps = self.steps(g)
            for k in (4, 3, 2, 1):
                c, inside = in_runs(tick, units.runs[k - 1])

                @pl.when(inside)
                def _(c=c, k=k, steps=steps):
                    for copy in steps[k - 1](c):
                        copy.wait()
                    if k < 4:
                        for copy in steps[k](c):
                            copy.start()

    def steps(self, g):
        units = self.units[g]
        own, far, both = self.own[units.a], self.w_all.at[units.a, 1], self.w_all.at[units.a, 2]

        def remote(step, c, src, dst, at, size, peer):
            place = units.place(c, at, size)
            return pltpu.make_async_remote_copy(
                src_ref=src.at[place],
                dst_ref=dst.at[place],
                send_sem=self.sends.at[g, step, c % 4],
                recv_sem=self.recvs.at[g, step, c % 4],
                device_id=peer,
                device_id_type=MESH,
            )

        def first(c):
            copies = [
                remote(0, c, own, far, self.by_z, 1, self.xn),
                remote(1, c, own, far, self.by_y, 1, self.xn),
            ]
            if units.parts == 9:
                copies.append(remote(2, c, own, far, 8, 1, self.xn))
            return copies

        def second(c):
            return [
                remote(3, c, far, far, self.by_z, 1, self.yn),
                remote(4, c, far, far, self.by_y, 1, self.zn),
            ]

        def third(c):
            return [
                remote(5, c, far, far, self.pair_z, 2, self.zn),
                remote(6, c, far, far, self.pair_y, 2, self.yn),
            ]

        def across(c):
            return [remote(7, c, far, both, 0, units.parts, self.sib)]

        return first, second, third, across


def gelu_both(v):
    c = (2.0 / jnp.pi) ** 0.5
    square = v * v
    t = jnp.tanh(c * v * (1.0 + 0.044715 * square))
    half = 0.5 * (1.0 + t)
    slope = half + 0.5 * v * (1.0 - t * t) * (c * (1.0 + 3.0 * 0.044715 * square))
    return v * half, slope


def pieces_of(ff):
    if ff != 1152:
        return [(0, ff)]
    return [(0, 256), (256, 256), (512, 256), (768, 384)]


def stream_of(ff, lw):
    at, downs, ups = 0, [], []
    for _, size in pieces_of(ff):
        downs.append(at)
        ups.append(at + size)
        at += 2 * size
    return downs, ups, at, at + lw


def split_stream(rows, ff, lw):
    downs, ups, out_row, qkv_row = stream_of(ff, lw)
    sizes = [size for _, size in pieces_of(ff)]
    down, up = (
        jnp.concatenate([rows[at : at + size] for at, size in zip(starts, sizes)])
        for starts in (downs, ups)
    )
    return down, up, rows[out_row:qkv_row], from_halves(rows[qkv_row : qkv_row + 3 * lw])


MID_TICKS, OUT_TICKS, LAST_TICKS = 2, 2, 4


def plan_of(ff, lw, n):
    downs, ups, out_row, qkv_row = stream_of(ff, lw)
    sizes = [size for _, size in pieces_of(ff)]
    tick, far, own = 0, [], []
    ends = [2 * size + at for size, at in zip(sizes, downs)]
    for end in ends:
        far.append((tick + 2, end))
        own.append((tick + n, end))
        tick += n
    tick += MID_TICKS + OUT_TICKS
    far.append((tick, qkv_row))
    own.append((tick, qkv_row))
    for half in (1, 2):
        far.append((tick + 2, qkv_row + half * 3 * lw // 2))
        own.append((tick + n, qkv_row + half * 3 * lw // 2))
        tick += n
    total = (2 * ff + 4 * lw) // CHUNK + 1
    far.append((tick + LAST_TICKS, total * CHUNK))
    own.append((tick + LAST_TICKS, total * CHUNK))

    def there(events, now, chunk):
        return any(at <= now and end >= (chunk + 1) * CHUNK for at, end in events)

    x_at, l_at, now = [], [], 0
    while len(l_at) < total:
        if len(l_at) < len(x_at) and x_at[len(l_at)] + 2 <= now and there(own, now, len(l_at)):
            l_at.append(now)
        if len(x_at) < total and there(far, now, len(x_at)):
            x_at.append(now)
        now += 1

    def runs(starts):
        out = []
        for chunk, at in enumerate(starts):
            if out and out[-1][0] + out[-1][2] == at:
                out[-1][2] += 1
            else:
                out.append([at, chunk, 1])
        return out

    return runs(x_at), runs(l_at), l_at[-1] + 14


def in_runs(tick, runs):
    chunk, inside = 0, False
    for start, first, size in runs:
        here = (tick >= start) & (tick < start + size)
        chunk = jnp.where(here, first + tick - start, chunk)
        inside = here | inside
    return chunk, inside


class Reduction:
    def __init__(self, runs, d_in, s_own, s_far, x_in, out_ref, lp, tb, ry, ub, rz1, vb, rz2, ob, dsend, drecv, xsend, xrecv, loads, sends, recvs, outs):
        self.x_runs, self.l_runs, self.last_tick = runs
        self.d_in, self.s_own, self.s_far, self.x_in, self.out_ref = d_in, s_own, s_far, x_in, out_ref
        self.lp, self.tb, self.ry, self.ub, self.rz1, self.vb, self.rz2, self.ob = lp, tb, ry, ub, rz1, vb, rz2, ob
        self.dsend, self.drecv, self.xsend, self.xrecv = dsend, drecv, xsend, xrecv
        self.loads, self.sends, self.recvs, self.outs = loads, sends, recvs, outs
        dp, mp = lax.axis_index("dp"), lax.axis_index("mp")
        core, self.yb = mp % 2, dp % 2
        xb, self.z0, self.z1 = mp // 2, (dp // 2) % 2, dp // 4
        self.sib = (dp, mp + 1 - 2 * core)
        self.xn = (dp, mp + 2 - 4 * xb)
        self.yn = (dp + 1 - 2 * self.yb, mp)
        self.z1n = (dp + 2 - 4 * self.z0, mp)
        self.z2n = (dp + 4 - 8 * self.z1, mp)

    def greet(self):
        barrier = pltpu.get_barrier_semaphore()
        for peer in (self.sib, self.xn, self.yn, self.z1n, self.z2n):
            pl.semaphore_signal(barrier, inc=1, device_id=peer, device_id_type=MESH)
        pl.semaphore_wait(barrier, 5)

    def to_sibling(self, which, flush, source, row, size):
        return pltpu.make_async_remote_copy(
            src_ref=source,
            dst_ref=self.d_in.at[which, pl.ds(row, size)],
            send_sem=self.dsend.at[which, flush],
            recv_sem=self.drecv.at[which, flush],
            device_id=self.sib,
            device_id_type=MESH,
        )

    def x_copy(self, c):
        return pltpu.make_async_remote_copy(
            src_ref=self.s_far.at[rows_at(c, CHUNK)],
            dst_ref=self.x_in.at[rows_at(c, CHUNK)],
            send_sem=self.xsend.at[c],
            recv_sem=self.xrecv.at[c],
            device_id=self.xn,
            device_id_type=MESH,
        )

    def tick(self, tick):
        yb, z0, z1 = self.yb, self.z0, self.z1
        half, quarter, eighth = CHUNK // 2, CHUNK // 4, CHUNK // 8
        at_y = pl.multiple_of(yb * half, half)
        at_z1 = pl.multiple_of(yb * half + z0 * quarter, quarter)
        at_z2 = pl.multiple_of(yb * half + z0 * quarter + z1 * eighth, eighth)
        lp, tb, ub, vb, ob = self.lp, self.tb, self.ub, self.vb, self.ob

        def remote(stage, slot, src, dst, peer):
            return pltpu.make_async_remote_copy(
                src_ref=src,
                dst_ref=dst,
                send_sem=self.sends.at[stage, slot],
                recv_sem=self.recvs.at[stage, slot],
                device_id=peer,
                device_id_type=MESH,
            )

        def load(which, c):
            source = (self.s_own, self.x_in)[which].at[rows_at(c, CHUNK)]
            return pltpu.make_async_copy(source, lp.at[c % 2, which], self.loads.at[which, c % 2])

        def y_copy(c):
            part = rows_at(1 - yb, half)
            return remote(0, c % 4, tb.at[c % 2, part], self.ry.at[c % 4], self.yn)

        def z1_copy(c):
            part = rows_at(1 - z0, quarter)
            return remote(1, c % 4, ub.at[c % 2, part], self.rz1.at[c % 4], self.z1n)

        def z2_copy(c):
            part = rows_at(1 - z1, eighth)
            return remote(2, c % 4, vb.at[c % 2, part], self.rz2.at[c % 4], self.z2n)

        def back(stage, c, at, size, peer):
            place = ob.at[c % OUT_SLOTS, pl.ds(at, size)]
            return remote(stage, c % 4, place, place, peer)

        def az2_copy(c):
            return back(3, c, at_z2, eighth, self.z2n)

        def az1_copy(c):
            return back(4, c, at_z1, quarter, self.z1n)

        def ay_copy(c):
            return back(5, c, at_y, half, self.yn)

        def out_copy(c):
            return pltpu.make_async_copy(
                ob.at[c % OUT_SLOTS], self.out_ref.at[rows_at(c, CHUNK)], self.outs.at[c % 2]
            )

        def stage(lag, work):
            c, inside = in_runs(tick - lag, self.l_runs)

            @pl.when(inside)
            def _():
                work(c)

        def leave(c):
            out_copy(c).wait()

        def store(c):
            ay_copy(c).wait()
            out_copy(c).start()

        def go_ay(c):
            az1_copy(c).wait()
            ay_copy(c).start()

        def go_az1(c):
            az2_copy(c).wait()
            az1_copy(c).start()

        def go_az2(c):
            z2_copy(c).wait()
            ob[c % OUT_SLOTS, pl.ds(at_z2, eighth)] = vb[c % 2, rows_at(z1, eighth)] + self.rz2[c % 4]
            az2_copy(c).start()

        def go_z2(c):
            z1_copy(c).wait()
            vb[c % 2] = ub[c % 2, rows_at(z0, quarter)] + self.rz1[c % 4]
            z2_copy(c).start()

        def go_z1(c):
            y_copy(c).wait()
            ub[c % 2] = tb[c % 2, rows_at(yb, half)] + self.ry[c % 4]
            z1_copy(c).start()

        def go_y(c):
            for which in range(2):
                load(which, c).wait()
            tb[c % 2] = lp[c % 2, 0] + lp[c % 2, 1]
            y_copy(c).start()

        def go_load(c):
            self.x_copy(c).wait()
            for which in range(2):
                load(which, c).start()

        stage(14, leave)
        stage(13, store)
        stage(11, go_ay)
        stage(9, go_az1)
        stage(7, go_az2)
        stage(5, go_z2)
        stage(3, go_z1)
        stage(1, go_y)
        stage(0, go_load)
        c, inside = in_runs(tick, self.x_runs)

        @pl.when(inside)
        def _():
            self.x_copy(c).start()


N_RED = 21


def block_kernel(n, heads, tile, paired, *refs):
    refs = list(refs)

    def take(count):
        taken = refs[:count]
        del refs[:count]
        return taken

    tokens, upstream, item, ids, ids_row, mod, qkv_bias, b_out, b_up, b_down, act = take(11)
    own = take(3) if paired else None
    w_all = None if paired else take(1)[0]
    output_hbm, gtok_hbm, sums_ref, gb_down, gb_out, gb_up, gb_qv = take(7)
    normed_hbm, branch_hbm, qkv_hbm, att_hbm = take(4)
    if paired:
        (w_all,), shared = take(1), take(5)
    else:
        (g_all,) = take(1)
    n_buf, d_buf, acc_a, acc_b, up_buf, down_buf, w_buf, hid_buf, dpre_buf, stage_buf, r_buf = take(11)
    qkv_buf, att_buf, datt_buf, dproj_buf, fold_buf, sum_buf, b_buf, lse = take(8)
    up_sem, down_sem, n_sem, stage_sem, r_sem, w_sem, qkv_sem, att_sem, b_sem = take(9)
    ff = w_all.shape[2]
    pieces = pieces_of(ff)
    if paired:
        gather = Gather(units_of(ff, pieces), own, w_all, *take(4))
        red = Reduction(plan_of(ff, heads * HEAD, n), *shared, *refs)
        red.greet()
        gather.begin()
        tick, gather_tick = red.tick, gather.tick
    else:

        def tick(t):
            pass

        gather_tick = tick

    rows, width = tokens.shape
    lw = heads * HEAD
    frames = rows // SLOT
    scale = HEAD ** (-0.5)
    tiles = rows // tile
    some, hh = 3 * lw // 2, heads // 2
    downs, ups, out_row, qkv_row = stream_of(ff, lw)
    fold_buf[...] = jnp.zeros_like(fold_buf)
    sum_buf[...] = jnp.zeros_like(sum_buf)
    gb_up[...] = jnp.zeros_like(gb_up)

    def landed(m, blocks):
        if not paired:
            return

        @pl.when(m % 2 == 0)
        def _():
            for slot, block in enumerate(blocks):
                if block is None:
                    continue
                flush, row, size = block
                stage = stage_buf.at[slot, pl.ds(0, size)]
                sent = red.to_sibling(m // 2, flush, stage, row, size)
                sent.wait()
                fetch(m // 2, slot, row, size).start()

    def fetch(which, slot, row, size):
        return pltpu.make_async_copy(
            red.d_in.at[which, pl.ds(row, size)], r_buf.at[slot, pl.ds(0, size)], r_sem.at[slot]
        )

    def put(target, slot, row, size):
        return pltpu.make_async_copy(
            stage_buf.at[slot, pl.ds(0, size)], target.at[pl.ds(row, size)], stage_sem.at[slot]
        )

    def settle(blocks):
        if paired:
            for slot, (flush, row, size) in enumerate(blocks):
                put(red.s_own, slot, row, size).wait()

    def leave(m, slot, block, value):
        flush, row, size = block
        if not paired:
            stage_buf[slot, pl.ds(0, size), :] = value.astype(bf16)
            copy = put(g_all.at[m], slot, row, size)
            copy.start()
            copy.wait()
            return

        @pl.when(m % 2 == 1)
        def _():
            stage_buf[slot, pl.ds(0, size), :] = value.astype(bf16)
            stage = stage_buf.at[slot, pl.ds(0, size)]
            red.to_sibling(m // 2, flush, stage, row, size).start()

        @pl.when(m % 2 == 0)
        def _():
            fetch(m // 2, slot, row, size).wait()
            total = value + r_buf[slot, pl.ds(0, size), :].astype(f32)
            stage_buf[slot, pl.ds(0, size), :] = total.astype(bf16)

            @pl.when(m == 0)
            def _():
                put(red.s_own, slot, row, size).start()

            @pl.when(m > 0)
            def _():
                put(red.s_far, slot, row, size).start()

    def w_copies(p, m, slot):
        at, size = pieces[p]
        here = pl.ds(at, size)
        up_part, down_part = up_buf.at[slot, :, pl.ds(0, size)], down_buf.at[slot, pl.ds(0, size), :]
        return (
            Shard(own, w_all, 1, m, (slice(None), here), up_part, up_sem.at[slot]),
            Shard(own, w_all, 2, m, (here, slice(None)), down_part, down_sem.at[slot]),
        )

    def f_copies(m):
        return [
            Shard(own, w_all, 0, m, pl.ds(half * some, some), w_buf.at[half], w_sem.at[half])
            for half in range(2)
        ] + [Shard(own, w_all, 0, m, pl.ds(3 * lw, lw), r_buf.at[m % 2, pl.ds(0, lw)], r_sem.at[m % 2])]

    def f_start(m):
        for copy in f_copies(m):
            copy.start()

    def qkv_out(m, half):
        return pltpu.make_async_copy(qkv_buf.at[half], qkv_hbm.at[m, half], qkv_sem.at[half])

    def att_out(m):
        return pltpu.make_async_copy(att_buf.at[m % 2], att_hbm.at[m], att_sem.at[m % 2])

    f_start(0)

    def normed_part(i, carry):
        gather_tick(i)

        def block(j, c):
            at = pl.ds(pl.multiple_of(i * SLOT + j * BLOCK, BLOCK), BLOCK)
            col = item[at, :]
            normed, _ = normal(tokens[at, :].astype(f32))
            n_buf[at, :] = (normed * (1.0 + pick(col, mod, 1)) + pick(col, mod, 0)).astype(bf16)
            acc_a[at, :] = jnp.broadcast_to(b_out[...], (BLOCK, width))
            return c

        lax.fori_loop(0, SLOT // BLOCK, block, 0, unroll=UNROLL)
        return carry

    lax.fori_loop(0, frames, normed_part, 0)
    normed_out = pltpu.make_async_copy(n_buf, normed_hbm, n_sem)
    normed_out.start()
    if paired:
        gather.near(0).wait()

    def attend_part(m, carry):
        for copy in f_copies(m):
            copy.wait()

        @pl.when(m >= 1)
        def _():
            for half in range(2):
                qkv_out(m - 1, half).wait()

        @pl.when(m >= 2)
        def _():
            att_out(m - 2).wait()

        for half in range(2):
            bias = jnp.transpose(jnp.broadcast_to(qkv_bias[m, half], (8, some)))[:, 0:1]
            proj = nt(w_buf[half], n_buf[...]) + bias
            for h in range(3 * hh):
                qkv_buf[half, h] = proj[h * HEAD : (h + 1) * HEAD].astype(bf16)
            qkv_out(m, half).start()

        if paired:

            @pl.when(m == 2)
            def _():
                gather_tick(frames * 3 + 2)

        @pl.when((m + 1 < n) & (m != 1) if paired else m + 1 < n)
        def _():
            f_start(m + 1)

        def frame(f, c):
            gather_tick(frames + m * frames + f + jnp.where(m > 1, EXTRA, 0))
            at = rows_at(f, SLOT)
            pairs = pair_bias(ids[at, :], ids_row[pl.ds(f, 1), :])
            heads_qkv = [
                [qkv_buf[h // hh, j * hh + h % hh, :, at] for j in range(3)] for h in range(heads)
            ]
            all_scores = [tn(k, q) * scale + pairs for q, k, _ in heads_qkv]
            all_weights = []
            for h, scores in enumerate(all_scores):
                peak = jnp.max(scores, axis=0, keepdims=True)
                weights = jnp.exp(scores - peak)
                total = jnp.sum(weights, axis=0, keepdims=True)
                lse[m, h : h + 1, at] = peak + jnp.log(total)
                all_weights.append((weights.astype(bf16), 1.0 / total))
            outs = [dot(v, w) * inverse for (_, _, v), (w, inverse) in zip(heads_qkv, all_weights)]
            att_buf[m % 2, :, at] = jnp.concatenate(outs, axis=0).astype(bf16)
            return c

        lax.fori_loop(0, frames, frame, 0)
        att_out(m).start()

        def branch(j, c):
            at = rows_at(j, tile)
            acc_a[at, :] += tn(att_buf[m % 2, :, at], r_buf[m % 2, pl.ds(0, lw), :])
            return c

        lax.fori_loop(0, tiles, branch, 0)
        if paired:

            @pl.when(m == 1)
            def _():
                gather_tick(frames * 3)
                gather_tick(frames * 3 + 1)
                f_start(m + 1)

        return carry

    lax.fori_loop(0, n, attend_part, 0)
    if paired:
        gather.near(1).wait()
        gather.near(2).wait()
    for copy in w_copies(0, n - 1, 0):
        copy.start()
    for half in range(2):
        qkv_out(n - 1, half).wait()
    for m in range(max(n - 2, 0), n):
        att_out(m).wait()
    normed_out.wait()

    def b_copy(i):
        return pltpu.make_async_copy(branch_hbm.at[rows_at(i, SLOT)], b_buf.at[i % 2], b_sem.at[i % 2])

    def b_out_copy(i):
        return pltpu.make_async_copy(b_buf.at[i % 2], branch_hbm.at[rows_at(i, SLOT)], b_sem.at[i % 2])

    def first(i, carry):
        gather_tick(frames * (n + 1) + EXTRA + i)

        @pl.when(i >= 2)
        def _():
            b_out_copy(i - 2).wait()

        def block(j, c):
            at = pl.ds(pl.multiple_of(i * SLOT + j * BLOCK, BLOCK), BLOCK)
            col = item[at, :]
            branch = acc_a[at, :]
            b_buf[i % 2, rows_at(j, BLOCK), :] = branch
            middle = tokens[at, :].astype(f32) + pick(col, mod, 2) * branch
            normed, _ = normal(middle)
            n_buf[at, :] = (normed * (1.0 + pick(col, mod, 4)) + pick(col, mod, 3)).astype(bf16)
            d = (pick(col, mod, 5) * upstream[at, :].astype(f32)).astype(bf16)
            d_buf[at, :] = d
            sum_buf[0] += fold(d.astype(f32))
            acc_a[at, :] = jnp.broadcast_to(b_down[...], (BLOCK, width))
            acc_b[at, :] = jnp.zeros((BLOCK, width), f32)
            return c

        lax.fori_loop(0, SLOT // BLOCK, block, 0, unroll=UNROLL)
        b_out_copy(i).start()
        return carry

    lax.fori_loop(0, frames, first, 0)
    for i in range(max(frames - 2, 0), frames):
        b_out_copy(i).wait()

    def by_slots(work, after):
        b_copy(0).start()

        def slot_part(i, carry):
            b_copy(i).wait()

            @pl.when(i + 1 < frames)
            def _():
                b_copy(i + 1).start()

            def block(j, c):
                work(i, pl.ds(pl.multiple_of(i * SLOT + j * BLOCK, BLOCK), BLOCK), rows_at(j, BLOCK))
                return c

            lax.fori_loop(0, SLOT // BLOCK, block, 0, unroll=UNROLL)
            after(i)
            return carry

        lax.fori_loop(0, frames, slot_part, 0)

    def blocks_of(p):
        size = pieces[p][1]
        return ((2 * p, downs[p], size), (2 * p + 1, ups[p], size))

    now = 0
    for p, (p_at, p_size) in enumerate(pieces):
        def shard(i, carry, p=p, p_at=p_at, p_size=p_size, now=now):
            m = n - 1 - i
            slot = (p * n + i) % 2
            for copy in w_copies(p, m, slot):
                copy.wait()

            @pl.when(i + 1 < n)
            def _():
                for copy in w_copies(p, m - 1, 1 - slot):
                    copy.start()

            if p + 1 < len(pieces):

                @pl.when(i + 1 == n)
                def _():
                    for copy in w_copies(p + 1, n - 1, 1 - slot):
                        copy.start()

            blocks = blocks_of(p)
            bias = b_up[m, :, pl.ds(p_at, p_size)]
            up = up_buf.at[slot, :, pl.ds(0, p_size)]
            down = down_buf.at[slot, pl.ds(0, p_size), :]

            def part(j, c):
                at = rows_at(j, tile)
                pre = jnp.dot(n_buf[at, :], up[...], preferred_element_type=f32) + bias
                hidden, slope = gelu_both(pre)
                hidden = hidden.astype(bf16)
                dpre = nt(d_buf[at, :], down[...]) * slope
                dpre = dpre.astype(bf16)
                hid_buf[at, pl.ds(0, p_size)] = hidden
                dpre_buf[at, pl.ds(0, p_size)] = dpre
                gb_up[m, :, pl.ds(p_at, p_size)] += jnp.sum(
                    dpre.astype(f32), axis=0, keepdims=True
                )
                acc_a[at, :] += jnp.dot(hidden, down[...], preferred_element_type=f32)
                acc_b[at, :] += nt(dpre, up[...])
                return c

            lax.fori_loop(0, tiles, part, 0)

            @pl.when(i == 2)
            def _():
                settle(blocks)

            if p:

                @pl.when(i == 0)
                def _():
                    settle(blocks_of(p - 1))

            if p < 2:
                gather_tick(frames * (n + 2) + EXTRA + now + i)
            tick(now + i)
            landed(m, blocks)
            leave(m, 0, blocks[0], tn(hid_buf[:, pl.ds(0, p_size)], d_buf[...]))
            leave(m, 1, blocks[1], tn(dpre_buf[:, pl.ds(0, p_size)], n_buf[...]))
            return carry

        lax.fori_loop(0, n, shard, 0)
        now += n
    settle(blocks_of(len(pieces) - 1))

    def out_copies(m, slot):
        there = pl.ds(3 * lw, lw)
        return (
            Shard(own, w_all, 0, m, there, w_buf.at[slot, pl.ds(0, lw)], w_sem.at[slot]),
            pltpu.make_async_copy(att_hbm.at[m], att_buf.at[slot], att_sem.at[slot]),
        )

    def a_copies(half, m, slot):
        there = pl.ds(half * some, some)
        return (
            Shard(own, w_all, 0, m, there, w_buf.at[slot], w_sem.at[slot]),
            pltpu.make_async_copy(qkv_hbm.at[m, half], qkv_buf.at[slot], qkv_sem.at[slot]),
        )

    normed_copy = pltpu.make_async_copy(normed_hbm, n_buf, n_sem)
    normed_copy.start()
    for copy in out_copies(n - 1, 0):
        copy.start()

    def row_copy(target, i):
        return pltpu.make_async_copy(
            stage_buf.at[i % 2, pl.ds(0, SLOT)], target.at[rows_at(i, SLOT)], stage_sem.at[i % 2]
        )

    def rows_done(target):
        for i in range(max(frames - 2, 0), frames):
            row_copy(target, i).wait()

    def middle_part(i, at, here):
        col = item[at, :]
        gate = pick(col, mod, 2)
        branch = b_buf[i % 2, here, :]
        middle = tokens[at, :].astype(f32) + gate * branch
        dy = upstream[at, :].astype(f32)
        second = acc_a[at, :]
        stage_buf[i % 2, here, :] = (middle + pick(col, mod, 5) * second).astype(bf16)
        add_by_item(fold_buf, 5, col, dy * second)
        grad = acc_b[at, :]
        normed, rstd = normal(middle)
        add_by_item(fold_buf, 3, col, grad)
        add_by_item(fold_buf, 4, col, grad * normed)
        dmiddle = dy + normal_back(grad, pick(col, mod, 4), normed, rstd)
        acc_a[at, :] = dmiddle
        add_by_item(fold_buf, 2, col, dmiddle * branch)
        d = (gate * dmiddle).astype(bf16)
        d_buf[at, :] = d
        sum_buf[1] += fold(d.astype(f32))
        acc_b[at, :] = jnp.zeros((BLOCK, width), f32)

    def middle_done(i):
        row_copy(output_hbm, i).start()

        @pl.when((i >= 1) & (i + 1 < frames))
        def _():
            row_copy(output_hbm, i - 1).wait()

        @pl.when(i % 2 == 1)
        def _():
            tick(now + i // 2)

    by_slots(middle_part, middle_done)
    rows_done(output_hbm)
    now += MID_TICKS
    normed_copy.wait()
    out_block = (2 * len(pieces), out_row, lw)

    def out_part(i, carry):
        m = n - 1 - i
        slot = i % 2
        for copy in out_copies(m, slot):
            copy.wait()

        @pl.when(i + 1 < n)
        def _():
            for copy in out_copies(m - 1, 1 - slot):
                copy.start()

        @pl.when(i == 2)
        def _():
            settle((out_block,))

        landed(m, (out_block,))
        leave(m, 0, out_block, dot(att_buf[slot], d_buf[...]))
        datt = nt(w_buf[slot, pl.ds(0, lw), :], d_buf[...])
        for h in range(heads):
            datt_buf[m, h] = datt[h * HEAD : (h + 1) * HEAD].astype(bf16)

        @pl.when(i % 2 == 1)
        def _():
            tick(now + i // 2)

        return carry

    lax.fori_loop(0, n, out_part, 0)
    settle((out_block,))
    now += OUT_TICKS
    for copy in a_copies(0, n - 1, 0):
        copy.start()

    def qkv_block(half):
        return (2 * len(pieces) + 1 + half, qkv_row + half * some, some)

    for half in range(2):

        def attn(i, carry, half=half, now=now):
            m = n - 1 - i
            slot = i % 2
            for copy in a_copies(half, m, slot):
                copy.wait()

            @pl.when(i + 1 < n)
            def _():
                for copy in a_copies(half, m - 1, 1 - slot):
                    copy.start()

            if half == 0:

                @pl.when(i + 1 == n)
                def _():
                    for copy in a_copies(1, n - 1, 1 - slot):
                        copy.start()

            def frame(f, c):
                at = rows_at(f, SLOT)
                pairs = pair_bias(ids[at, :], ids_row[pl.ds(f, 1), :])
                each = range(hh)
                q, k, v = ([qkv_buf[slot, j * hh + h, :, at] for h in each] for j in range(3))
                d = [datt_buf[m, half * hh + h, :, at] for h in each]
                lses = [lse[m, half * hh + h : half * hh + h + 1, at] for h in each]
                scores = [tn(k[h], q[h]) * scale + pairs for h in each]
                probs = [jnp.exp(scores[h] - lses[h]) for h in each]
                dprobs = [tn(v[h], d[h]) for h in each]
                low, dscores = [], []
                for h in each:
                    inner = jnp.sum(dprobs[h] * probs[h], axis=0, keepdims=True)
                    low.append(probs[h].astype(bf16))
                    dscores.append((probs[h] * (dprobs[h] - inner)).astype(bf16))
                dvs = [nt(d[h], low[h]) for h in each]
                dqs = [dot(k[h], dscores[h]) * scale for h in each]
                dks = [nt(q[h], dscores[h]) * scale for h in each]
                dproj_buf[:, at] = jnp.concatenate(dqs + dks + dvs, axis=0).astype(bf16)
                return c

            lax.fori_loop(0, frames, frame, 0)

            @pl.when(i == 2)
            def _():
                settle((qkv_block(half),))

            if half == 1:

                @pl.when(i == 0)
                def _():
                    settle((qkv_block(0),))

            tick(now + i)
            landed(m, (qkv_block(half),))
            gb_qv[m, half] = nt(jnp.ones((8, rows), bf16), dproj_buf[...])[0:1]
            leave(m, 0, qkv_block(half), dot(dproj_buf[...], n_buf[...]))

            def part(j, c):
                at = rows_at(j, tile)
                acc_b[at, :] += tn(dproj_buf[:, at], w_buf[slot, pl.ds(0, some), :])
                return c

            lax.fori_loop(0, tiles, part, 0)
            return carry

        lax.fori_loop(0, n, attn, 0)
        now += n
    settle((qkv_block(1),))

    def last(i, carry):
        def block(j, c):
            at = pl.ds(pl.multiple_of(i * SLOT + j * BLOCK, BLOCK), BLOCK)
            col = item[at, :]
            normed, rstd = normal(tokens[at, :].astype(f32))
            grad = acc_b[at, :]
            add_by_item(fold_buf, 0, col, grad)
            add_by_item(fold_buf, 1, col, grad * normed)
            value = acc_a[at, :] + normal_back(grad, pick(col, mod, 1), normed, rstd)
            stage_buf[i % 2, rows_at(j, BLOCK), :] = value.astype(bf16)
            return c

        lax.fori_loop(0, SLOT // BLOCK, block, 0, unroll=UNROLL)
        row_copy(gtok_hbm, i).start()

        @pl.when((i >= 1) & (i + 1 < frames))
        def _():
            row_copy(gtok_hbm, i - 1).wait()

        tick(now + i)
        return carry

    lax.fori_loop(0, frames, last, 0)
    rows_done(gtok_hbm)
    for j in range(sums_ref.shape[0]):
        for k in range(6):
            sums_ref[j, k : k + 1, :] = jnp.sum(fold_buf[j, k], axis=0, keepdims=True)
    gb_down[...] = jnp.sum(sum_buf[0], axis=0, keepdims=True)
    gb_out[...] = jnp.sum(sum_buf[1], axis=0, keepdims=True)
    if paired:
        dp, mp = lax.axis_index("dp"), lax.axis_index("mp")
        items = sums_ref.shape[0]
        base = lax.axis_size("dp") * items * 6
        block = (2 * len(pieces) + 3, 2 * ff + 4 * lw, CHUNK)

        def line(a, row):
            return acc_b.at[pl.ds(a * CHUNK + row, 1)]

        more_at = base + lax.axis_size("dp") * items
        acc_b[pl.ds(0, n * CHUNK), :] = jnp.zeros((n * CHUNK, width), f32)
        for a in range(n):
            for j in range(items):
                own_sums = sums_ref[j, :, a * lw : (a + 1) * lw]
                for k in range(6):
                    line(a, (dp * items + j) * 6 + k)[:, pl.ds(0, lw)] = own_sums[k : k + 1]
                line(a, base + dp * items + j)[...] = jnp.where(mp == 0, act[j : j + 1, :], 0.0)
            line(a, more_at)[...] = gb_out[...]
            line(a, more_at + 1)[...] = gb_down[...]
        core, xb = mp % 2, mp // 2
        for m, slot in ((3, 0), (1, 1), (2, 0), (0, 1)):
            here = (xb if m < 2 else 1 - xb) * 2 + (core if m % 2 == 0 else 1 - core)
            line(here, more_at + 2)[...] = gb_up[m]
            for j in range(2):
                for half in range(2):
                    line(here, more_at + 3 + j)[:, half * lw // 2 : (half + 1) * lw // 2] = gb_qv[m, half, :, j * lw : j * lw + lw // 2]
            if m % 2 == 0:
                landed(m, (None,) * slot + (block,))
            leave(m, slot, block, acc_b[rows_at(here, CHUNK), :])
        settle((block, block))

        def drain(t, carry):
            tick(t)
            return carry

        lax.fori_loop(now + LAST_TICKS, red.last_tick + 1, drain, 0)


def block(tokens, upstream, item, ids, mod, qkv_bias, b_out, b_up, b_down, act, weights, paired):
    rows, width = tokens.shape
    n, ff = b_up.shape[0], b_up.shape[2]
    heads = 4
    lw = heads * HEAD
    pieces = pieces_of(ff)
    widest = max(size for _, size in pieces)
    tile = min(512, rows)
    total = 2 * ff + 4 * lw
    deep = max(widest, 3 * lw // 2, SLOT)
    slots = 2
    flushes = 2 * len(pieces) + 4
    half, quarter, eighth = CHUNK // 2, CHUNK // 4, CHUNK // 8
    vmem = pl.BlockSpec(memory_space=pltpu.VMEM)
    hbm = pl.BlockSpec(memory_space=pl.ANY)
    dma = pltpu.SemaphoreType.DMA

    def low(*shape):
        return jax.ShapeDtypeStruct(shape, bf16)

    def full(*shape):
        return jax.ShapeDtypeStruct(shape, f32)

    def buf(*shape):
        return pltpu.VMEM(shape, bf16)

    grads = [low(n, total, width)]
    extra = []
    if paired:
        total += CHUNK
        grads = [low(3, n - 1, ff, width), low(2, total, width)] + [low(total, width)] * 4
        extra = [
            dma((5, 8, 4)),
            dma((5, 8, 4)),
            dma((3,)),
            dma((3,)),
            buf(2, 2, CHUNK, width),
            buf(2, CHUNK, width),
            buf(4, half, width),
            buf(2, half, width),
            buf(4, quarter, width),
            buf(2, quarter, width),
            buf(4, eighth, width),
            buf(OUT_SLOTS, CHUNK, width),
            dma((2, flushes)),
            dma((2, flushes)),
            dma((total // CHUNK,)),
            dma((total // CHUNK,)),
            dma((2, 2)),
            dma((6, 4)),
            dma((6, 4)),
            dma((2,)),
        ]
    return pl.pallas_call(
        functools.partial(block_kernel, n, heads, tile, paired),
        out_shape=(
            low(rows, width),
            low(rows, width),
            jax.ShapeDtypeStruct(mod.shape, f32),
            full(1, width),
            full(1, width),
            full(n, 1, ff),
            full(n, 2, 1, 3 * lw // 2),
            low(rows, width),
            full(rows, width),
            low(n, 2, 3 * heads // 2, HEAD, rows),
            low(n, lw, rows),
            *grads,
        ),
        in_specs=[vmem] * 11 + [hbm] * len(weights),
        out_specs=(hbm,) * 2 + (vmem,) * 5 + (hbm,) * (4 + len(grads)),
        scratch_shapes=[
            buf(rows, width),
            buf(rows, width),
            pltpu.VMEM((rows, width), f32),
            pltpu.VMEM((rows, width), f32),
            buf(2, width, widest),
            buf(2, widest, width),
            buf(2, 3 * lw // 2, width),
            buf(rows, widest),
            buf(rows, widest),
            buf(slots, deep, width),
            buf(slots, deep, width),
            buf(2, 3 * heads // 2, HEAD, rows),
            buf(2, lw, rows),
            buf(n, heads, HEAD, rows),
            buf(3 * lw // 2, rows),
            pltpu.VMEM((mod.shape[0], 6, 8, width), f32),
            pltpu.VMEM((2, 8, width), f32),
            pltpu.VMEM((2, SLOT, width), f32),
            pltpu.VMEM((n, heads, rows), f32),
            dma((2,)),
            dma((2,)),
            dma,
            dma((slots,)),
            dma((slots,)),
            dma((2,)),
            dma((2,)),
            dma((2,)),
            dma((2,)),
            *extra,
        ],
        compiler_params=pltpu.CompilerParams(
            collective_id=0 if paired else None, has_side_effects=paired, vmem_limit_bytes=63 << 20
        ),
    )(
        tokens, upstream, item[:, None], ids[:, None], ids.reshape(-1, SLOT), mod,
        qkv_bias.reshape(n, 2, 1, 3 * lw // 2), b_out, b_up, b_down, act, *weights,
    )


def by_halves(rows):
    halves = rows.reshape(3, 2, -1, *rows.shape[1:])
    return jnp.swapaxes(halves, 0, 1).reshape(rows.shape)


def from_halves(rows):
    halves = rows.reshape(2, 3, -1, *rows.shape[1:])
    return jnp.swapaxes(halves, 0, 1).reshape(rows.shape)


def swap(values, axis, bit):
    n = lax.axis_size(axis)
    return lax.ppermute(values, axis, [(i, i ^ bit) for i in range(n)])


def shards(
    paired,
    tokens,
    condition,
    grid_rows,
    grid_cols,
    frame_start,
    frame_item,
    group_frames,
    w_qkv,
    qv_bias,
    w_out,
    b_out,
    w_up,
    b_up,
    w_down,
    b_down,
    w_ada,
    b_ada,
    cotangent,
):
    own_rows, width = tokens.shape
    local_width = w_qkv.shape[2]
    local_ff = w_up.shape[1]
    items = condition.shape[0]
    n_mp, n_dp = lax.axis_size("mp"), lax.axis_size("dp")
    mp, dp = lax.axis_index("mp"), lax.axis_index("dp")
    n = width // (4 * HEAD)
    lw, ff = width // n, local_ff * n_mp // n
    frame_id, item_id = frame_tables(
        grid_rows, grid_cols, frame_start, frame_item, group_frames[0], mp * own_rows, own_rows
    )
    cond_value = condition.astype(f32)
    act_low = jax.nn.silu(cond_value).astype(bf16)
    ada_flat = w_ada.reshape(width, -1)
    ada_local = dot(act_low, ada_flat) + b_ada.reshape(-1).astype(f32)
    ada_local = ada_local.reshape(items, 6, local_width)
    qkv_local = w_qkv.transpose(1, 2, 0)
    if paired:
        qkv_bias = jnp.concatenate(
            [qv_bias[0].astype(f32), jnp.zeros((lw,), f32), qv_bias[1].astype(f32)]
        )
        small = jnp.concatenate([ada_local.reshape(-1), by_halves(qkv_bias), b_up.astype(f32)])
        small = jnp.stack([small] + [swap(small, "mp", bit) for bit in range(1, n)])
        sorted_small = jnp.where(mp % 2 == 0, small, small[jnp.array([1, 0, 3, 2])])
        sorted_small = jnp.where(mp < 2, sorted_small, sorted_small[jnp.array([2, 3, 0, 1])])
        n_ada = ada_local.size
        modulation = sorted_small[:, :n_ada].reshape(n, items, 6, lw)
        qkv_bias = small[:, n_ada : n_ada + 3 * lw]
        up_bias = small[:, n_ada + 3 * lw :]
        weights = [
            jnp.concatenate([by_halves(qkv_local.reshape(3 * lw, width)), w_out], axis=0),
            w_up,
            w_down,
        ]
    else:
        modulation = lax.all_gather(ada_local, "mp", axis=0)
        qv = lax.all_gather(qv_bias.astype(f32), "mp", axis=1, tiled=True)
        qkv_bias = jnp.stack([qv[0], jnp.zeros((width,), f32), qv[1]])
        qkv_bias = jax.vmap(by_halves)(qkv_bias.reshape(3, n, lw).transpose(1, 0, 2).reshape(n, 3 * lw))
        up_bias = lax.all_gather(b_up.astype(f32), "mp", axis=0, tiled=True).reshape(n, ff)
        qkv = lax.all_gather(qkv_local, "mp", axis=1, tiled=True)
        qkv = qkv.reshape(3, n, lw, width).transpose(1, 0, 2, 3).reshape(n, 3 * lw, width)
        qkv = jax.vmap(by_halves)(qkv)
        out = lax.all_gather(w_out, "mp", axis=0, tiled=True).reshape(n, lw, width)
        up = lax.all_gather(w_up, "mp", axis=1, tiled=True)
        up = up.reshape(width, n, ff).transpose(1, 0, 2)
        down = lax.all_gather(w_down, "mp", axis=0, tiled=True).reshape(n, ff, width)
        weights = [jnp.stack([jnp.concatenate([qkv, out], axis=1), up, down])]
    modulation = modulation.transpose(1, 2, 0, 3).reshape(items, 6, width)
    b_out_row, b_down_row = (b.astype(f32)[None] for b in (b_out, b_down))
    output, grad_tokens, item_grad, gb_down, gb_out, gb_up, gb_qv, *rest = block(
        tokens,
        cotangent,
        item_id,
        frame_id,
        modulation,
        qkv_bias,
        b_out_row,
        up_bias[:, None],
        b_down_row,
        act_low.astype(f32),
        weights,
        paired,
    )
    if paired:
        total_items = items * n_dp
        tail = rest[-1][2 * ff + 4 * lw :].astype(f32)
        at = total_items * 6
        dmod = tail[:at, :lw].reshape(total_items, 6, lw)
        act_all = tail[at : at + total_items]
        at += total_items
        gb_out, gb_down, gb_up = tail[at], tail[at + 1], tail[at + 2]
        gb_qv = tail[at + 3 : at + 5, :lw]
        own_dmod = lax.dynamic_slice_in_dim(dmod, dp * items, items)
        g_down, g_up, g_out, g_qkv = split_stream(rest[-1], ff, lw)
        g_down, g_out = g_down.astype(f32), g_out.astype(f32)
        g_up, g_qkv = g_up.astype(f32).T, g_qkv.astype(f32).T.reshape(width, 3, lw)
    else:

        gb_qv = jax.vmap(from_halves)(gb_qv.reshape(n, 3 * lw)).reshape(n, 3, lw)[:, ::2]

        def over_all(values, axis):
            part = lax.psum_scatter(values, "mp", scatter_dimension=axis, tiled=True)
            return lax.psum(part.astype(bf16), "dp").astype(f32)

        own_dmod = lax.psum_scatter(item_grad, "mp", scatter_dimension=2, tiled=True)
        dmod = lax.all_gather(own_dmod, "dp", axis=0, tiled=True)
        act_all = lax.all_gather(act_low, "dp", axis=0, tiled=True).astype(f32)
        g_down, g_up, g_out, g_qkv = jax.vmap(lambda g: split_stream(g, ff, lw))(rest[-1])
        g_down = over_all(g_down.reshape(n * ff, width), 0)
        g_up = over_all(g_up.reshape(n * ff, width).T, 1)
        g_qkv = g_qkv.reshape(n, 3, lw, width).transpose(3, 1, 0, 2).reshape(width, 3, width)
        g_qkv = over_all(g_qkv, 2)
        g_out = over_all(g_out.reshape(width, width), 0)
        gb_up = over_all(gb_up.reshape(-1), 0)
        gb_qv = over_all(gb_qv.transpose(1, 0, 2).reshape(2, width), 1)
        gb_out = lax.psum(gb_out[0], ("dp", "mp"))
        gb_down = lax.psum(gb_down[0], ("dp", "mp"))
    grad_w_ada = lax.dot_general(
        act_all,
        dmod.reshape(dmod.shape[0], -1),
        (((0,), (0,)), ((), ())),
        precision=lax.Precision.HIGHEST,
    ).reshape(width, 6, local_width)
    grad_b_ada = jnp.sum(dmod, axis=0)
    cond_term = lax.dot_general(
        own_dmod.reshape(items, -1),
        ada_flat.astype(f32),
        (((1,), (1,)), ((), ())),
        precision=lax.Precision.HIGHEST,
    )
    if paired:
        cond_term = cond_term + swap(cond_term, "mp", 1)
        cond_term = cond_term + swap(cond_term, "mp", 2)
    else:
        cond_term = lax.psum(cond_term, "mp")
    grad_condition = jax.vjp(jax.nn.silu, cond_value)[1](cond_term)[0]
    return (
        output,
        grad_tokens,
        grad_condition,
        g_qkv,
        gb_qv,
        g_out,
        gb_out,
        g_up,
        gb_up,
        g_down,
        gb_down,
        grad_w_ada,
        grad_b_ada,
    )


def solution(mesh):
    paired = dict(mesh.shape) == {"dp": 8, "mp": 4}
    return jax.shard_map(
        functools.partial(shards, paired),
        mesh=mesh,
        in_specs=(
            P(("dp", "mp"), None),
            P("dp", None),
            P("dp"),
            P("dp"),
            P("dp"),
            P("dp"),
            P("dp"),
            P(None, None, "mp"),
            P(None, "mp"),
            P("mp", None),
            P(),
            P(None, "mp"),
            P("mp"),
            P("mp", None),
            P(),
            P(None, None, "mp"),
            P(None, "mp"),
            P(("dp", "mp"), None),
        ),
        out_specs=(
            P(("dp", "mp"), None),
            P(("dp", "mp"), None),
            P("dp", None),
            P(None, None, "mp"),
            P(None, "mp"),
            P("mp", None),
            P(),
            P(None, "mp"),
            P("mp"),
            P("mp", None),
            P(),
            P(None, None, "mp"),
            P(None, "mp"),
        ),
        check_vma=False,
    )
```

```python
import functools

import jax
import jax.numpy as jnp
from jax import lax
from jax.experimental import pallas as pl
from jax.experimental.pallas import tpu as pltpu
from jax.sharding import PartitionSpec as P

HEAD = 72
SLOT = 256
CHUNK = 128
BLOCK = 128
UNROLL = 1
OUT_SLOTS = 10
TAIL = 48
MESH = pl.DeviceIdType.MESH
epsilon = 1e-06
f32 = jnp.float32
bf16 = jnp.bfloat16


def frame_tables(grid_rows, grid_cols, frame_start, frame_item, used, first, length):
    rows = first + jnp.arange(length, dtype=jnp.int32)[:, None]
    slots = jnp.arange(grid_rows.shape[0], dtype=jnp.int32)[None, :]
    ends = (frame_start + grid_rows * grid_cols)[None, :]
    inside = (rows >= frame_start[None, :]) & (rows < ends) & (slots < used)
    frame_id = jnp.sum(jnp.where(inside, slots + 1, 0), axis=1) - 1
    item_id = jnp.sum(jnp.where(inside, frame_item[None, :], 0), axis=1)
    return (frame_id, item_id)


def normal(values):
    centred = values - jnp.mean(values, axis=-1, keepdims=True)
    rstd = lax.rsqrt(jnp.mean(centred * centred, axis=-1, keepdims=True) + epsilon)
    return centred * rstd, rstd


def normal_back(grad, scale, normed, rstd):
    u = grad * (1.0 + scale)
    return rstd * (
        u
        - jnp.mean(u, axis=-1, keepdims=True)
        - normed * jnp.mean(u * normed, axis=-1, keepdims=True)
    )


def dot(left, right):
    return jnp.dot(left, right, preferred_element_type=f32)


def rows_at(i, size):
    return pl.ds(pl.multiple_of(i * size, size), size)


def pick(item_col, mod_ref, k):
    total = mod_ref[0, k : k + 1, :]
    for item in range(1, mod_ref.shape[0]):
        total = jnp.where(item_col == item, mod_ref[item, k : k + 1, :], total)
    return total


def fold(values):
    return jnp.sum(values.reshape(-1, 8, values.shape[-1]), axis=0)


def add_by_item(sums_ref, k, item_col, values):
    for item in range(sums_ref.shape[0]):
        sums_ref[item, k] += fold(jnp.where(item_col == item, values, 0.0))


def tn(left, right):
    return lax.dot_general(left, right, (((0,), (0,)), ((), ())), preferred_element_type=f32)


def nt(left, right):
    return lax.dot_general(left, right, (((1,), (1,)), ((), ())), preferred_element_type=f32)


class Shard:
    def __init__(self, own, others, a, m, part, target, sem):
        self.own, self.others, self.a, self.m, self.part = own, others, a, m, part
        self.target, self.sem = target, sem

    def copy(self, source):
        return pltpu.make_async_copy(source.at[self.part], self.target, self.sem)

    def start(self):
        if self.own is None:
            self.copy(self.others.at[self.a, self.m]).start()
            return

        @pl.when(self.m == 0)
        def _():
            self.copy(self.own[self.a]).start()

        @pl.when(self.m > 0)
        def _():
            self.copy(self.others.at[self.a, self.m - 1]).start()

    def wait(self):
        source = self.others.at[self.a, 0] if self.own is None else self.own[self.a]
        self.copy(source).wait()


def pair_bias(id_col, id_row):
    shape = (SLOT, SLOT)
    one = lax.broadcasted_iota(jnp.int32, shape, 0) == lax.broadcasted_iota(jnp.int32, shape, 1)
    same = (id_col == id_row) & (id_col >= 0)
    return jnp.where(same | one, 0.0, -1e30)


EXTRA = 4


class Units:
    def __init__(self, a, parts, ticks, place):
        self.a, self.parts, self.place, self.count = a, parts, place, len(ticks)
        self.runs = [[(unit[k], c, 1) for c, unit in enumerate(ticks)] for k in range(4)]


def units_of(depth, pieces):
    attn = depth // 4
    (_, wide), (last_at, last) = pieces[0], pieces[-1]

    def rows(first, part):
        return lambda c, at, size: (pl.ds(pl.multiple_of(first(c) + at * part, part), size * part), slice(None))

    def columns(first, width):
        return lambda c, at, size: (
            pl.ds(pl.multiple_of(at * (depth // 9), depth // 9), size * (depth // 9)),
            pl.ds(pl.multiple_of(first(c), 128), width),
        )

    return (
        Units(0, 9, ((4, 7, 8, 10), (8, 11, 12, 13), (10, 12, 13, 14), (12, 13, 14, 15)), rows(lambda c: c * attn, attn // 9)),
        Units(1, 9, ((16, 20, 23, 26), (19, 22, 25, 28), (24, 26, 28, 30)), columns(lambda c: c * wide, wide)),
        Units(2, 8, ((17, 21, 24, 27), (20, 24, 26, 29), (26, 28, 29, 31)), rows(lambda c: c * wide, wide // 8)),
        Units(1, 9, ((29, 30, 31, 32),), columns(lambda c: last_at, last)),
        Units(2, 8, ((30, 31, 32, 33),), rows(lambda c: last_at, last // 8)),
    )


class Gather:
    def __init__(self, units, own, w_all, sends, recvs, near_send, near_recv):
        self.units, self.own, self.w_all = units, own, w_all
        self.sends, self.recvs, self.near_send, self.near_recv = sends, recvs, near_send, near_recv
        dp, mp = lax.axis_index("dp"), lax.axis_index("mp")
        core, yb = mp % 2, dp % 2
        xb, z0 = mp // 2, (dp // 2) % 2
        self.sib = (dp, mp + 1 - 2 * core)
        self.xn = (dp, mp + 2 - 4 * xb)
        self.yn = (dp + 1 - 2 * yb, mp)
        self.zn = (dp + 2 - 4 * z0, mp)
        self.by_z, self.by_y = z0 * 2 + yb, 4 + yb * 2 + z0
        self.pair_z, self.pair_y = z0 * 2, 4 + yb * 2

    def near(self, a):
        return pltpu.make_async_remote_copy(
            src_ref=self.own[a],
            dst_ref=self.w_all.at[a, 0],
            send_sem=self.near_send.at[a],
            recv_sem=self.near_recv.at[a],
            device_id=self.sib,
            device_id_type=MESH,
        )

    def begin(self):
        self.near(0).start()
        for g, c in ((0, 0), (0, 1), (0, 2), (0, 3), (1, 0), (2, 0), (1, 1), (2, 1), (1, 2), (2, 2), (3, 0), (4, 0)):
            for copy in self.steps(g)[0](c):
                copy.start()
        self.near(1).start()
        self.near(2).start()

    def tick(self, tick):
        for g, units in enumerate(self.units):
            steps = self.steps(g)
            for k in (4, 3, 2, 1):
                c, inside = in_runs(tick, units.runs[k - 1])

                @pl.when(inside)
                def _(c=c, k=k, steps=steps):
                    for copy in steps[k - 1](c):
                        copy.wait()
                    if k < 4:
                        for copy in steps[k](c):
                            copy.start()

    def steps(self, g):
        units = self.units[g]
        own, far, both = self.own[units.a], self.w_all.at[units.a, 1], self.w_all.at[units.a, 2]

        def remote(step, c, src, dst, at, size, peer):
            place = units.place(c, at, size)
            return pltpu.make_async_remote_copy(
                src_ref=src.at[place],
                dst_ref=dst.at[place],
                send_sem=self.sends.at[g, step, c % 4],
                recv_sem=self.recvs.at[g, step, c % 4],
                device_id=peer,
                device_id_type=MESH,
            )

        def first(c):
            copies = [
                remote(0, c, own, far, self.by_z, 1, self.xn),
                remote(1, c, own, far, self.by_y, 1, self.xn),
            ]
            if units.parts == 9:
                copies.append(remote(2, c, own, far, 8, 1, self.xn))
            return copies

        def second(c):
            return [
                remote(3, c, far, far, self.by_z, 1, self.yn),
                remote(4, c, far, far, self.by_y, 1, self.zn),
            ]

        def third(c):
            return [
                remote(5, c, far, far, self.pair_z, 2, self.zn),
                remote(6, c, far, far, self.pair_y, 2, self.yn),
            ]

        def across(c):
            return [remote(7, c, far, both, 0, units.parts, self.sib)]

        return first, second, third, across


def gelu_both(v):
    c = (2.0 / jnp.pi) ** 0.5
    square = v * v
    t = jnp.tanh(c * v * (1.0 + 0.044715 * square))
    half = 0.5 * (1.0 + t)
    slope = half + 0.5 * v * (1.0 - t * t) * (c * (1.0 + 3.0 * 0.044715 * square))
    return v * half, slope


def pieces_of(ff):
    if ff != 1152:
        return [(0, ff)]
    return [(0, 256), (256, 256), (512, 256), (768, 384)]


def stream_of(ff, lw):
    at, downs, ups = 0, [], []
    for _, size in pieces_of(ff):
        downs.append(at)
        ups.append(at + size)
        at += 2 * size
    return downs, ups, at, at + lw


def split_stream(rows, ff, lw):
    downs, ups, out_row, qkv_row = stream_of(ff, lw)
    sizes = [size for _, size in pieces_of(ff)]
    down, up = (
        jnp.concatenate([rows[at : at + size] for at, size in zip(starts, sizes)])
        for starts in (downs, ups)
    )
    return down, up, rows[out_row:qkv_row], from_halves(rows[qkv_row : qkv_row + 3 * lw])


MID_TICKS, OUT_TICKS, LAST_TICKS, STEP_TICKS, ATTN_TICKS = 2, 2, 4, (1, 1, 1, 2), 1


def plan_of(ff, lw, n):
    downs, ups, out_row, qkv_row = stream_of(ff, lw)
    sizes = [size for _, size in pieces_of(ff)]
    tick, far, own = 0, [], []
    ends = [2 * size + at for size, at in zip(sizes, downs)]
    for beats, end in zip(STEP_TICKS, ends):
        far.append((tick + 2 * beats, end))
        own.append((tick + n * beats, end))
        tick += n * beats
    tick += MID_TICKS + OUT_TICKS
    far.append((tick, qkv_row))
    own.append((tick, qkv_row))
    for half in (1, 2):
        far.append((tick + 2 * ATTN_TICKS, qkv_row + half * 3 * lw // 2))
        own.append((tick + n * ATTN_TICKS, qkv_row + half * 3 * lw // 2))
        tick += n * ATTN_TICKS
    total = (2 * ff + 4 * lw) // CHUNK

    def there(events, now, chunk):
        return any(at <= now and end >= (chunk + 1) * CHUNK for at, end in events)

    x_at, l_at, now = [], [], 0
    while len(l_at) < total:
        if len(l_at) < len(x_at) and x_at[len(l_at)] + 2 <= now and there(own, now, len(l_at)):
            l_at.append(now)
        if len(x_at) < total and there(far, now, len(x_at)):
            x_at.append(now)
        now += 1

    def runs(starts):
        out = []
        for chunk, at in enumerate(starts):
            if out and out[-1][0] + out[-1][2] == at:
                out[-1][2] += 1
            else:
                out.append([at, chunk, 1])
        return out

    return runs(x_at), runs(l_at), l_at[-1] + 14


def in_runs(tick, runs):
    chunk, inside = 0, False
    for start, first, size in runs:
        here = (tick >= start) & (tick < start + size)
        chunk = jnp.where(here, first + tick - start, chunk)
        inside = here | inside
    return chunk, inside


class Reduction:
    def __init__(self, runs, t_buf, t_in, tsend, trecv, d_in, s_own, s_far, x_in, out_ref, lp, tb, ry, ub, rz1, vb, rz2, ob, dsend, drecv, xsend, xrecv, loads, sends, recvs, outs):
        self.x_runs, self.l_runs, self.last_tick = runs
        self.t_buf, self.t_in, self.tsend, self.trecv = t_buf, t_in, tsend, trecv
        self.d_in, self.s_own, self.s_far, self.x_in, self.out_ref = d_in, s_own, s_far, x_in, out_ref
        self.lp, self.tb, self.ry, self.ub, self.rz1, self.vb, self.rz2, self.ob = lp, tb, ry, ub, rz1, vb, rz2, ob
        self.dsend, self.drecv, self.xsend, self.xrecv = dsend, drecv, xsend, xrecv
        self.loads, self.sends, self.recvs, self.outs = loads, sends, recvs, outs
        dp, mp = lax.axis_index("dp"), lax.axis_index("mp")
        core, self.yb = mp % 2, dp % 2
        xb, self.z0, self.z1 = mp // 2, (dp // 2) % 2, dp // 4
        self.sib = (dp, mp + 1 - 2 * core)
        self.xn = (dp, mp + 2 - 4 * xb)
        self.yn = (dp + 1 - 2 * self.yb, mp)
        self.z1n = (dp + 2 - 4 * self.z0, mp)
        self.z2n = (dp + 4 - 8 * self.z1, mp)

    def greet(self):
        barrier = pltpu.get_barrier_semaphore()
        for peer in (self.sib, self.xn, self.yn, self.z1n, self.z2n):
            pl.semaphore_signal(barrier, inc=1, device_id=peer, device_id_type=MESH)
        pl.semaphore_wait(barrier, 5)

    def to_sibling(self, which, flush, source, row, size):
        return pltpu.make_async_remote_copy(
            src_ref=source,
            dst_ref=self.d_in.at[which, pl.ds(row, size)],
            send_sem=self.dsend.at[which, flush],
            recv_sem=self.drecv.at[which, flush],
            device_id=self.sib,
            device_id_type=MESH,
        )

    def x_copy(self, c):
        return pltpu.make_async_remote_copy(
            src_ref=self.s_far.at[rows_at(c, CHUNK)],
            dst_ref=self.x_in.at[rows_at(c, CHUNK)],
            send_sem=self.xsend.at[c],
            recv_sem=self.xrecv.at[c],
            device_id=self.xn,
            device_id_type=MESH,
        )

    def tail_copy(self, source, step, peer):
        return pltpu.make_async_remote_copy(
            src_ref=self.t_buf.at[source],
            dst_ref=self.t_in.at[step],
            send_sem=self.tsend.at[step],
            recv_sem=self.trecv.at[step],
            device_id=peer,
            device_id_type=MESH,
        )

    def tail(self, between):
        t_buf, t_in = self.t_buf, self.t_in
        copies = [self.tail_copy(1, 0, self.sib), self.tail_copy(3, 1, self.sib)]
        for copy in copies:
            copy.start()
        between(0)
        for copy in copies:
            copy.wait()
        t_buf[0] = t_buf[0] + t_in[0]
        t_buf[2] = t_buf[2] + t_in[1]
        for step, source, peer in ((2, 2, self.xn), (3, 0, self.yn), (4, 0, self.z1n), (5, 0, self.z2n)):
            copy = self.tail_copy(source, step, peer)
            copy.start()
            between(step - 1)
            copy.wait()
            t_buf[0] = t_buf[0] + t_in[step]

    def tick(self, tick):
        yb, z0, z1 = self.yb, self.z0, self.z1
        half, quarter, eighth = CHUNK // 2, CHUNK // 4, CHUNK // 8
        at_y = pl.multiple_of(yb * half, half)
        at_z1 = pl.multiple_of(yb * half + z0 * quarter, quarter)
        at_z2 = pl.multiple_of(yb * half + z0 * quarter + z1 * eighth, eighth)
        lp, tb, ub, vb, ob = self.lp, self.tb, self.ub, self.vb, self.ob

        def remote(stage, slot, src, dst, peer):
            return pltpu.make_async_remote_copy(
                src_ref=src,
                dst_ref=dst,
                send_sem=self.sends.at[stage, slot],
                recv_sem=self.recvs.at[stage, slot],
                device_id=peer,
                device_id_type=MESH,
            )

        def load(which, c):
            source = (self.s_own, self.x_in)[which].at[rows_at(c, CHUNK)]
            return pltpu.make_async_copy(source, lp.at[c % 2, which], self.loads.at[which, c % 2])

        def y_copy(c):
            part = rows_at(1 - yb, half)
            return remote(0, c % 4, tb.at[c % 2, part], self.ry.at[c % 4], self.yn)

        def z1_copy(c):
            part = rows_at(1 - z0, quarter)
            return remote(1, c % 4, ub.at[c % 2, part], self.rz1.at[c % 4], self.z1n)

        def z2_copy(c):
            part = rows_at(1 - z1, eighth)
            return remote(2, c % 4, vb.at[c % 2, part], self.rz2.at[c % 4], self.z2n)

        def back(stage, c, at, size, peer):
            place = ob.at[c % OUT_SLOTS, pl.ds(at, size)]
            return remote(stage, c % 4, place, place, peer)

        def az2_copy(c):
            return back(3, c, at_z2, eighth, self.z2n)

        def az1_copy(c):
            return back(4, c, at_z1, quarter, self.z1n)

        def ay_copy(c):
            return back(5, c, at_y, half, self.yn)

        def out_copy(c):
            return pltpu.make_async_copy(
                ob.at[c % OUT_SLOTS], self.out_ref.at[rows_at(c, CHUNK)], self.outs.at[c % 2]
            )

        def stage(lag, work):
            c, inside = in_runs(tick - lag, self.l_runs)

            @pl.when(inside)
            def _():
                work(c)

        def leave(c):
            out_copy(c).wait()

        def store(c):
            ay_copy(c).wait()
            out_copy(c).start()

        def go_ay(c):
            az1_copy(c).wait()
            ay_copy(c).start()

        def go_az1(c):
            az2_copy(c).wait()
            az1_copy(c).start()

        def go_az2(c):
            z2_copy(c).wait()
            ob[c % OUT_SLOTS, pl.ds(at_z2, eighth)] = vb[c % 2, rows_at(z1, eighth)] + self.rz2[c % 4]
            az2_copy(c).start()

        def go_z2(c):
            z1_copy(c).wait()
            vb[c % 2] = ub[c % 2, rows_at(z0, quarter)] + self.rz1[c % 4]
            z2_copy(c).start()

        def go_z1(c):
            y_copy(c).wait()
            ub[c % 2] = tb[c % 2, rows_at(yb, half)] + self.ry[c % 4]
            z1_copy(c).start()

        def go_y(c):
            for which in range(2):
                load(which, c).wait()
            tb[c % 2] = lp[c % 2, 0] + lp[c % 2, 1]
            y_copy(c).start()

        def go_load(c):
            self.x_copy(c).wait()
            for which in range(2):
                load(which, c).start()

        stage(14, leave)
        stage(13, store)
        stage(11, go_ay)
        stage(9, go_az1)
        stage(7, go_az2)
        stage(5, go_z2)
        stage(3, go_z1)
        stage(1, go_y)
        stage(0, go_load)
        c, inside = in_runs(tick, self.x_runs)

        @pl.when(inside)
        def _():
            self.x_copy(c).start()


N_RED = 21


def block_kernel(n, heads, tile, paired, *refs):
    refs = list(refs)

    def take(count):
        taken = refs[:count]
        del refs[:count]
        return taken

    tokens, upstream, item, ids, ids_row, mod, qkv_bias, b_out, b_up, b_down, act = take(11)
    own = take(3) if paired else None
    w_all = None if paired else take(1)[0]
    output_hbm, gtok_hbm, sums_ref, gb_down, gb_out, gb_up, gb_qv = take(7)
    normed_hbm, branch_hbm, qkv_hbm, att_hbm = take(4)
    if paired:
        (w_all,), shared = take(1), take(5)
    else:
        (g_all,) = take(1)
    n_buf, d_buf, acc_a, acc_b, up_buf, down_buf, w_buf, hid_buf, dpre_buf, stage_buf, r_buf = take(11)
    qkv_buf, att_buf, datt_buf, dproj_buf, fold_buf, sum_buf, b_buf, lse = take(8)
    up_sem, down_sem, n_sem, stage_sem, r_sem, w_sem, qkv_sem, att_sem, b_sem = take(9)
    ff = w_all.shape[2]
    pieces = pieces_of(ff)
    if paired:
        gather = Gather(units_of(ff, pieces), own, w_all, *take(4))
        red = Reduction(plan_of(ff, heads * HEAD, n), *take(4), *shared, *refs)
        red.greet()
        gather.begin()
        tick, gather_tick = red.tick, gather.tick
    else:

        def tick(t):
            pass

        gather_tick = tick

    rows, width = tokens.shape
    lw = heads * HEAD
    frames = rows // SLOT
    scale = HEAD ** (-0.5)
    tiles = rows // tile
    some, hh = 3 * lw // 2, heads // 2
    downs, ups, out_row, qkv_row = stream_of(ff, lw)
    fold_buf[...] = jnp.zeros_like(fold_buf)
    sum_buf[...] = jnp.zeros_like(sum_buf)
    gb_up[...] = jnp.zeros_like(gb_up)

    def landed(m, blocks):
        if not paired:
            return

        @pl.when(m % 2 == 0)
        def _():
            for slot, block in enumerate(blocks):
                if block is None:
                    continue
                flush, row, size = block
                stage = stage_buf.at[slot, pl.ds(0, size)]
                sent = red.to_sibling(m // 2, flush, stage, row, size)
                sent.wait()
                fetch(m // 2, slot, row, size).start()

    def fetch(which, slot, row, size):
        return pltpu.make_async_copy(
            red.d_in.at[which, pl.ds(row, size)], r_buf.at[slot, pl.ds(0, size)], r_sem.at[slot]
        )

    def put(target, slot, row, size):
        return pltpu.make_async_copy(
            stage_buf.at[slot, pl.ds(0, size)], target.at[pl.ds(row, size)], stage_sem.at[slot]
        )

    def settle(blocks):
        if paired:
            for slot, (flush, row, size) in enumerate(blocks):
                put(red.s_own, slot, row, size).wait()

    def leave(m, slot, block, value):
        flush, row, size = block
        if not paired:
            stage_buf[slot, pl.ds(0, size), :] = value.astype(bf16)
            copy = put(g_all.at[m], slot, row, size)
            copy.start()
            copy.wait()
            return

        @pl.when(m % 2 == 1)
        def _():
            stage_buf[slot, pl.ds(0, size), :] = value.astype(bf16)
            stage = stage_buf.at[slot, pl.ds(0, size)]
            red.to_sibling(m // 2, flush, stage, row, size).start()

        @pl.when(m % 2 == 0)
        def _():
            fetch(m // 2, slot, row, size).wait()
            total = value + r_buf[slot, pl.ds(0, size), :].astype(f32)
            stage_buf[slot, pl.ds(0, size), :] = total.astype(bf16)

            @pl.when(m == 0)
            def _():
                put(red.s_own, slot, row, size).start()

            @pl.when(m > 0)
            def _():
                put(red.s_far, slot, row, size).start()

    def w_copies(p, m, slot):
        at, size = pieces[p]
        here = pl.ds(at, size)
        up_part, down_part = up_buf.at[slot, :, pl.ds(0, size)], down_buf.at[slot, pl.ds(0, size), :]
        return (
            Shard(own, w_all, 1, m, (slice(None), here), up_part, up_sem.at[slot]),
            Shard(own, w_all, 2, m, (here, slice(None)), down_part, down_sem.at[slot]),
        )

    def f_copies(m):
        return [
            Shard(own, w_all, 0, m, pl.ds(half * some, some), w_buf.at[half], w_sem.at[half])
            for half in range(2)
        ] + [Shard(own, w_all, 0, m, pl.ds(3 * lw, lw), r_buf.at[m % 2, pl.ds(0, lw)], r_sem.at[m % 2])]

    def f_start(m):
        for copy in f_copies(m):
            copy.start()

    def qkv_out(m, half):
        return pltpu.make_async_copy(qkv_buf.at[half], qkv_hbm.at[m, half], qkv_sem.at[half])

    def att_out(m):
        return pltpu.make_async_copy(att_buf.at[m % 2], att_hbm.at[m], att_sem.at[m % 2])

    f_start(0)

    def normed_part(i, carry):
        gather_tick(i)

        def block(j, c):
            at = pl.ds(pl.multiple_of(i * SLOT + j * BLOCK, BLOCK), BLOCK)
            col = item[at, :]
            normed, _ = normal(tokens[at, :].astype(f32))
            n_buf[at, :] = (normed * (1.0 + pick(col, mod, 1)) + pick(col, mod, 0)).astype(bf16)
            acc_a[at, :] = jnp.broadcast_to(b_out[...], (BLOCK, width))
            return c

        lax.fori_loop(0, SLOT // BLOCK, block, 0, unroll=UNROLL)
        return carry

    lax.fori_loop(0, frames, normed_part, 0)
    normed_out = pltpu.make_async_copy(n_buf, normed_hbm, n_sem)
    normed_out.start()
    if paired:
        gather.near(0).wait()

    def upstream_part(i):
        def block(j, c):
            at = pl.ds(pl.multiple_of(i * SLOT + j * BLOCK, BLOCK), BLOCK)
            d = (pick(item[at, :], mod, 5) * upstream[at, :].astype(f32)).astype(bf16)
            d_buf[at, :] = d
            sum_buf[0] += fold(d.astype(f32))
            acc_b[at, :] = jnp.zeros((BLOCK, width), f32)
            return c

        lax.fori_loop(0, SLOT // BLOCK, block, 0, unroll=UNROLL)

    def attend_part(m, carry):
        for copy in f_copies(m):
            copy.wait()

        @pl.when(m >= 1)
        def _():
            for half in range(2):
                qkv_out(m - 1, half).wait()

        @pl.when(m >= 2)
        def _():
            att_out(m - 2).wait()

        for half in range(2):
            bias = jnp.transpose(jnp.broadcast_to(qkv_bias[m, half], (8, some)))[:, 0:1]
            proj = nt(w_buf[half], n_buf[...]) + bias
            for h in range(3 * hh):
                qkv_buf[half, h] = proj[h * HEAD : (h + 1) * HEAD].astype(bf16)
            qkv_out(m, half).start()

        if paired:

            @pl.when(m == 2)
            def _():
                gather_tick(frames * 3 + 3)

        @pl.when((m + 1 < n) & (m != 1) if paired else m + 1 < n)
        def _():
            f_start(m + 1)

        def frame(f, c):
            gather_tick(frames + m * frames + f + jnp.where(m > 1, EXTRA, 0))
            at = rows_at(f, SLOT)
            pairs = pair_bias(ids[at, :], ids_row[pl.ds(f, 1), :])
            heads_qkv = [
                [qkv_buf[h // hh, j * hh + h % hh, :, at] for j in range(3)] for h in range(heads)
            ]
            all_scores = [tn(k, q) * scale + pairs for q, k, _ in heads_qkv]
            all_weights = []
            for h, scores in enumerate(all_scores):
                peak = jnp.max(scores, axis=0, keepdims=True)
                weights = jnp.exp(scores - peak)
                total = jnp.sum(weights, axis=0, keepdims=True)
                lse[m, h : h + 1, at] = peak + jnp.log(total)
                all_weights.append((weights.astype(bf16), 1.0 / total))
            outs = [dot(v, w) * inverse for (_, _, v), (w, inverse) in zip(heads_qkv, all_weights)]
            att_buf[m % 2, :, at] = jnp.concatenate(outs, axis=0).astype(bf16)
            return c

        lax.fori_loop(0, frames, frame, 0)
        att_out(m).start()

        def branch(j, c):
            at = rows_at(j, tile)
            acc_a[at, :] += tn(att_buf[m % 2, :, at], r_buf[m % 2, pl.ds(0, lw), :])
            return c

        lax.fori_loop(0, tiles, branch, 0)
        @pl.when(m == 1)
        def _():
            def slot_part(i, c):
                if paired:

                    @pl.when(i % 2 == 0)
                    def _():
                        gather_tick(frames * 3 + i // 2)

                upstream_part(i)
                return c

            lax.fori_loop(0, frames, slot_part, 0)
            if paired:
                gather_tick(frames * 3 + 2)
                f_start(m + 1)

        return carry

    lax.fori_loop(0, n, attend_part, 0)
    if paired:
        gather.near(1).wait()
        gather.near(2).wait()
    for half in range(2):
        qkv_out(n - 1, half).wait()
    for m in range(max(n - 2, 0), n):
        att_out(m).wait()
    normed_out.wait()

    def b_copy(i):
        return pltpu.make_async_copy(branch_hbm.at[rows_at(i, SLOT)], b_buf.at[i % 2], b_sem.at[i % 2])

    def b_out_copy(i):
        return pltpu.make_async_copy(b_buf.at[i % 2], branch_hbm.at[rows_at(i, SLOT)], b_sem.at[i % 2])

    def first(i, carry):
        gather_tick(frames * (n + 1) + EXTRA + i)

        @pl.when(i >= 2)
        def _():
            b_out_copy(i - 2).wait()

        def block(j, c):
            at = pl.ds(pl.multiple_of(i * SLOT + j * BLOCK, BLOCK), BLOCK)
            col = item[at, :]
            branch = acc_a[at, :]
            b_buf[i % 2, rows_at(j, BLOCK), :] = branch
            middle = tokens[at, :].astype(f32) + pick(col, mod, 2) * branch
            normed, _ = normal(middle)
            n_buf[at, :] = (normed * (1.0 + pick(col, mod, 4)) + pick(col, mod, 3)).astype(bf16)
            acc_a[at, :] = jnp.broadcast_to(b_down[...], (BLOCK, width))
            return c

        @pl.when(i + 1 == frames)
        def _():
            for copy in w_copies(0, n - 1, 0):
                copy.start()

        lax.fori_loop(0, SLOT // BLOCK, block, 0, unroll=UNROLL)
        b_out_copy(i).start()
        return carry

    lax.fori_loop(0, frames, first, 0)
    for i in range(max(frames - 2, 0), frames):
        b_out_copy(i).wait()

    def by_slots(work, after):
        b_copy(0).start()

        def slot_part(i, carry):
            b_copy(i).wait()

            @pl.when(i + 1 < frames)
            def _():
                b_copy(i + 1).start()

            def block(j, c):
                work(i, pl.ds(pl.multiple_of(i * SLOT + j * BLOCK, BLOCK), BLOCK), rows_at(j, BLOCK))
                return c

            lax.fori_loop(0, SLOT // BLOCK, block, 0, unroll=UNROLL)
            after(i)
            return carry

        lax.fori_loop(0, frames, slot_part, 0)

    def blocks_of(p):
        size = pieces[p][1]
        return ((2 * p, downs[p], size), (2 * p + 1, ups[p], size))

    now = 0
    for p, (p_at, p_size) in enumerate(pieces):
        def shard(i, carry, p=p, p_at=p_at, p_size=p_size, now=now):
            m = n - 1 - i
            slot = (p * n + i) % 2
            for copy in w_copies(p, m, slot):
                copy.wait()

            @pl.when(i + 1 < n)
            def _():
                for copy in w_copies(p, m - 1, 1 - slot):
                    copy.start()

            if p + 1 < len(pieces):

                @pl.when(i + 1 == n)
                def _():
                    for copy in w_copies(p + 1, n - 1, 1 - slot):
                        copy.start()

            blocks = blocks_of(p)
            bias = b_up[m, :, pl.ds(p_at, p_size)]
            up = up_buf.at[slot, :, pl.ds(0, p_size)]
            down = down_buf.at[slot, pl.ds(0, p_size), :]

            def part(j, c):
                at = rows_at(j, tile)
                pre = jnp.dot(n_buf[at, :], up[...], preferred_element_type=f32) + bias
                hidden, slope = gelu_both(pre)
                hidden = hidden.astype(bf16)
                dpre = nt(d_buf[at, :], down[...]) * slope
                dpre = dpre.astype(bf16)
                hid_buf[at, pl.ds(0, p_size)] = hidden
                dpre_buf[at, pl.ds(0, p_size)] = dpre
                gb_up[m, :, pl.ds(p_at, p_size)] += jnp.sum(
                    dpre.astype(f32), axis=0, keepdims=True
                )
                acc_a[at, :] += jnp.dot(hidden, down[...], preferred_element_type=f32)
                acc_b[at, :] += nt(dpre, up[...])
                return c

            lax.fori_loop(0, tiles, part, 0)

            @pl.when(i == 2)
            def _():
                settle(blocks)

            if p:

                @pl.when(i == 0)
                def _():
                    settle(blocks_of(p - 1))

            if p < 2:
                gather_tick(frames * (n + 2) + EXTRA + now + i)
            tick(now + STEP_TICKS[p] * i)
            landed(m, blocks)
            leave(m, 0, blocks[0], tn(hid_buf[:, pl.ds(0, p_size)], d_buf[...]))
            leave(m, 1, blocks[1], tn(dpre_buf[:, pl.ds(0, p_size)], n_buf[...]))
            if STEP_TICKS[p] > 1:
                tick(now + STEP_TICKS[p] * i + 1)
            return carry

        lax.fori_loop(0, n, shard, 0)
        now += n * STEP_TICKS[p]
    settle(blocks_of(len(pieces) - 1))

    def out_copies(m, slot):
        there = pl.ds(3 * lw, lw)
        return (
            Shard(own, w_all, 0, m, there, w_buf.at[slot, pl.ds(0, lw)], w_sem.at[slot]),
            pltpu.make_async_copy(att_hbm.at[m], att_buf.at[slot], att_sem.at[slot]),
        )

    def a_copies(half, m, slot):
        there = pl.ds(half * some, some)
        return (
            Shard(own, w_all, 0, m, there, w_buf.at[slot], w_sem.at[slot]),
            pltpu.make_async_copy(qkv_hbm.at[m, half], qkv_buf.at[slot], qkv_sem.at[slot]),
        )

    normed_copy = pltpu.make_async_copy(normed_hbm, n_buf, n_sem)
    normed_copy.start()
    for copy in out_copies(n - 1, 0):
        copy.start()

    def row_copy(target, i):
        return pltpu.make_async_copy(
            stage_buf.at[i % 2, pl.ds(0, SLOT)], target.at[rows_at(i, SLOT)], stage_sem.at[i % 2]
        )

    def rows_done(target):
        for i in range(max(frames - 2, 0), frames):
            row_copy(target, i).wait()

    def middle_part(i, at, here):
        col = item[at, :]
        gate = pick(col, mod, 2)
        branch = b_buf[i % 2, here, :]
        middle = tokens[at, :].astype(f32) + gate * branch
        dy = upstream[at, :].astype(f32)
        second = acc_a[at, :]
        stage_buf[i % 2, here, :] = (middle + pick(col, mod, 5) * second).astype(bf16)
        add_by_item(fold_buf, 5, col, dy * second)
        grad = acc_b[at, :]
        normed, rstd = normal(middle)
        add_by_item(fold_buf, 3, col, grad)
        add_by_item(fold_buf, 4, col, grad * normed)
        dmiddle = dy + normal_back(grad, pick(col, mod, 4), normed, rstd)
        acc_a[at, :] = dmiddle
        add_by_item(fold_buf, 2, col, dmiddle * branch)
        d = (gate * dmiddle).astype(bf16)
        d_buf[at, :] = d
        sum_buf[1] += fold(d.astype(f32))
        acc_b[at, :] = jnp.zeros((BLOCK, width), f32)

    def middle_done(i):
        row_copy(output_hbm, i).start()

        @pl.when((i >= 1) & (i + 1 < frames))
        def _():
            row_copy(output_hbm, i - 1).wait()

        if MID_TICKS == 4:
            tick(now + i)
        else:

            @pl.when(i % 2 == 1)
            def _():
                tick(now + i // 2)

    by_slots(middle_part, middle_done)
    rows_done(output_hbm)
    now += MID_TICKS
    normed_copy.wait()
    out_block = (2 * len(pieces), out_row, lw)

    def out_part(i, carry):
        m = n - 1 - i
        slot = i % 2
        for copy in out_copies(m, slot):
            copy.wait()

        @pl.when(i + 1 < n)
        def _():
            for copy in out_copies(m - 1, 1 - slot):
                copy.start()

        @pl.when(i == 2)
        def _():
            settle((out_block,))

        landed(m, (out_block,))
        leave(m, 0, out_block, dot(att_buf[slot], d_buf[...]))
        datt = nt(w_buf[slot, pl.ds(0, lw), :], d_buf[...])
        for h in range(heads):
            datt_buf[m, h] = datt[h * HEAD : (h + 1) * HEAD].astype(bf16)

        if OUT_TICKS == 4:
            tick(now + i)
        else:

            @pl.when(i % 2 == 1)
            def _():
                tick(now + i // 2)

        return carry

    lax.fori_loop(0, n, out_part, 0)
    settle((out_block,))
    now += OUT_TICKS
    for copy in a_copies(0, n - 1, 0):
        copy.start()

    def qkv_block(half):
        return (2 * len(pieces) + 1 + half, qkv_row + half * some, some)

    for half in range(2):

        def attn(i, carry, half=half, now=now):
            m = n - 1 - i
            slot = i % 2
            for copy in a_copies(half, m, slot):
                copy.wait()

            @pl.when(i + 1 < n)
            def _():
                for copy in a_copies(half, m - 1, 1 - slot):
                    copy.start()

            if half == 0:

                @pl.when(i + 1 == n)
                def _():
                    for copy in a_copies(1, n - 1, 1 - slot):
                        copy.start()

            def frame(f, c):
                at = rows_at(f, SLOT)
                pairs = pair_bias(ids[at, :], ids_row[pl.ds(f, 1), :])
                each = range(hh)
                q, k, v = ([qkv_buf[slot, j * hh + h, :, at] for h in each] for j in range(3))
                d = [datt_buf[m, half * hh + h, :, at] for h in each]
                lses = [lse[m, half * hh + h : half * hh + h + 1, at] for h in each]
                scores = [tn(k[h], q[h]) * scale + pairs for h in each]
                probs = [jnp.exp(scores[h] - lses[h]) for h in each]
                dprobs = [tn(v[h], d[h]) for h in each]
                low, dscores = [], []
                for h in each:
                    inner = jnp.sum(dprobs[h] * probs[h], axis=0, keepdims=True)
                    low.append(probs[h].astype(bf16))
                    dscores.append((probs[h] * (dprobs[h] - inner)).astype(bf16))
                dvs = [nt(d[h], low[h]) for h in each]
                dqs = [dot(k[h], dscores[h]) * scale for h in each]
                dks = [nt(q[h], dscores[h]) * scale for h in each]
                dproj_buf[:, at] = jnp.concatenate(dqs + dks + dvs, axis=0).astype(bf16)
                return c

            lax.fori_loop(0, frames, frame, 0)

            @pl.when(i == 2)
            def _():
                settle((qkv_block(half),))

            if half == 1:

                @pl.when(i == 0)
                def _():
                    settle((qkv_block(0),))

            tick(now + ATTN_TICKS * i)
            landed(m, (qkv_block(half),))
            gb_qv[m, half] = nt(jnp.ones((8, rows), bf16), dproj_buf[...])[0:1]
            leave(m, 0, qkv_block(half), dot(dproj_buf[...], n_buf[...]))

            def part(j, c):
                at = rows_at(j, tile)
                acc_b[at, :] += tn(dproj_buf[:, at], w_buf[slot, pl.ds(0, some), :])
                return c

            lax.fori_loop(0, tiles, part, 0)
            if ATTN_TICKS > 1:
                tick(now + ATTN_TICKS * i + 1)
            return carry

        lax.fori_loop(0, n, attn, 0)
        now += n * ATTN_TICKS
    settle((qkv_block(1),))

    def last(i, carry):
        def block(j, c):
            at = pl.ds(pl.multiple_of(i * SLOT + j * BLOCK, BLOCK), BLOCK)
            col = item[at, :]
            normed, rstd = normal(tokens[at, :].astype(f32))
            grad = acc_b[at, :]
            add_by_item(fold_buf, 0, col, grad)
            add_by_item(fold_buf, 1, col, grad * normed)
            value = acc_a[at, :] + normal_back(grad, pick(col, mod, 1), normed, rstd)
            stage_buf[i % 2, rows_at(j, BLOCK), :] = value.astype(bf16)
            return c

        lax.fori_loop(0, SLOT // BLOCK, block, 0, unroll=UNROLL)
        row_copy(gtok_hbm, i).start()

        @pl.when((i >= 1) & (i + 1 < frames))
        def _():
            row_copy(gtok_hbm, i - 1).wait()

        tick(now + i)
        return carry

    lax.fori_loop(0, frames, last, 0)
    rows_done(gtok_hbm)
    for j in range(sums_ref.shape[0]):
        for k in range(6):
            sums_ref[j, k : k + 1, :] = jnp.sum(fold_buf[j, k], axis=0, keepdims=True)
    gb_down[...] = jnp.sum(sum_buf[0], axis=0, keepdims=True)
    gb_out[...] = jnp.sum(sum_buf[1], axis=0, keepdims=True)
    if paired:
        dp, mp = lax.axis_index("dp"), lax.axis_index("mp")
        items = sums_ref.shape[0]
        total_items = lax.axis_size("dp") * items
        core, xb = mp % 2, mp // 2
        acc_b[pl.ds(0, n * TAIL), :] = jnp.zeros((n * TAIL, width), f32)

        def line(a, row, at=0, size=width):
            return acc_b.at[pl.ds(a * TAIL + row, 1), pl.ds(at, size)]

        for a in range(n):
            for j in range(items):
                for k in range(6):
                    row = dp * items + j + k // 4 * total_items
                    line(a, row, k % 4 * lw, lw)[...] = sums_ref[j, k : k + 1, a * lw : (a + 1) * lw]
                line(a, 2 * total_items + dp * items + j)[...] = jnp.where(mp == 0, act[j : j + 1, :], 0.0)
        for m in range(n):
            here = (xb if m < 2 else 1 - xb) * 2 + (core if m % 2 == 0 else 1 - core)
            for k, values in enumerate((gb_out, gb_down, gb_up.at[m])):
                for j in range(4):
                    line(here, total_items + 4 * k + j, 2 * lw, lw)[...] = values[:, j * lw : (j + 1) * lw]
            for j in range(2):
                for half in range(2):
                    place = line(here, total_items + 12 + j, 2 * lw + half * lw // 2, lw // 2)
                    place[...] = gb_qv[m, half, :, j * lw : j * lw + lw // 2]
            red.t_buf[m] = acc_b[pl.ds(pl.multiple_of(here * TAIL, TAIL), TAIL), :].astype(bf16)

        start, end = now + LAST_TICKS, red.last_tick + 1
        bounds = [start + (end - start) * step // 5 for step in range(6)]

        def drain(t, carry):
            tick(t)
            return carry

        def between(step):
            lax.fori_loop(bounds[step], bounds[step + 1], drain, 0)

        red.tail(between)
        tail_out = pltpu.make_async_copy(
            red.t_buf.at[0], red.out_ref.at[pl.ds(2 * ff + 4 * lw, TAIL)], n_sem
        )
        tail_out.start()
        tail_out.wait()


def block(tokens, upstream, item, ids, mod, qkv_bias, b_out, b_up, b_down, act, weights, paired):
    rows, width = tokens.shape
    n, ff = b_up.shape[0], b_up.shape[2]
    heads = 4
    lw = heads * HEAD
    pieces = pieces_of(ff)
    widest = max(size for _, size in pieces)
    tile = min(512, rows)
    total = 2 * ff + 4 * lw
    deep = max(widest, 3 * lw // 2, SLOT)
    slots = 2
    flushes = 2 * len(pieces) + 3
    half, quarter, eighth = CHUNK // 2, CHUNK // 4, CHUNK // 8
    vmem = pl.BlockSpec(memory_space=pltpu.VMEM)
    hbm = pl.BlockSpec(memory_space=pl.ANY)
    dma = pltpu.SemaphoreType.DMA

    def low(*shape):
        return jax.ShapeDtypeStruct(shape, bf16)

    def full(*shape):
        return jax.ShapeDtypeStruct(shape, f32)

    def buf(*shape):
        return pltpu.VMEM(shape, bf16)

    grads = [low(n, total, width)]
    extra = []
    if paired:
        grads = [low(3, n - 1, ff, width), low(2, total, width)] + [low(total, width)] * 3
        grads.append(low(total + TAIL, width))
        extra = [
            dma((5, 8, 4)),
            dma((5, 8, 4)),
            dma((3,)),
            dma((3,)),
            buf(n, TAIL, width),
            buf(6, TAIL, width),
            dma((6,)),
            dma((6,)),
            buf(2, 2, CHUNK, width),
            buf(2, CHUNK, width),
            buf(4, half, width),
            buf(2, half, width),
            buf(4, quarter, width),
            buf(2, quarter, width),
            buf(4, eighth, width),
            buf(OUT_SLOTS, CHUNK, width),
            dma((2, flushes)),
            dma((2, flushes)),
            dma((total // CHUNK,)),
            dma((total // CHUNK,)),
            dma((2, 2)),
            dma((6, 4)),
            dma((6, 4)),
            dma((2,)),
        ]
    return pl.pallas_call(
        functools.partial(block_kernel, n, heads, tile, paired),
        out_shape=(
            low(rows, width),
            low(rows, width),
            jax.ShapeDtypeStruct(mod.shape, f32),
            full(1, width),
            full(1, width),
            full(n, 1, ff),
            full(n, 2, 1, 3 * lw // 2),
            low(rows, width),
            full(rows, width),
            low(n, 2, 3 * heads // 2, HEAD, rows),
            low(n, lw, rows),
            *grads,
        ),
        in_specs=[vmem] * 11 + [hbm] * len(weights),
        out_specs=(hbm,) * 2 + (vmem,) * 5 + (hbm,) * (4 + len(grads)),
        scratch_shapes=[
            buf(rows, width),
            buf(rows, width),
            pltpu.VMEM((rows, width), f32),
            pltpu.VMEM((rows, width), f32),
            buf(2, width, widest),
            buf(2, widest, width),
            buf(2, 3 * lw // 2, width),
            buf(rows, widest),
            buf(rows, widest),
            buf(slots, deep, width),
            buf(slots, deep, width),
            buf(2, 3 * heads // 2, HEAD, rows),
            buf(2, lw, rows),
            buf(n, heads, HEAD, rows),
            buf(3 * lw // 2, rows),
            pltpu.VMEM((mod.shape[0], 6, 8, width), f32),
            pltpu.VMEM((2, 8, width), f32),
            pltpu.VMEM((2, SLOT, width), f32),
            pltpu.VMEM((n, heads, rows), f32),
            dma((2,)),
            dma((2,)),
            dma,
            dma((slots,)),
            dma((slots,)),
            dma((2,)),
            dma((2,)),
            dma((2,)),
            dma((2,)),
            *extra,
        ],
        compiler_params=pltpu.CompilerParams(
            collective_id=0 if paired else None, has_side_effects=paired, vmem_limit_bytes=63 << 20
        ),
    )(
        tokens, upstream, item[:, None], ids[:, None], ids.reshape(-1, SLOT), mod,
        qkv_bias.reshape(n, 2, 1, 3 * lw // 2), b_out, b_up, b_down, act, *weights,
    )


def finish_kernel(ff, lw, total_items, columns, downs, outs, tail, up_out, down_out, qkv_out, out_out, ada_out, bias_out, qv_out, bada_out):
    size = columns.shape[1]
    _, ups, out_row, qkv_row = stream_of(ff, lw)
    up = jnp.concatenate([columns[at : at + n, :] for at, (_, n) in zip(ups, pieces_of(ff))], axis=0)
    up_out[...] = jnp.transpose(up.astype(f32))
    down_out[...] = downs[...].astype(f32)
    out_out[...] = outs[...].astype(f32)
    half = lw // 2
    for j in range(3):
        rows = [columns[qkv_row + h * 3 * half + j * half : qkv_row + h * 3 * half + (j + 1) * half, :] for h in range(2)]
        qkv_out[j] = jnp.concatenate(rows, axis=0).astype(f32)
    tail_row = 2 * ff + 4 * lw
    act = columns[tail_row + 2 * total_items : tail_row + 3 * total_items, :]
    for k in range(6):
        first = k // 4 * total_items
        dmod = tail[first : first + total_items, k % 4 * lw : (k % 4 + 1) * lw]
        ada_out[k] = tn(dmod, act)
        bada_out[k : k + 1, :] = jnp.sum(dmod.astype(f32), axis=0, keepdims=True)
    more = tail[total_items : 2 * total_items, 2 * lw : 3 * lw].astype(f32)
    for k in range(3):
        for j in range(4):
            bias_out[k : k + 1, j * lw : (j + 1) * lw] = more[4 * k + j : 4 * k + j + 1]
    qv_out[...] = more[12:14]


def finish(total, ff, lw, total_items):
    width = total.shape[1]
    size = 128
    steps = width // size
    piece, last = pieces_of(ff)[0][1] // size, len(pieces_of(ff)) - 1
    out_rows = lw // steps

    def down_place(i):
        return (i + piece * jnp.minimum(i // piece, last), 0)

    def full(*shape):
        return jax.ShapeDtypeStruct(shape, f32)

    return pl.pallas_call(
        functools.partial(finish_kernel, ff, lw, total_items),
        grid=(steps,),
        out_shape=(
            full(width, ff),
            full(ff, width),
            full(3, lw, width),
            full(lw, width),
            full(6, lw, width),
            full(3, width),
            full(2, lw),
            full(6, lw),
        ),
        in_specs=[
            pl.BlockSpec((total.shape[0], size), lambda i: (0, i)),
            pl.BlockSpec((size, width), down_place),
            pl.BlockSpec((out_rows, width), lambda i: (2 * ff // out_rows + i, 0)),
            pl.BlockSpec((TAIL, width), lambda i: ((2 * ff + 4 * lw) // TAIL, 0)),
        ],
        out_specs=(
            pl.BlockSpec((size, ff), lambda i: (i, 0)),
            pl.BlockSpec((size, width), lambda i: (i, 0)),
            pl.BlockSpec((3, lw, size), lambda i: (0, 0, i)),
            pl.BlockSpec((out_rows, width), lambda i: (i, 0)),
            pl.BlockSpec((6, lw, size), lambda i: (0, 0, i)),
            pl.BlockSpec((3, width), lambda i: (0, 0)),
            pl.BlockSpec((2, lw), lambda i: (0, 0)),
            pl.BlockSpec((6, lw), lambda i: (0, 0)),
        ),
        compiler_params=pltpu.CompilerParams(vmem_limit_bytes=32 << 20),
        cost_estimate=pl.CostEstimate(flops=10**8, bytes_accessed=5 * 10**7, transcendentals=0),
    )(total, total, total, total)


def by_halves(rows):
    halves = rows.reshape(3, 2, -1, *rows.shape[1:])
    return jnp.swapaxes(halves, 0, 1).reshape(rows.shape)


def from_halves(rows):
    halves = rows.reshape(2, 3, -1, *rows.shape[1:])
    return jnp.swapaxes(halves, 0, 1).reshape(rows.shape)


def swap(values, axis, bit):
    n = lax.axis_size(axis)
    return lax.ppermute(values, axis, [(i, i ^ bit) for i in range(n)])


def shards(
    paired,
    tokens,
    condition,
    grid_rows,
    grid_cols,
    frame_start,
    frame_item,
    group_frames,
    w_qkv,
    qv_bias,
    w_out,
    b_out,
    w_up,
    b_up,
    w_down,
    b_down,
    w_ada,
    b_ada,
    cotangent,
):
    own_rows, width = tokens.shape
    local_width = w_qkv.shape[2]
    local_ff = w_up.shape[1]
    items = condition.shape[0]
    n_mp, n_dp = lax.axis_size("mp"), lax.axis_size("dp")
    mp, dp = lax.axis_index("mp"), lax.axis_index("dp")
    n = width // (4 * HEAD)
    lw, ff = width // n, local_ff * n_mp // n
    frame_id, item_id = frame_tables(
        grid_rows, grid_cols, frame_start, frame_item, group_frames[0], mp * own_rows, own_rows
    )
    cond_value = condition.astype(f32)
    act_low = jax.nn.silu(cond_value).astype(bf16)
    ada_flat = w_ada.reshape(width, -1)
    ada_local = dot(act_low, ada_flat) + b_ada.reshape(-1).astype(f32)
    ada_local = ada_local.reshape(items, 6, local_width)
    qkv_local = w_qkv.transpose(1, 2, 0)
    if paired:
        qkv_bias = jnp.concatenate(
            [qv_bias[0].astype(f32), jnp.zeros((lw,), f32), qv_bias[1].astype(f32)]
        )
        small = jnp.concatenate([ada_local.reshape(-1), by_halves(qkv_bias), b_up.astype(f32)])
        small = jnp.stack([small] + [swap(small, "mp", bit) for bit in range(1, n)])
        sorted_small = jnp.where(mp % 2 == 0, small, small[jnp.array([1, 0, 3, 2])])
        sorted_small = jnp.where(mp < 2, sorted_small, sorted_small[jnp.array([2, 3, 0, 1])])
        n_ada = ada_local.size
        modulation = sorted_small[:, :n_ada].reshape(n, items, 6, lw)
        qkv_bias = small[:, n_ada : n_ada + 3 * lw]
        up_bias = small[:, n_ada + 3 * lw :]
        weights = [
            jnp.concatenate([by_halves(qkv_local.reshape(3 * lw, width)), w_out], axis=0),
            w_up,
            w_down,
        ]
    else:
        modulation = lax.all_gather(ada_local, "mp", axis=0)
        qv = lax.all_gather(qv_bias.astype(f32), "mp", axis=1, tiled=True)
        qkv_bias = jnp.stack([qv[0], jnp.zeros((width,), f32), qv[1]])
        qkv_bias = jax.vmap(by_halves)(qkv_bias.reshape(3, n, lw).transpose(1, 0, 2).reshape(n, 3 * lw))
        up_bias = lax.all_gather(b_up.astype(f32), "mp", axis=0, tiled=True).reshape(n, ff)
        qkv = lax.all_gather(qkv_local, "mp", axis=1, tiled=True)
        qkv = qkv.reshape(3, n, lw, width).transpose(1, 0, 2, 3).reshape(n, 3 * lw, width)
        qkv = jax.vmap(by_halves)(qkv)
        out = lax.all_gather(w_out, "mp", axis=0, tiled=True).reshape(n, lw, width)
        up = lax.all_gather(w_up, "mp", axis=1, tiled=True)
        up = up.reshape(width, n, ff).transpose(1, 0, 2)
        down = lax.all_gather(w_down, "mp", axis=0, tiled=True).reshape(n, ff, width)
        weights = [jnp.stack([jnp.concatenate([qkv, out], axis=1), up, down])]
    modulation = modulation.transpose(1, 2, 0, 3).reshape(items, 6, width)
    b_out_row, b_down_row = (b.astype(f32)[None] for b in (b_out, b_down))
    output, grad_tokens, item_grad, gb_down, gb_out, gb_up, gb_qv, *rest = block(
        tokens,
        cotangent,
        item_id,
        frame_id,
        modulation,
        qkv_bias,
        b_out_row,
        up_bias[:, None],
        b_down_row,
        act_low.astype(f32),
        weights,
        paired,
    )
    if paired:
        total = rest[-1]
        total_items = items * n_dp
        g_up, g_down, g_qkv, g_out, grad_w_ada, biases, gb_qv, grad_b_ada = finish(
            total, ff, lw, total_items
        )
        g_qkv, grad_w_ada = g_qkv.transpose(2, 0, 1), grad_w_ada.transpose(2, 0, 1)
        gb_out, gb_down, gb_up = biases
        tail = lax.dynamic_slice_in_dim(total[2 * ff + 4 * lw :], dp * items, total_items + items)
        own_dmod = jnp.concatenate([tail[:items], tail[-items:, : 2 * lw]], axis=1).astype(f32)
    else:

        gb_qv = jax.vmap(from_halves)(gb_qv.reshape(n, 3 * lw)).reshape(n, 3, lw)[:, ::2]

        def over_all(values, axis):
            part = lax.psum_scatter(values, "mp", scatter_dimension=axis, tiled=True)
            return lax.psum(part.astype(bf16), "dp").astype(f32)

        own_dmod = lax.psum_scatter(item_grad, "mp", scatter_dimension=2, tiled=True)
        dmod = lax.all_gather(own_dmod, "dp", axis=0, tiled=True)
        act_all = lax.all_gather(act_low, "dp", axis=0, tiled=True).astype(f32)
        g_down, g_up, g_out, g_qkv = jax.vmap(lambda g: split_stream(g, ff, lw))(rest[-1])
        g_down = over_all(g_down.reshape(n * ff, width), 0)
        g_up = over_all(g_up.reshape(n * ff, width).T, 1)
        g_qkv = g_qkv.reshape(n, 3, lw, width).transpose(3, 1, 0, 2).reshape(width, 3, width)
        g_qkv = over_all(g_qkv, 2)
        g_out = over_all(g_out.reshape(width, width), 0)
        gb_up = over_all(gb_up.reshape(-1), 0)
        gb_qv = over_all(gb_qv.transpose(1, 0, 2).reshape(2, width), 1)
        gb_out = lax.psum(gb_out[0], ("dp", "mp"))
        gb_down = lax.psum(gb_down[0], ("dp", "mp"))
        grad_w_ada = lax.dot_general(
            act_all,
            dmod.reshape(dmod.shape[0], -1),
            (((0,), (0,)), ((), ())),
            precision=lax.Precision.HIGHEST,
        ).reshape(width, 6, local_width)
        grad_b_ada = jnp.sum(dmod, axis=0)
    cond_term = lax.dot_general(
        own_dmod.reshape(items, -1),
        ada_flat.astype(f32),
        (((1,), (1,)), ((), ())),
        precision=lax.Precision.HIGHEST,
    )
    if paired:
        cond_term = cond_term + swap(cond_term, "mp", 1)
        cond_term = cond_term + swap(cond_term, "mp", 2)
    else:
        cond_term = lax.psum(cond_term, "mp")
    grad_condition = jax.vjp(jax.nn.silu, cond_value)[1](cond_term)[0]
    return (
        output,
        grad_tokens,
        grad_condition,
        g_qkv,
        gb_qv,
        g_out,
        gb_out,
        g_up,
        gb_up,
        g_down,
        gb_down,
        grad_w_ada,
        grad_b_ada,
    )


def solution(mesh):
    paired = dict(mesh.shape) == {"dp": 8, "mp": 4}
    return jax.shard_map(
        functools.partial(shards, paired),
        mesh=mesh,
        in_specs=(
            P(("dp", "mp"), None),
            P("dp", None),
            P("dp"),
            P("dp"),
            P("dp"),
            P("dp"),
            P("dp"),
            P(None, None, "mp"),
            P(None, "mp"),
            P("mp", None),
            P(),
            P(None, "mp"),
            P("mp"),
            P("mp", None),
            P(),
            P(None, None, "mp"),
            P(None, "mp"),
            P(("dp", "mp"), None),
        ),
        out_specs=(
            P(("dp", "mp"), None),
            P(("dp", "mp"), None),
            P("dp", None),
            P(None, None, "mp"),
            P(None, "mp"),
            P("mp", None),
            P(),
            P(None, "mp"),
            P("mp"),
            P("mp", None),
            P(),
            P(None, None, "mp"),
            P(None, "mp"),
        ),
        check_vma=False,
    )
```

```python
import functools

import jax
import jax.numpy as jnp
from jax import lax
from jax.experimental import pallas as pl
from jax.experimental.pallas import tpu as pltpu
from jax.sharding import PartitionSpec as P

HEAD = 72
SLOT = 256
CHUNK = 128
BLOCK = 128
UNROLL = 1
OUT_SLOTS = 10
TAIL = 48
MESH = pl.DeviceIdType.MESH
epsilon = 1e-06
f32 = jnp.float32
bf16 = jnp.bfloat16


def frame_tables(grid_rows, grid_cols, frame_start, frame_item, used, first, length):
    rows = first + jnp.arange(length, dtype=jnp.int32)[:, None]
    slots = jnp.arange(grid_rows.shape[0], dtype=jnp.int32)[None, :]
    ends = (frame_start + grid_rows * grid_cols)[None, :]
    inside = (rows >= frame_start[None, :]) & (rows < ends) & (slots < used)
    frame_id = jnp.sum(jnp.where(inside, slots + 1, 0), axis=1) - 1
    item_id = jnp.sum(jnp.where(inside, frame_item[None, :], 0), axis=1)
    return (frame_id, item_id)


def normal(values):
    centred = values - jnp.mean(values, axis=-1, keepdims=True)
    rstd = lax.rsqrt(jnp.mean(centred * centred, axis=-1, keepdims=True) + epsilon)
    return centred * rstd, rstd


def normal_back(grad, scale, normed, rstd):
    u = grad * (1.0 + scale)
    return rstd * (
        u
        - jnp.mean(u, axis=-1, keepdims=True)
        - normed * jnp.mean(u * normed, axis=-1, keepdims=True)
    )


def dot(left, right):
    return jnp.dot(left, right, preferred_element_type=f32)


def rows_at(i, size):
    return pl.ds(pl.multiple_of(i * size, size), size)


def pick(item_col, mod_ref, k):
    total = mod_ref[0, k : k + 1, :]
    for item in range(1, mod_ref.shape[0]):
        total = jnp.where(item_col == item, mod_ref[item, k : k + 1, :], total)
    return total


def fold(values):
    return jnp.sum(values.reshape(-1, 8, values.shape[-1]), axis=0)


def add_by_item(sums_ref, k, item_col, values):
    for item in range(sums_ref.shape[0]):
        sums_ref[item, k] += fold(jnp.where(item_col == item, values, 0.0))


def tn(left, right):
    return lax.dot_general(left, right, (((0,), (0,)), ((), ())), preferred_element_type=f32)


def nt(left, right):
    return lax.dot_general(left, right, (((1,), (1,)), ((), ())), preferred_element_type=f32)


class Shard:
    def __init__(self, own, others, a, m, part, target, sem):
        self.own, self.others, self.a, self.m, self.part = own, others, a, m, part
        self.target, self.sem = target, sem

    def copy(self, source):
        return pltpu.make_async_copy(source.at[self.part], self.target, self.sem)

    def start(self):
        if self.own is None:
            self.copy(self.others.at[self.a, self.m]).start()
            return

        @pl.when(self.m == 0)
        def _():
            self.copy(self.own[self.a]).start()

        @pl.when(self.m > 0)
        def _():
            self.copy(self.others.at[self.a, self.m - 1]).start()

    def wait(self):
        source = self.others.at[self.a, 0] if self.own is None else self.own[self.a]
        self.copy(source).wait()


def pair_bias(id_col, id_row):
    shape = (SLOT, SLOT)
    one = lax.broadcasted_iota(jnp.int32, shape, 0) == lax.broadcasted_iota(jnp.int32, shape, 1)
    same = (id_col == id_row) & (id_col >= 0)
    return jnp.where(same | one, 0.0, -1e30)


EXTRA = 4


class Units:
    def __init__(self, a, parts, ticks, place):
        self.a, self.parts, self.place, self.count = a, parts, place, len(ticks)
        self.runs = [[(unit[k], c, 1) for c, unit in enumerate(ticks)] for k in range(4)]


def units_of(depth, pieces):
    attn = depth // 4
    (_, wide), (last_at, last) = pieces[0], pieces[-1]

    def rows(first, part):
        return lambda c, at, size: (pl.ds(pl.multiple_of(first(c) + at * part, part), size * part), slice(None))

    def columns(first, width):
        return lambda c, at, size: (
            pl.ds(pl.multiple_of(at * (depth // 9), depth // 9), size * (depth // 9)),
            pl.ds(pl.multiple_of(first(c), 128), width),
        )

    return (
        Units(0, 9, ((4, 7, 8, 10), (8, 11, 12, 13), (10, 12, 13, 14), (12, 13, 14, 15)), rows(lambda c: c * attn, attn // 9)),
        Units(1, 9, ((16, 20, 23, 26), (19, 22, 25, 28), (24, 26, 28, 30)), columns(lambda c: c * wide, wide)),
        Units(2, 8, ((17, 21, 24, 27), (20, 24, 26, 29), (26, 28, 29, 31)), rows(lambda c: c * wide, wide // 8)),
        Units(1, 9, ((29, 30, 31, 32),), columns(lambda c: last_at, last)),
        Units(2, 8, ((30, 31, 32, 33),), rows(lambda c: last_at, last // 8)),
    )


class Gather:
    def __init__(self, units, own, w_all, sends, recvs, near_send, near_recv):
        self.units, self.own, self.w_all = units, own, w_all
        self.sends, self.recvs, self.near_send, self.near_recv = sends, recvs, near_send, near_recv
        dp, mp = lax.axis_index("dp"), lax.axis_index("mp")
        core, yb = mp % 2, dp % 2
        xb, z0 = mp // 2, (dp // 2) % 2
        self.sib = (dp, mp + 1 - 2 * core)
        self.xn = (dp, mp + 2 - 4 * xb)
        self.yn = (dp + 1 - 2 * yb, mp)
        self.zn = (dp + 2 - 4 * z0, mp)
        self.by_z, self.by_y = z0 * 2 + yb, 4 + yb * 2 + z0
        self.pair_z, self.pair_y = z0 * 2, 4 + yb * 2

    def near(self, a):
        return pltpu.make_async_remote_copy(
            src_ref=self.own[a],
            dst_ref=self.w_all.at[a, 0],
            send_sem=self.near_send.at[a],
            recv_sem=self.near_recv.at[a],
            device_id=self.sib,
            device_id_type=MESH,
        )

    def begin(self):
        self.near(0).start()
        for g, c in ((0, 0), (0, 1), (0, 2), (0, 3), (1, 0), (2, 0), (1, 1), (2, 1), (1, 2), (2, 2), (3, 0), (4, 0)):
            for copy in self.steps(g)[0](c):
                copy.start()
        self.near(1).start()
        self.near(2).start()

    def tick(self, tick):
        for g, units in enumerate(self.units):
            steps = self.steps(g)
            for k in (4, 3, 2, 1):
                c, inside = in_runs(tick, units.runs[k - 1])

                @pl.when(inside)
                def _(c=c, k=k, steps=steps):
                    for copy in steps[k - 1](c):
                        copy.wait()
                    if k < 4:
                        for copy in steps[k](c):
                            copy.start()

    def steps(self, g):
        units = self.units[g]
        own, far, both = self.own[units.a], self.w_all.at[units.a, 1], self.w_all.at[units.a, 2]

        def remote(step, c, src, dst, at, size, peer):
            place = units.place(c, at, size)
            return pltpu.make_async_remote_copy(
                src_ref=src.at[place],
                dst_ref=dst.at[place],
                send_sem=self.sends.at[g, step, c % 4],
                recv_sem=self.recvs.at[g, step, c % 4],
                device_id=peer,
                device_id_type=MESH,
            )

        def first(c):
            copies = [
                remote(0, c, own, far, self.by_z, 1, self.xn),
                remote(1, c, own, far, self.by_y, 1, self.xn),
            ]
            if units.parts == 9:
                copies.append(remote(2, c, own, far, 8, 1, self.xn))
            return copies

        def second(c):
            return [
                remote(3, c, far, far, self.by_z, 1, self.yn),
                remote(4, c, far, far, self.by_y, 1, self.zn),
            ]

        def third(c):
            return [
                remote(5, c, far, far, self.pair_z, 2, self.zn),
                remote(6, c, far, far, self.pair_y, 2, self.yn),
            ]

        def across(c):
            return [remote(7, c, far, both, 0, units.parts, self.sib)]

        return first, second, third, across


def gelu_both(v):
    c = (2.0 / jnp.pi) ** 0.5
    square = v * v
    t = jnp.tanh(c * v * (1.0 + 0.044715 * square))
    half = 0.5 * (1.0 + t)
    slope = half + 0.5 * v * (1.0 - t * t) * (c * (1.0 + 3.0 * 0.044715 * square))
    return v * half, slope


def pieces_of(ff):
    if ff != 1152:
        return [(0, ff)]
    return [(0, 256), (256, 256), (512, 256), (768, 384)]


def stream_of(ff, lw):
    at, downs, ups = 0, [], []
    for _, size in pieces_of(ff):
        downs.append(at)
        ups.append(at + size)
        at += 2 * size
    return downs, ups, at, at + lw


def split_stream(rows, ff, lw):
    downs, ups, out_row, qkv_row = stream_of(ff, lw)
    sizes = [size for _, size in pieces_of(ff)]
    down, up = (
        jnp.concatenate([rows[at : at + size] for at, size in zip(starts, sizes)])
        for starts in (downs, ups)
    )
    return down, up, rows[out_row:qkv_row], from_halves(rows[qkv_row : qkv_row + 3 * lw])


MID_TICKS, OUT_TICKS, LAST_TICKS, STEP_TICKS, ATTN_TICKS = 4, 2, 4, (1, 1, 1, 2), 1


def plan_of(ff, lw, n):
    downs, ups, out_row, qkv_row = stream_of(ff, lw)
    sizes = [size for _, size in pieces_of(ff)]
    tick, far, own = 0, [], []
    ends = [2 * size + at for size, at in zip(sizes, downs)]
    for beats, end in zip(STEP_TICKS, ends):
        far.append((tick + 2 * beats, end))
        own.append((tick + n * beats, end))
        tick += n * beats
    tick += MID_TICKS + OUT_TICKS
    far.append((tick, qkv_row))
    own.append((tick, qkv_row))
    for half in (1, 2):
        far.append((tick + 2 * ATTN_TICKS, qkv_row + half * 3 * lw // 2))
        own.append((tick + n * ATTN_TICKS, qkv_row + half * 3 * lw // 2))
        tick += n * ATTN_TICKS
    total = (2 * ff + 4 * lw) // CHUNK

    def there(events, now, chunk):
        return any(at <= now and end >= (chunk + 1) * CHUNK for at, end in events)

    x_at, l_at, now = [], [], 0
    while len(l_at) < total:
        if len(l_at) < len(x_at) and x_at[len(l_at)] + 2 <= now and there(own, now, len(l_at)):
            l_at.append(now)
        if len(x_at) < total and there(far, now, len(x_at)):
            x_at.append(now)
        now += 1

    def runs(starts):
        out = []
        for chunk, at in enumerate(starts):
            if out and out[-1][0] + out[-1][2] == at:
                out[-1][2] += 1
            else:
                out.append([at, chunk, 1])
        return out

    return runs(x_at), runs(l_at), l_at[-1] + 14


def in_runs(tick, runs):
    chunk, inside = 0, False
    for start, first, size in runs:
        here = (tick >= start) & (tick < start + size)
        chunk = jnp.where(here, first + tick - start, chunk)
        inside = here | inside
    return chunk, inside


class Reduction:
    def __init__(self, runs, t_buf, t_in, tsend, trecv, d_in, s_own, s_far, x_in, out_ref, lp, tb, ry, ub, rz1, vb, rz2, ob, dsend, drecv, xsend, xrecv, loads, sends, recvs, outs):
        self.x_runs, self.l_runs, self.last_tick = runs
        self.t_buf, self.t_in, self.tsend, self.trecv = t_buf, t_in, tsend, trecv
        self.d_in, self.s_own, self.s_far, self.x_in, self.out_ref = d_in, s_own, s_far, x_in, out_ref
        self.lp, self.tb, self.ry, self.ub, self.rz1, self.vb, self.rz2, self.ob = lp, tb, ry, ub, rz1, vb, rz2, ob
        self.dsend, self.drecv, self.xsend, self.xrecv = dsend, drecv, xsend, xrecv
        self.loads, self.sends, self.recvs, self.outs = loads, sends, recvs, outs
        dp, mp = lax.axis_index("dp"), lax.axis_index("mp")
        core, self.yb = mp % 2, dp % 2
        xb, self.z0, self.z1 = mp // 2, (dp // 2) % 2, dp // 4
        self.sib = (dp, mp + 1 - 2 * core)
        self.xn = (dp, mp + 2 - 4 * xb)
        self.yn = (dp + 1 - 2 * self.yb, mp)
        self.z1n = (dp + 2 - 4 * self.z0, mp)
        self.z2n = (dp + 4 - 8 * self.z1, mp)

    def greet(self):
        barrier = pltpu.get_barrier_semaphore()
        for peer in (self.sib, self.xn, self.yn, self.z1n, self.z2n):
            pl.semaphore_signal(barrier, inc=1, device_id=peer, device_id_type=MESH)
        pl.semaphore_wait(barrier, 5)

    def to_sibling(self, which, flush, source, row, size):
        return pltpu.make_async_remote_copy(
            src_ref=source,
            dst_ref=self.d_in.at[which, pl.ds(row, size)],
            send_sem=self.dsend.at[which, flush],
            recv_sem=self.drecv.at[which, flush],
            device_id=self.sib,
            device_id_type=MESH,
        )

    def x_copy(self, c):
        return pltpu.make_async_remote_copy(
            src_ref=self.s_far.at[rows_at(c, CHUNK)],
            dst_ref=self.x_in.at[rows_at(c, CHUNK)],
            send_sem=self.xsend.at[c],
            recv_sem=self.xrecv.at[c],
            device_id=self.xn,
            device_id_type=MESH,
        )

    def tail_copy(self, source, step, peer):
        return pltpu.make_async_remote_copy(
            src_ref=self.t_buf.at[source],
            dst_ref=self.t_in.at[step],
            send_sem=self.tsend.at[step],
            recv_sem=self.trecv.at[step],
            device_id=peer,
            device_id_type=MESH,
        )

    def tail(self, between):
        t_buf, t_in = self.t_buf, self.t_in
        copies = [self.tail_copy(1, 0, self.sib), self.tail_copy(3, 1, self.sib)]
        for copy in copies:
            copy.start()
        between(0)
        for copy in copies:
            copy.wait()
        t_buf[0] = t_buf[0] + t_in[0]
        t_buf[2] = t_buf[2] + t_in[1]
        for step, source, peer in ((2, 2, self.xn), (3, 0, self.yn), (4, 0, self.z1n), (5, 0, self.z2n)):
            copy = self.tail_copy(source, step, peer)
            copy.start()
            between(step - 1)
            copy.wait()
            t_buf[0] = t_buf[0] + t_in[step]

    def tick(self, tick):
        yb, z0, z1 = self.yb, self.z0, self.z1
        half, quarter, eighth = CHUNK // 2, CHUNK // 4, CHUNK // 8
        at_y = pl.multiple_of(yb * half, half)
        at_z1 = pl.multiple_of(yb * half + z0 * quarter, quarter)
        at_z2 = pl.multiple_of(yb * half + z0 * quarter + z1 * eighth, eighth)
        lp, tb, ub, vb, ob = self.lp, self.tb, self.ub, self.vb, self.ob

        def remote(stage, slot, src, dst, peer):
            return pltpu.make_async_remote_copy(
                src_ref=src,
                dst_ref=dst,
                send_sem=self.sends.at[stage, slot],
                recv_sem=self.recvs.at[stage, slot],
                device_id=peer,
                device_id_type=MESH,
            )

        def load(which, c):
            source = (self.s_own, self.x_in)[which].at[rows_at(c, CHUNK)]
            return pltpu.make_async_copy(source, lp.at[c % 2, which], self.loads.at[which, c % 2])

        def y_copy(c):
            part = rows_at(1 - yb, half)
            return remote(0, c % 4, tb.at[c % 2, part], self.ry.at[c % 4], self.yn)

        def z1_copy(c):
            part = rows_at(1 - z0, quarter)
            return remote(1, c % 4, ub.at[c % 2, part], self.rz1.at[c % 4], self.z1n)

        def z2_copy(c):
            part = rows_at(1 - z1, eighth)
            return remote(2, c % 4, vb.at[c % 2, part], self.rz2.at[c % 4], self.z2n)

        def back(stage, c, at, size, peer):
            place = ob.at[c % OUT_SLOTS, pl.ds(at, size)]
            return remote(stage, c % 4, place, place, peer)

        def az2_copy(c):
            return back(3, c, at_z2, eighth, self.z2n)

        def az1_copy(c):
            return back(4, c, at_z1, quarter, self.z1n)

        def ay_copy(c):
            return back(5, c, at_y, half, self.yn)

        def out_copy(c):
            return pltpu.make_async_copy(
                ob.at[c % OUT_SLOTS], self.out_ref.at[rows_at(c, CHUNK)], self.outs.at[c % 2]
            )

        def stage(lag, work):
            c, inside = in_runs(tick - lag, self.l_runs)

            @pl.when(inside)
            def _():
                work(c)

        def leave(c):
            out_copy(c).wait()

        def store(c):
            ay_copy(c).wait()
            out_copy(c).start()

        def go_ay(c):
            az1_copy(c).wait()
            ay_copy(c).start()

        def go_az1(c):
            az2_copy(c).wait()
            az1_copy(c).start()

        def go_az2(c):
            z2_copy(c).wait()
            ob[c % OUT_SLOTS, pl.ds(at_z2, eighth)] = vb[c % 2, rows_at(z1, eighth)] + self.rz2[c % 4]
            az2_copy(c).start()

        def go_z2(c):
            z1_copy(c).wait()
            vb[c % 2] = ub[c % 2, rows_at(z0, quarter)] + self.rz1[c % 4]
            z2_copy(c).start()

        def go_z1(c):
            y_copy(c).wait()
            ub[c % 2] = tb[c % 2, rows_at(yb, half)] + self.ry[c % 4]
            z1_copy(c).start()

        def go_y(c):
            for which in range(2):
                load(which, c).wait()
            tb[c % 2] = lp[c % 2, 0] + lp[c % 2, 1]
            y_copy(c).start()

        def go_load(c):
            self.x_copy(c).wait()
            for which in range(2):
                load(which, c).start()

        stage(14, leave)
        stage(13, store)
        stage(11, go_ay)
        stage(9, go_az1)
        stage(7, go_az2)
        stage(5, go_z2)
        stage(3, go_z1)
        stage(1, go_y)
        stage(0, go_load)
        c, inside = in_runs(tick, self.x_runs)

        @pl.when(inside)
        def _():
            self.x_copy(c).start()


N_RED = 21


def block_kernel(n, heads, tile, paired, *refs):
    refs = list(refs)

    def take(count):
        taken = refs[:count]
        del refs[:count]
        return taken

    tokens, upstream, item, ids, ids_row, mod, qkv_bias, b_out, b_up, b_down, act = take(11)
    own = take(3) if paired else None
    w_all = None if paired else take(1)[0]
    output_hbm, gtok_hbm, sums_ref, gb_down, gb_out, gb_up, gb_qv = take(7)
    normed_hbm, branch_hbm, qkv_hbm, att_hbm = take(4)
    if paired:
        (w_all,), shared = take(1), take(5)
    else:
        (g_all,) = take(1)
    n_buf, d_buf, acc_a, acc_b, up_buf, down_buf, w_buf, hid_buf, dpre_buf, stage_buf, r_buf = take(11)
    qkv_buf, att_buf, datt_buf, dproj_buf, fold_buf, sum_buf, b_buf, lse = take(8)
    up_sem, down_sem, n_sem, stage_sem, r_sem, w_sem, qkv_sem, att_sem, b_sem = take(9)
    ff = w_all.shape[2]
    pieces = pieces_of(ff)
    if paired:
        gather = Gather(units_of(ff, pieces), own, w_all, *take(4))
        red = Reduction(plan_of(ff, heads * HEAD, n), *take(4), *shared, *refs)
        red.greet()
        gather.begin()
        tick, gather_tick = red.tick, gather.tick
    else:

        def tick(t):
            pass

        gather_tick = tick

    rows, width = tokens.shape
    lw = heads * HEAD
    frames = rows // SLOT
    scale = HEAD ** (-0.5)
    tiles = rows // tile
    some, hh = 3 * lw // 2, heads // 2
    downs, ups, out_row, qkv_row = stream_of(ff, lw)
    fold_buf[...] = jnp.zeros_like(fold_buf)
    sum_buf[...] = jnp.zeros_like(sum_buf)
    gb_up[...] = jnp.zeros_like(gb_up)

    def landed(m, blocks):
        if not paired:
            return

        @pl.when(m % 2 == 0)
        def _():
            for slot, block in enumerate(blocks):
                if block is None:
                    continue
                flush, row, size = block
                stage = stage_buf.at[slot, pl.ds(0, size)]
                sent = red.to_sibling(m // 2, flush, stage, row, size)
                sent.wait()
                fetch(m // 2, slot, row, size).start()

    def fetch(which, slot, row, size):
        return pltpu.make_async_copy(
            red.d_in.at[which, pl.ds(row, size)], r_buf.at[slot, pl.ds(0, size)], r_sem.at[slot]
        )

    def put(target, slot, row, size):
        return pltpu.make_async_copy(
            stage_buf.at[slot, pl.ds(0, size)], target.at[pl.ds(row, size)], stage_sem.at[slot]
        )

    def settle(blocks):
        if paired:
            for slot, (flush, row, size) in enumerate(blocks):
                put(red.s_own, slot, row, size).wait()

    def leave(m, slot, block, value):
        flush, row, size = block
        if not paired:
            stage_buf[slot, pl.ds(0, size), :] = value.astype(bf16)
            copy = put(g_all.at[m], slot, row, size)
            copy.start()
            copy.wait()
            return

        @pl.when(m % 2 == 1)
        def _():
            stage_buf[slot, pl.ds(0, size), :] = value.astype(bf16)
            stage = stage_buf.at[slot, pl.ds(0, size)]
            red.to_sibling(m // 2, flush, stage, row, size).start()

        @pl.when(m % 2 == 0)
        def _():
            fetch(m // 2, slot, row, size).wait()
            total = value + r_buf[slot, pl.ds(0, size), :].astype(f32)
            stage_buf[slot, pl.ds(0, size), :] = total.astype(bf16)

            @pl.when(m == 0)
            def _():
                put(red.s_own, slot, row, size).start()

            @pl.when(m > 0)
            def _():
                put(red.s_far, slot, row, size).start()

    def w_copies(p, m, slot):
        at, size = pieces[p]
        here = pl.ds(at, size)
        up_part, down_part = up_buf.at[slot, :, pl.ds(0, size)], down_buf.at[slot, pl.ds(0, size), :]
        return (
            Shard(own, w_all, 1, m, (slice(None), here), up_part, up_sem.at[slot]),
            Shard(own, w_all, 2, m, (here, slice(None)), down_part, down_sem.at[slot]),
        )

    def f_copies(m):
        return [
            Shard(own, w_all, 0, m, pl.ds(half * some, some), w_buf.at[half], w_sem.at[half])
            for half in range(2)
        ] + [Shard(own, w_all, 0, m, pl.ds(3 * lw, lw), r_buf.at[m % 2, pl.ds(0, lw)], r_sem.at[m % 2])]

    def f_start(m):
        for copy in f_copies(m):
            copy.start()

    def qkv_out(m, half):
        return pltpu.make_async_copy(qkv_buf.at[half], qkv_hbm.at[m, half], qkv_sem.at[half])

    def att_out(m):
        return pltpu.make_async_copy(att_buf.at[m % 2], att_hbm.at[m], att_sem.at[m % 2])

    f_start(0)

    def normed_part(i, carry):
        gather_tick(i)

        def block(j, c):
            at = pl.ds(pl.multiple_of(i * SLOT + j * BLOCK, BLOCK), BLOCK)
            col = item[at, :]
            normed, _ = normal(tokens[at, :].astype(f32))
            n_buf[at, :] = (normed * (1.0 + pick(col, mod, 1)) + pick(col, mod, 0)).astype(bf16)
            acc_a[at, :] = jnp.broadcast_to(b_out[...], (BLOCK, width))
            return c

        lax.fori_loop(0, SLOT // BLOCK, block, 0, unroll=UNROLL)
        return carry

    lax.fori_loop(0, frames, normed_part, 0)
    normed_out = pltpu.make_async_copy(n_buf, normed_hbm, n_sem)
    normed_out.start()
    if paired:
        gather.near(0).wait()

    def upstream_part(i):
        def block(j, c):
            at = pl.ds(pl.multiple_of(i * SLOT + j * BLOCK, BLOCK), BLOCK)
            d = (pick(item[at, :], mod, 5) * upstream[at, :].astype(f32)).astype(bf16)
            d_buf[at, :] = d
            sum_buf[0] += fold(d.astype(f32))
            acc_b[at, :] = jnp.zeros((BLOCK, width), f32)
            return c

        lax.fori_loop(0, SLOT // BLOCK, block, 0, unroll=UNROLL)

    def attend_part(m, carry):
        for copy in f_copies(m):
            copy.wait()

        @pl.when(m >= 1)
        def _():
            for half in range(2):
                qkv_out(m - 1, half).wait()

        @pl.when(m >= 2)
        def _():
            att_out(m - 2).wait()

        for half in range(2):
            bias = jnp.transpose(jnp.broadcast_to(qkv_bias[m, half], (8, some)))[:, 0:1]
            proj = nt(w_buf[half], n_buf[...]) + bias
            for h in range(3 * hh):
                qkv_buf[half, h] = proj[h * HEAD : (h + 1) * HEAD].astype(bf16)
            qkv_out(m, half).start()

        if paired:

            @pl.when(m == 2)
            def _():
                gather_tick(frames * 3 + 3)

        @pl.when((m + 1 < n) & (m != 1) if paired else m + 1 < n)
        def _():
            f_start(m + 1)

        def frame(f, c):
            gather_tick(frames + m * frames + f + jnp.where(m > 1, EXTRA, 0))
            at = rows_at(f, SLOT)
            pairs = pair_bias(ids[at, :], ids_row[pl.ds(f, 1), :])
            heads_qkv = [
                [qkv_buf[h // hh, j * hh + h % hh, :, at] for j in range(3)] for h in range(heads)
            ]
            all_scores = [tn(k, q) * scale + pairs for q, k, _ in heads_qkv]
            all_weights = []
            for h, scores in enumerate(all_scores):
                peak = jnp.max(scores, axis=0, keepdims=True)
                weights = jnp.exp(scores - peak)
                total = jnp.sum(weights, axis=0, keepdims=True)
                lse[m, h : h + 1, at] = peak + jnp.log(total)
                all_weights.append((weights.astype(bf16), 1.0 / total))
            outs = [dot(v, w) * inverse for (_, _, v), (w, inverse) in zip(heads_qkv, all_weights)]
            att_buf[m % 2, :, at] = jnp.concatenate(outs, axis=0).astype(bf16)
            return c

        lax.fori_loop(0, frames, frame, 0)
        att_out(m).start()

        def branch(j, c):
            at = rows_at(j, tile)
            acc_a[at, :] += tn(att_buf[m % 2, :, at], r_buf[m % 2, pl.ds(0, lw), :])
            return c

        lax.fori_loop(0, tiles, branch, 0)
        @pl.when(m == 1)
        def _():
            def slot_part(i, c):
                if paired:

                    @pl.when(i % 2 == 0)
                    def _():
                        gather_tick(frames * 3 + i // 2)

                upstream_part(i)
                return c

            lax.fori_loop(0, frames, slot_part, 0)
            if paired:
                gather_tick(frames * 3 + 2)
                f_start(m + 1)

        return carry

    lax.fori_loop(0, n, attend_part, 0)
    if paired:
        gather.near(1).wait()
        gather.near(2).wait()
    for half in range(2):
        qkv_out(n - 1, half).wait()
    for m in range(max(n - 2, 0), n):
        att_out(m).wait()
    normed_out.wait()

    def b_copy(i):
        return pltpu.make_async_copy(branch_hbm.at[rows_at(i, SLOT)], b_buf.at[i % 2], b_sem.at[i % 2])

    def b_out_copy(i):
        return pltpu.make_async_copy(b_buf.at[i % 2], branch_hbm.at[rows_at(i, SLOT)], b_sem.at[i % 2])

    def first(i, carry):
        gather_tick(frames * (n + 1) + EXTRA + i)

        @pl.when(i >= 2)
        def _():
            b_out_copy(i - 2).wait()

        def block(j, c):
            at = pl.ds(pl.multiple_of(i * SLOT + j * BLOCK, BLOCK), BLOCK)
            col = item[at, :]
            branch = acc_a[at, :]
            b_buf[i % 2, rows_at(j, BLOCK), :] = branch
            middle = tokens[at, :].astype(f32) + pick(col, mod, 2) * branch
            normed, _ = normal(middle)
            n_buf[at, :] = (normed * (1.0 + pick(col, mod, 4)) + pick(col, mod, 3)).astype(bf16)
            acc_a[at, :] = jnp.broadcast_to(b_down[...], (BLOCK, width))
            return c

        @pl.when(i + 1 == frames)
        def _():
            for copy in w_copies(0, n - 1, 0):
                copy.start()

        lax.fori_loop(0, SLOT // BLOCK, block, 0, unroll=UNROLL)
        b_out_copy(i).start()
        return carry

    lax.fori_loop(0, frames, first, 0)
    for i in range(max(frames - 2, 0), frames):
        b_out_copy(i).wait()

    def by_slots(work, after):
        b_copy(0).start()

        def slot_part(i, carry):
            b_copy(i).wait()

            @pl.when(i + 1 < frames)
            def _():
                b_copy(i + 1).start()

            def block(j, c):
                work(i, pl.ds(pl.multiple_of(i * SLOT + j * BLOCK, BLOCK), BLOCK), rows_at(j, BLOCK))
                return c

            lax.fori_loop(0, SLOT // BLOCK, block, 0, unroll=UNROLL)
            after(i)
            return carry

        lax.fori_loop(0, frames, slot_part, 0)

    def blocks_of(p):
        size = pieces[p][1]
        return ((2 * p, downs[p], size), (2 * p + 1, ups[p], size))

    now = 0
    for p, (p_at, p_size) in enumerate(pieces):
        def shard(i, carry, p=p, p_at=p_at, p_size=p_size, now=now):
            m = n - 1 - i
            slot = (p * n + i) % 2
            for copy in w_copies(p, m, slot):
                copy.wait()

            @pl.when(i + 1 < n)
            def _():
                for copy in w_copies(p, m - 1, 1 - slot):
                    copy.start()

            if p + 1 < len(pieces):

                @pl.when(i + 1 == n)
                def _():
                    for copy in w_copies(p + 1, n - 1, 1 - slot):
                        copy.start()

            blocks = blocks_of(p)
            bias = b_up[m, :, pl.ds(p_at, p_size)]
            up = up_buf.at[slot, :, pl.ds(0, p_size)]
            down = down_buf.at[slot, pl.ds(0, p_size), :]

            def part(j, c):
                at = rows_at(j, tile)
                pre = jnp.dot(n_buf[at, :], up[...], preferred_element_type=f32) + bias
                hidden, slope = gelu_both(pre)
                hidden = hidden.astype(bf16)
                dpre = nt(d_buf[at, :], down[...]) * slope
                dpre = dpre.astype(bf16)
                hid_buf[at, pl.ds(0, p_size)] = hidden
                dpre_buf[at, pl.ds(0, p_size)] = dpre
                gb_up[m, :, pl.ds(p_at, p_size)] += jnp.sum(
                    dpre.astype(f32), axis=0, keepdims=True
                )
                acc_a[at, :] += jnp.dot(hidden, down[...], preferred_element_type=f32)
                acc_b[at, :] += nt(dpre, up[...])
                return c

            lax.fori_loop(0, tiles, part, 0)

            @pl.when(i == 2)
            def _():
                settle(blocks)

            if p:

                @pl.when(i == 0)
                def _():
                    settle(blocks_of(p - 1))

            if p < 2:
                gather_tick(frames * (n + 2) + EXTRA + now + i)
            tick(now + STEP_TICKS[p] * i)
            landed(m, blocks)
            leave(m, 0, blocks[0], tn(hid_buf[:, pl.ds(0, p_size)], d_buf[...]))
            leave(m, 1, blocks[1], tn(dpre_buf[:, pl.ds(0, p_size)], n_buf[...]))
            if STEP_TICKS[p] > 1:
                tick(now + STEP_TICKS[p] * i + 1)
            return carry

        lax.fori_loop(0, n, shard, 0)
        now += n * STEP_TICKS[p]
    settle(blocks_of(len(pieces) - 1))

    def out_copies(m, slot):
        there = pl.ds(3 * lw, lw)
        return (
            Shard(own, w_all, 0, m, there, w_buf.at[slot, pl.ds(0, lw)], w_sem.at[slot]),
            pltpu.make_async_copy(att_hbm.at[m], att_buf.at[slot], att_sem.at[slot]),
        )

    def a_copies(half, m, slot):
        there = pl.ds(half * some, some)
        return (
            Shard(own, w_all, 0, m, there, w_buf.at[slot], w_sem.at[slot]),
            pltpu.make_async_copy(qkv_hbm.at[m, half], qkv_buf.at[slot], qkv_sem.at[slot]),
        )

    normed_copy = pltpu.make_async_copy(normed_hbm, n_buf, n_sem)
    normed_copy.start()
    for copy in out_copies(n - 1, 0):
        copy.start()

    def row_copy(target, i):
        return pltpu.make_async_copy(
            stage_buf.at[i % 2, pl.ds(0, SLOT)], target.at[rows_at(i, SLOT)], stage_sem.at[i % 2]
        )

    def rows_done(target):
        for i in range(max(frames - 2, 0), frames):
            row_copy(target, i).wait()

    def middle_part(i, at, here):
        col = item[at, :]
        gate = pick(col, mod, 2)
        branch = b_buf[i % 2, here, :]
        middle = tokens[at, :].astype(f32) + gate * branch
        dy = upstream[at, :].astype(f32)
        second = acc_a[at, :]
        stage_buf[i % 2, here, :] = (middle + pick(col, mod, 5) * second).astype(bf16)
        add_by_item(fold_buf, 5, col, dy * second)
        grad = acc_b[at, :]
        normed, rstd = normal(middle)
        add_by_item(fold_buf, 3, col, grad)
        add_by_item(fold_buf, 4, col, grad * normed)
        dmiddle = dy + normal_back(grad, pick(col, mod, 4), normed, rstd)
        acc_a[at, :] = dmiddle
        add_by_item(fold_buf, 2, col, dmiddle * branch)
        d = (gate * dmiddle).astype(bf16)
        d_buf[at, :] = d
        sum_buf[1] += fold(d.astype(f32))
        acc_b[at, :] = jnp.zeros((BLOCK, width), f32)

    def middle_done(i):
        row_copy(output_hbm, i).start()

        @pl.when((i >= 1) & (i + 1 < frames))
        def _():
            row_copy(output_hbm, i - 1).wait()

        if MID_TICKS == 4:
            tick(now + i)
        else:

            @pl.when(i % 2 == 1)
            def _():
                tick(now + i // 2)

    by_slots(middle_part, middle_done)
    rows_done(output_hbm)
    now += MID_TICKS
    normed_copy.wait()
    out_block = (2 * len(pieces), out_row, lw)

    def out_part(i, carry):
        m = n - 1 - i
        slot = i % 2
        for copy in out_copies(m, slot):
            copy.wait()

        @pl.when(i + 1 < n)
        def _():
            for copy in out_copies(m - 1, 1 - slot):
                copy.start()

        @pl.when(i == 2)
        def _():
            settle((out_block,))

        landed(m, (out_block,))
        leave(m, 0, out_block, dot(att_buf[slot], d_buf[...]))
        datt = nt(w_buf[slot, pl.ds(0, lw), :], d_buf[...])
        for h in range(heads):
            datt_buf[m, h] = datt[h * HEAD : (h + 1) * HEAD].astype(bf16)

        if OUT_TICKS == 4:
            tick(now + i)
        else:

            @pl.when(i % 2 == 1)
            def _():
                tick(now + i // 2)

        return carry

    lax.fori_loop(0, n, out_part, 0)
    settle((out_block,))
    now += OUT_TICKS
    for copy in a_copies(0, n - 1, 0):
        copy.start()

    def qkv_block(half):
        return (2 * len(pieces) + 1 + half, qkv_row + half * some, some)

    for half in range(2):

        def attn(i, carry, half=half, now=now):
            m = n - 1 - i
            slot = i % 2
            for copy in a_copies(half, m, slot):
                copy.wait()

            @pl.when(i + 1 < n)
            def _():
                for copy in a_copies(half, m - 1, 1 - slot):
                    copy.start()

            if half == 0:

                @pl.when(i + 1 == n)
                def _():
                    for copy in a_copies(1, n - 1, 1 - slot):
                        copy.start()

            def frame(f, c):
                at = rows_at(f, SLOT)
                pairs = pair_bias(ids[at, :], ids_row[pl.ds(f, 1), :])
                each = range(hh)
                q, k, v = ([qkv_buf[slot, j * hh + h, :, at] for h in each] for j in range(3))
                d = [datt_buf[m, half * hh + h, :, at] for h in each]
                lses = [lse[m, half * hh + h : half * hh + h + 1, at] for h in each]
                scores = [tn(k[h], q[h]) * scale + pairs for h in each]
                probs = [jnp.exp(scores[h] - lses[h]) for h in each]
                dprobs = [tn(v[h], d[h]) for h in each]
                low, dscores = [], []
                for h in each:
                    inner = jnp.sum(dprobs[h] * probs[h], axis=0, keepdims=True)
                    low.append(probs[h].astype(bf16))
                    dscores.append((probs[h] * (dprobs[h] - inner)).astype(bf16))
                dvs = [nt(d[h], low[h]) for h in each]
                dqs = [dot(k[h], dscores[h]) * scale for h in each]
                dks = [nt(q[h], dscores[h]) * scale for h in each]
                dproj_buf[:, at] = jnp.concatenate(dqs + dks + dvs, axis=0).astype(bf16)
                return c

            lax.fori_loop(0, frames, frame, 0)

            @pl.when(i == 2)
            def _():
                settle((qkv_block(half),))

            if half == 1:

                @pl.when(i == 0)
                def _():
                    settle((qkv_block(0),))

            tick(now + ATTN_TICKS * i)
            landed(m, (qkv_block(half),))
            gb_qv[m, half] = nt(jnp.ones((8, rows), bf16), dproj_buf[...])[0:1]
            leave(m, 0, qkv_block(half), dot(dproj_buf[...], n_buf[...]))

            def part(j, c):
                at = rows_at(j, tile)
                acc_b[at, :] += tn(dproj_buf[:, at], w_buf[slot, pl.ds(0, some), :])
                return c

            lax.fori_loop(0, tiles, part, 0)
            if ATTN_TICKS > 1:
                tick(now + ATTN_TICKS * i + 1)
            return carry

        lax.fori_loop(0, n, attn, 0)
        now += n * ATTN_TICKS
    settle((qkv_block(1),))

    def last(i, carry):
        def block(j, c):
            at = pl.ds(pl.multiple_of(i * SLOT + j * BLOCK, BLOCK), BLOCK)
            col = item[at, :]
            normed, rstd = normal(tokens[at, :].astype(f32))
            grad = acc_b[at, :]
            add_by_item(fold_buf, 0, col, grad)
            add_by_item(fold_buf, 1, col, grad * normed)
            value = acc_a[at, :] + normal_back(grad, pick(col, mod, 1), normed, rstd)
            stage_buf[i % 2, rows_at(j, BLOCK), :] = value.astype(bf16)
            return c

        lax.fori_loop(0, SLOT // BLOCK, block, 0, unroll=UNROLL)
        row_copy(gtok_hbm, i).start()

        @pl.when((i >= 1) & (i + 1 < frames))
        def _():
            row_copy(gtok_hbm, i - 1).wait()

        tick(now + i)
        return carry

    lax.fori_loop(0, frames, last, 0)
    rows_done(gtok_hbm)
    for j in range(sums_ref.shape[0]):
        for k in range(6):
            sums_ref[j, k : k + 1, :] = jnp.sum(fold_buf[j, k], axis=0, keepdims=True)
    gb_down[...] = jnp.sum(sum_buf[0], axis=0, keepdims=True)
    gb_out[...] = jnp.sum(sum_buf[1], axis=0, keepdims=True)
    if paired:
        dp, mp = lax.axis_index("dp"), lax.axis_index("mp")
        items = sums_ref.shape[0]
        total_items = lax.axis_size("dp") * items
        core, xb = mp % 2, mp // 2
        acc_b[pl.ds(0, n * TAIL), :] = jnp.zeros((n * TAIL, width), f32)

        def line(a, row, at=0, size=width):
            return acc_b.at[pl.ds(a * TAIL + row, 1), pl.ds(at, size)]

        for a in range(n):
            for j in range(items):
                for k in range(6):
                    row = dp * items + j + k // 4 * total_items
                    line(a, row, k % 4 * lw, lw)[...] = sums_ref[j, k : k + 1, a * lw : (a + 1) * lw]
                line(a, 2 * total_items + dp * items + j)[...] = jnp.where(mp == 0, act[j : j + 1, :], 0.0)
        for m in range(n):
            here = (xb if m < 2 else 1 - xb) * 2 + (core if m % 2 == 0 else 1 - core)
            for k, values in enumerate((gb_out, gb_down, gb_up.at[m])):
                for j in range(4):
                    line(here, total_items + 4 * k + j, 2 * lw, lw)[...] = values[:, j * lw : (j + 1) * lw]
            for j in range(2):
                for half in range(2):
                    place = line(here, total_items + 12 + j, 2 * lw + half * lw // 2, lw // 2)
                    place[...] = gb_qv[m, half, :, j * lw : j * lw + lw // 2]
            red.t_buf[m] = acc_b[pl.ds(pl.multiple_of(here * TAIL, TAIL), TAIL), :].astype(bf16)

        start, end = now + LAST_TICKS, red.last_tick + 1
        bounds = [start + (end - start) * step // 5 for step in range(6)]

        def drain(t, carry):
            tick(t)
            return carry

        def between(step):
            lax.fori_loop(bounds[step], bounds[step + 1], drain, 0)

        red.tail(between)
        tail_out = pltpu.make_async_copy(
            red.t_buf.at[0], red.out_ref.at[pl.ds(2 * ff + 4 * lw, TAIL)], n_sem
        )
        tail_out.start()
        tail_out.wait()


def block(tokens, upstream, item, ids, mod, qkv_bias, b_out, b_up, b_down, act, weights, paired):
    rows, width = tokens.shape
    n, ff = b_up.shape[0], b_up.shape[2]
    heads = 4
    lw = heads * HEAD
    pieces = pieces_of(ff)
    widest = max(size for _, size in pieces)
    tile = min(1024, rows)
    total = 2 * ff + 4 * lw
    deep = max(widest, 3 * lw // 2, SLOT)
    slots = 2
    flushes = 2 * len(pieces) + 3
    half, quarter, eighth = CHUNK // 2, CHUNK // 4, CHUNK // 8
    vmem = pl.BlockSpec(memory_space=pltpu.VMEM)
    hbm = pl.BlockSpec(memory_space=pl.ANY)
    dma = pltpu.SemaphoreType.DMA

    def low(*shape):
        return jax.ShapeDtypeStruct(shape, bf16)

    def full(*shape):
        return jax.ShapeDtypeStruct(shape, f32)

    def buf(*shape):
        return pltpu.VMEM(shape, bf16)

    grads = [low(n, total, width)]
    extra = []
    if paired:
        grads = [low(3, n - 1, ff, width), low(2, total, width)] + [low(total, width)] * 3
        grads.append(low(total + TAIL, width))
        extra = [
            dma((5, 8, 4)),
            dma((5, 8, 4)),
            dma((3,)),
            dma((3,)),
            buf(n, TAIL, width),
            buf(6, TAIL, width),
            dma((6,)),
            dma((6,)),
            buf(2, 2, CHUNK, width),
            buf(2, CHUNK, width),
            buf(4, half, width),
            buf(2, half, width),
            buf(4, quarter, width),
            buf(2, quarter, width),
            buf(4, eighth, width),
            buf(OUT_SLOTS, CHUNK, width),
            dma((2, flushes)),
            dma((2, flushes)),
            dma((total // CHUNK,)),
            dma((total // CHUNK,)),
            dma((2, 2)),
            dma((6, 4)),
            dma((6, 4)),
            dma((2,)),
        ]
    return pl.pallas_call(
        functools.partial(block_kernel, n, heads, tile, paired),
        out_shape=(
            low(rows, width),
            low(rows, width),
            jax.ShapeDtypeStruct(mod.shape, f32),
            full(1, width),
            full(1, width),
            full(n, 1, ff),
            full(n, 2, 1, 3 * lw // 2),
            low(rows, width),
            full(rows, width),
            low(n, 2, 3 * heads // 2, HEAD, rows),
            low(n, lw, rows),
            *grads,
        ),
        in_specs=[vmem] * 11 + [hbm] * len(weights),
        out_specs=(hbm,) * 2 + (vmem,) * 5 + (hbm,) * (4 + len(grads)),
        scratch_shapes=[
            buf(rows, width),
            buf(rows, width),
            pltpu.VMEM((rows, width), f32),
            pltpu.VMEM((rows, width), f32),
            buf(2, width, widest),
            buf(2, widest, width),
            buf(2, 3 * lw // 2, width),
            buf(rows, widest),
            buf(rows, widest),
            buf(slots, deep, width),
            buf(slots, deep, width),
            buf(2, 3 * heads // 2, HEAD, rows),
            buf(2, lw, rows),
            buf(n, heads, HEAD, rows),
            buf(3 * lw // 2, rows),
            pltpu.VMEM((mod.shape[0], 6, 8, width), f32),
            pltpu.VMEM((2, 8, width), f32),
            pltpu.VMEM((2, SLOT, width), f32),
            pltpu.VMEM((n, heads, rows), f32),
            dma((2,)),
            dma((2,)),
            dma,
            dma((slots,)),
            dma((slots,)),
            dma((2,)),
            dma((2,)),
            dma((2,)),
            dma((2,)),
            *extra,
        ],
        compiler_params=pltpu.CompilerParams(
            collective_id=0 if paired else None, has_side_effects=paired, vmem_limit_bytes=63 << 20
        ),
    )(
        tokens, upstream, item[:, None], ids[:, None], ids.reshape(-1, SLOT), mod,
        qkv_bias.reshape(n, 2, 1, 3 * lw // 2), b_out, b_up, b_down, act, *weights,
    )


def finish_kernel(ff, lw, total_items, columns, downs, outs, tail, up_out, down_out, qkv_out, out_out, ada_out, bias_out, qv_out, bada_out):
    size = columns.shape[1]
    _, ups, out_row, qkv_row = stream_of(ff, lw)
    up = jnp.concatenate([columns[at : at + n, :] for at, (_, n) in zip(ups, pieces_of(ff))], axis=0)
    up_out[...] = jnp.transpose(up.astype(f32))
    down_out[...] = downs[...].astype(f32)
    out_out[...] = outs[...].astype(f32)
    half = lw // 2
    for j in range(3):
        rows = [columns[qkv_row + h * 3 * half + j * half : qkv_row + h * 3 * half + (j + 1) * half, :] for h in range(2)]
        qkv_out[j] = jnp.concatenate(rows, axis=0).astype(f32)
    tail_row = 2 * ff + 4 * lw
    act = columns[tail_row + 2 * total_items : tail_row + 3 * total_items, :]
    for k in range(6):
        first = k // 4 * total_items
        dmod = tail[first : first + total_items, k % 4 * lw : (k % 4 + 1) * lw]
        ada_out[k] = tn(dmod, act)
        bada_out[k : k + 1, :] = jnp.sum(dmod.astype(f32), axis=0, keepdims=True)
    more = tail[total_items : 2 * total_items, 2 * lw : 3 * lw].astype(f32)
    for k in range(3):
        for j in range(4):
            bias_out[k : k + 1, j * lw : (j + 1) * lw] = more[4 * k + j : 4 * k + j + 1]
    qv_out[...] = more[12:14]


def finish(total, ff, lw, total_items):
    width = total.shape[1]
    size = 128
    steps = width // size
    piece, last = pieces_of(ff)[0][1] // size, len(pieces_of(ff)) - 1
    out_rows = lw // steps

    def down_place(i):
        return (i + piece * jnp.minimum(i // piece, last), 0)

    def full(*shape):
        return jax.ShapeDtypeStruct(shape, f32)

    return pl.pallas_call(
        functools.partial(finish_kernel, ff, lw, total_items),
        grid=(steps,),
        out_shape=(
            full(width, ff),
            full(ff, width),
            full(3, lw, width),
            full(lw, width),
            full(6, lw, width),
            full(3, width),
            full(2, lw),
            full(6, lw),
        ),
        in_specs=[
            pl.BlockSpec((total.shape[0], size), lambda i: (0, i)),
            pl.BlockSpec((size, width), down_place),
            pl.BlockSpec((out_rows, width), lambda i: (2 * ff // out_rows + i, 0)),
            pl.BlockSpec((TAIL, width), lambda i: ((2 * ff + 4 * lw) // TAIL, 0)),
        ],
        out_specs=(
            pl.BlockSpec((size, ff), lambda i: (i, 0)),
            pl.BlockSpec((size, width), lambda i: (i, 0)),
            pl.BlockSpec((3, lw, size), lambda i: (0, 0, i)),
            pl.BlockSpec((out_rows, width), lambda i: (i, 0)),
            pl.BlockSpec((6, lw, size), lambda i: (0, 0, i)),
            pl.BlockSpec((3, width), lambda i: (0, 0)),
            pl.BlockSpec((2, lw), lambda i: (0, 0)),
            pl.BlockSpec((6, lw), lambda i: (0, 0)),
        ),
        compiler_params=pltpu.CompilerParams(vmem_limit_bytes=32 << 20),
        cost_estimate=pl.CostEstimate(flops=10**8, bytes_accessed=5 * 10**7, transcendentals=0),
    )(total, total, total, total)


def by_halves(rows):
    halves = rows.reshape(3, 2, -1, *rows.shape[1:])
    return jnp.swapaxes(halves, 0, 1).reshape(rows.shape)


def from_halves(rows):
    halves = rows.reshape(2, 3, -1, *rows.shape[1:])
    return jnp.swapaxes(halves, 0, 1).reshape(rows.shape)


def swap(values, axis, bit):
    n = lax.axis_size(axis)
    return lax.ppermute(values, axis, [(i, i ^ bit) for i in range(n)])


def shards(
    paired,
    tokens,
    condition,
    grid_rows,
    grid_cols,
    frame_start,
    frame_item,
    group_frames,
    w_qkv,
    qv_bias,
    w_out,
    b_out,
    w_up,
    b_up,
    w_down,
    b_down,
    w_ada,
    b_ada,
    cotangent,
):
    own_rows, width = tokens.shape
    local_width = w_qkv.shape[2]
    local_ff = w_up.shape[1]
    items = condition.shape[0]
    n_mp, n_dp = lax.axis_size("mp"), lax.axis_size("dp")
    mp, dp = lax.axis_index("mp"), lax.axis_index("dp")
    n = width // (4 * HEAD)
    lw, ff = width // n, local_ff * n_mp // n
    frame_id, item_id = frame_tables(
        grid_rows, grid_cols, frame_start, frame_item, group_frames[0], mp * own_rows, own_rows
    )
    cond_value = condition.astype(f32)
    act_low = jax.nn.silu(cond_value).astype(bf16)
    ada_flat = w_ada.reshape(width, -1)
    ada_local = dot(act_low, ada_flat) + b_ada.reshape(-1).astype(f32)
    ada_local = ada_local.reshape(items, 6, local_width)
    qkv_local = w_qkv.transpose(1, 2, 0)
    if paired:
        qkv_bias = jnp.concatenate(
            [qv_bias[0].astype(f32), jnp.zeros((lw,), f32), qv_bias[1].astype(f32)]
        )
        small = jnp.concatenate([ada_local.reshape(-1), by_halves(qkv_bias), b_up.astype(f32)])
        small = jnp.stack([small] + [swap(small, "mp", bit) for bit in range(1, n)])
        sorted_small = jnp.where(mp % 2 == 0, small, small[jnp.array([1, 0, 3, 2])])
        sorted_small = jnp.where(mp < 2, sorted_small, sorted_small[jnp.array([2, 3, 0, 1])])
        n_ada = ada_local.size
        modulation = sorted_small[:, :n_ada].reshape(n, items, 6, lw)
        qkv_bias = small[:, n_ada : n_ada + 3 * lw]
        up_bias = small[:, n_ada + 3 * lw :]
        weights = [
            jnp.concatenate([by_halves(qkv_local.reshape(3 * lw, width)), w_out], axis=0),
            w_up,
            w_down,
        ]
    else:
        modulation = lax.all_gather(ada_local, "mp", axis=0)
        qv = lax.all_gather(qv_bias.astype(f32), "mp", axis=1, tiled=True)
        qkv_bias = jnp.stack([qv[0], jnp.zeros((width,), f32), qv[1]])
        qkv_bias = jax.vmap(by_halves)(qkv_bias.reshape(3, n, lw).transpose(1, 0, 2).reshape(n, 3 * lw))
        up_bias = lax.all_gather(b_up.astype(f32), "mp", axis=0, tiled=True).reshape(n, ff)
        qkv = lax.all_gather(qkv_local, "mp", axis=1, tiled=True)
        qkv = qkv.reshape(3, n, lw, width).transpose(1, 0, 2, 3).reshape(n, 3 * lw, width)
        qkv = jax.vmap(by_halves)(qkv)
        out = lax.all_gather(w_out, "mp", axis=0, tiled=True).reshape(n, lw, width)
        up = lax.all_gather(w_up, "mp", axis=1, tiled=True)
        up = up.reshape(width, n, ff).transpose(1, 0, 2)
        down = lax.all_gather(w_down, "mp", axis=0, tiled=True).reshape(n, ff, width)
        weights = [jnp.stack([jnp.concatenate([qkv, out], axis=1), up, down])]
    modulation = modulation.transpose(1, 2, 0, 3).reshape(items, 6, width)
    b_out_row, b_down_row = (b.astype(f32)[None] for b in (b_out, b_down))
    output, grad_tokens, item_grad, gb_down, gb_out, gb_up, gb_qv, *rest = block(
        tokens,
        cotangent,
        item_id,
        frame_id,
        modulation,
        qkv_bias,
        b_out_row,
        up_bias[:, None],
        b_down_row,
        act_low.astype(f32),
        weights,
        paired,
    )
    if paired:
        total = rest[-1]
        total_items = items * n_dp
        g_up, g_down, g_qkv, g_out, grad_w_ada, biases, gb_qv, grad_b_ada = finish(
            total, ff, lw, total_items
        )
        g_qkv, grad_w_ada = g_qkv.transpose(2, 0, 1), grad_w_ada.transpose(2, 0, 1)
        gb_out, gb_down, gb_up = biases
        tail = lax.dynamic_slice_in_dim(total[2 * ff + 4 * lw :], dp * items, total_items + items)
        own_dmod = jnp.concatenate([tail[:items], tail[-items:, : 2 * lw]], axis=1).astype(f32)
    else:

        gb_qv = jax.vmap(from_halves)(gb_qv.reshape(n, 3 * lw)).reshape(n, 3, lw)[:, ::2]

        def over_all(values, axis):
            part = lax.psum_scatter(values, "mp", scatter_dimension=axis, tiled=True)
            return lax.psum(part.astype(bf16), "dp").astype(f32)

        own_dmod = lax.psum_scatter(item_grad, "mp", scatter_dimension=2, tiled=True)
        dmod = lax.all_gather(own_dmod, "dp", axis=0, tiled=True)
        act_all = lax.all_gather(act_low, "dp", axis=0, tiled=True).astype(f32)
        g_down, g_up, g_out, g_qkv = jax.vmap(lambda g: split_stream(g, ff, lw))(rest[-1])
        g_down = over_all(g_down.reshape(n * ff, width), 0)
        g_up = over_all(g_up.reshape(n * ff, width).T, 1)
        g_qkv = g_qkv.reshape(n, 3, lw, width).transpose(3, 1, 0, 2).reshape(width, 3, width)
        g_qkv = over_all(g_qkv, 2)
        g_out = over_all(g_out.reshape(width, width), 0)
        gb_up = over_all(gb_up.reshape(-1), 0)
        gb_qv = over_all(gb_qv.transpose(1, 0, 2).reshape(2, width), 1)
        gb_out = lax.psum(gb_out[0], ("dp", "mp"))
        gb_down = lax.psum(gb_down[0], ("dp", "mp"))
        grad_w_ada = lax.dot_general(
            act_all,
            dmod.reshape(dmod.shape[0], -1),
            (((0,), (0,)), ((), ())),
            precision=lax.Precision.HIGHEST,
        ).reshape(width, 6, local_width)
        grad_b_ada = jnp.sum(dmod, axis=0)
    cond_term = lax.dot_general(
        own_dmod.reshape(items, -1),
        ada_flat.astype(f32),
        (((1,), (1,)), ((), ())),
        precision=lax.Precision.HIGHEST,
    )
    if paired:
        cond_term = cond_term + swap(cond_term, "mp", 1)
        cond_term = cond_term + swap(cond_term, "mp", 2)
    else:
        cond_term = lax.psum(cond_term, "mp")
    grad_condition = jax.vjp(jax.nn.silu, cond_value)[1](cond_term)[0]
    return (
        output,
        grad_tokens,
        grad_condition,
        g_qkv,
        gb_qv,
        g_out,
        gb_out,
        g_up,
        gb_up,
        g_down,
        gb_down,
        grad_w_ada,
        grad_b_ada,
    )


def solution(mesh):
    paired = dict(mesh.shape) == {"dp": 8, "mp": 4}
    return jax.shard_map(
        functools.partial(shards, paired),
        mesh=mesh,
        in_specs=(
            P(("dp", "mp"), None),
            P("dp", None),
            P("dp"),
            P("dp"),
            P("dp"),
            P("dp"),
            P("dp"),
            P(None, None, "mp"),
            P(None, "mp"),
            P("mp", None),
            P(),
            P(None, "mp"),
            P("mp"),
            P("mp", None),
            P(),
            P(None, None, "mp"),
            P(None, "mp"),
            P(("dp", "mp"), None),
        ),
        out_specs=(
            P(("dp", "mp"), None),
            P(("dp", "mp"), None),
            P("dp", None),
            P(None, None, "mp"),
            P(None, "mp"),
            P("mp", None),
            P(),
            P(None, "mp"),
            P("mp"),
            P("mp", None),
            P(),
            P(None, None, "mp"),
            P(None, "mp"),
        ),
        check_vma=False,
    )
```
